32 devices in a mesh: groups: 2 (over x), wide: 16 (over z, y, core).
Axes of the slice: x: 2, y: 2, z: 4, core: 2. Of those that a mesh axis runs over, the one named last changes fastest.
Arguments:
- acts: bfloat16 [160, 28672], P(('groups', 'wide')), parts along dimension 0, may hold values from -6 to 6
- grads: bfloat16 [160, 8192], P(('groups', 'wide')), parts along dimension 0, may hold values from -6 to 6
- basis_in: bfloat16 [57344, 1536], P('groups', 'wide'), parts along dimension 0, may hold values from -0.03125 to 0.03125
- basis_out: bfloat16 [16384, 8192], P('groups', 'wide'), parts along dimension 0, may hold values from -0.0625 to 0.0625
Outputs:
- eigenvalues: bfloat16 [3072, 8192], P(('groups', 'wide')), parts along dimension 0
The draws below stay inside these ranges and needn't reach their ends.
There are 2 independent parts, one for each index of `groups`. The reference program is written for one: setup_inputs(seed, part) draws one part's arguments, and reference() takes and returns one part's arrays. A program takes and returns all parts, laid end to end along the dimension named above; each array names one. Nothing has to cross between parts.
All inputs are finite; a program needn't handle non-finite values.
Results may differ from the reference program's by a relative error of at most 0.0045.
Values may be sent and summed in bfloat16 or wider, within the bound.
No kernel may reach another device: no remote copies, remote signals or barrier semaphores. Data moves between devices by JAX's collectives and lax.ppermute only.
A program may use at most 128 MiB of HBM per device.

```python
import jax
import jax.numpy as jnp

A = 28672
G = 8192
TOKENS = 80
KA = 1536


def shard_levels(stream_key, dims, cuts, low, largest):
    loudness, own = 1.0, jax.random.fold_in(stream_key, 6)
    for dim, shards_of in cuts:
        draws = jnp.exp(jax.random.uniform(jax.random.fold_in(own, dim), (shards_of,), jnp.float32, low / len(cuts), largest / len(cuts)))
        loudness = loudness * jnp.repeat(draws, dims[dim] // shards_of).reshape([-1 if axis == dim else 1 for axis in range(len(dims))])
    return loudness


def gaussian(stream_key, extent, deviation, most, pieces=(), held_as=jnp.bfloat16):
    result = deviation * jax.random.normal(stream_key, extent, jnp.float32)
    if pieces:
        result = result * shard_levels(stream_key, extent, pieces, -0.22, 0.18)
    return jnp.clip(result, -most, most).astype(held_as)


def setup_inputs(seed: int = 0, part: int = 0) -> dict:
    keys = jax.random.split(jax.random.key(seed), 5)
    part_keys = jax.random.split(jax.random.fold_in(keys[4], part), 5)
    acts = gaussian(part_keys[0], (TOKENS, A), 1.0, 6.0, ((0, 16),))
    grads = gaussian(part_keys[1], (TOKENS, G), 1.0, 6.0, ((0, 16),))
    basis_in = gaussian(part_keys[2], (A, KA), A ** -0.5, 0.03125, ((1, 16),))
    basis_out = gaussian(part_keys[3], (G, G), G ** -0.5, 0.0625, ((1, 16),))
    return dict(acts=acts, grads=grads, basis_in=basis_in, basis_out=basis_out)


def reference(acts, grads, basis_in, basis_out):
    rot_in = jnp.dot(acts, basis_in, preferred_element_type=jnp.float32)
    sq_in = (rot_in * rot_in).astype(jnp.bfloat16)
    rot_out = jnp.dot(grads, basis_out, preferred_element_type=jnp.float32)
    sq_out = (rot_out * rot_out).astype(jnp.bfloat16)
    total = jnp.dot(sq_in.T, sq_out, preferred_element_type=jnp.float32)
    return (total / TOKENS).astype(jnp.bfloat16)
```

```python
import jax
import jax.numpy as jnp
from jax import lax
from jax.sharding import PartitionSpec as P

CORES = 2
SUBLANES = 8


def ring_of(chips):
    return list(range(0, chips, 2)) + list(range(1, chips, 2))[::-1]


class Ring:
    def __init__(self, devices):
        self.chips = devices // CORES
        self.order = ring_of(self.chips)

    def shift(self, by):
        n = self.chips
        return [
            (self.order[i] * CORES + c, self.order[(i + by) % n] * CORES + c)
            for i in range(n)
            for c in range(CORES)
        ]

    def swap(self):
        return [(d, d ^ 1) for d in range(self.chips * CORES)]

    def place(self):
        places = [self.order.index(chip) for chip in range(self.chips)]
        return jnp.array(places, jnp.int32)[lax.axis_index("wide") // CORES]

    def gather(self, block):
        n = self.chips
        got = {0: block}
        down = up = block
        for step in range(1, (n - 1) // 2 + 1):
            down = lax.ppermute(down, "wide", self.shift(1))
            up = lax.ppermute(up, "wide", self.shift(-1))
            got[n - step], got[step] = down, up
        if n % 2 == 0:
            half = block.shape[0] // 2
            first = lax.ppermute(down[:half], "wide", self.shift(1))
            second = lax.ppermute(up[half:], "wide", self.shift(-1))
            got[n // 2] = jnp.concatenate([first, second])
        return [got[r] for r in range(n)]


def local(acts, grads, basis_in, basis_out):
    devices = lax.axis_size("wide")
    ring = Ring(devices)
    tokens = acts.shape[0]
    total_tokens = tokens * devices
    core = lax.axis_index("wide") % CORES
    place = ring.place()

    def whole(array):
        width = array.shape[1]
        blocks = jnp.stack(ring.gather(array.reshape(tokens * SUBLANES, width // SUBLANES)))
        other = lax.ppermute(blocks, "wide", ring.swap())
        pair = jnp.stack([jnp.where(core == 0, blocks, other), jnp.where(core == 0, other, blocks)])
        return pair.reshape(total_tokens, width)

    def canonical(squares, axis):
        shape = squares.shape
        split = shape[:axis] + (CORES, ring.chips, tokens) + shape[axis + 1 :]
        return jnp.roll(squares.reshape(split), place, axis=axis + 1).reshape(shape)

    rotated = jnp.dot(whole(grads), basis_out, preferred_element_type=jnp.float32)
    sq_out = canonical((rotated * rotated).astype(jnp.bfloat16), 0)

    rotated = lax.dot_general(
        basis_in, whole(acts), (((0,), (1,)), ((), ())), preferred_element_type=jnp.float32
    )
    sq_in = canonical((rotated * rotated).astype(jnp.bfloat16), 1)

    blocks = jnp.stack(ring.gather(sq_out))
    other = lax.ppermute(blocks, "wide", ring.swap())
    pair = jnp.stack([jnp.where(core == 0, blocks, other), jnp.where(core == 0, other, blocks)], 1)
    order = jnp.array(ring.order, jnp.int32)
    at = jnp.argsort(order)
    pair = pair[(at - place) % ring.chips]
    gathered = pair.transpose(2, 0, 1, 3).reshape(total_tokens, -1)
    total = jnp.dot(sq_in, gathered, preferred_element_type=jnp.float32)
    return (total / total_tokens).astype(jnp.bfloat16)


def solution(mesh):
    return jax.shard_map(
        local,
        mesh=mesh,
        in_specs=(
            P(("groups", "wide"), None),
            P(("groups", "wide"), None),
            P("groups", "wide"),
            P("groups", "wide"),
        ),
        out_specs=P(("groups", "wide"), None),
        check_vma=False,
    )
```

```python
import functools

import jax
import jax.numpy as jnp
from jax import lax
from jax.experimental import pallas as pl
from jax.experimental.pallas import tpu as pltpu
from jax.sharding import PartitionSpec as P

CORES = 2
PAIR = 2
SUBLANES = 8
CHUNKS = 2
VMEM = pl.BlockSpec(memory_space=pltpu.VMEM)
SMEM = pl.BlockSpec(memory_space=pltpu.SMEM)


def along(devices, by):
    each = CORES * PAIR
    return [(d, (d + by * each) % devices) for d in range(devices)]


def across(devices):
    return [(d, d ^ CORES) for d in range(devices)]


def swap(devices):
    return [(d, d ^ 1) for d in range(devices)]


def send(block, pairs):
    return lax.ppermute(block, "wide", pairs)


def origin(me, devices, step, other_chip, other_core):
    each = CORES * PAIR
    pair = lax.rem(me // each + devices // each - step, devices // each)
    chip = lax.rem(me // CORES, PAIR)
    core = lax.rem(me, CORES)
    if other_chip:
        chip = 1 - chip
    if other_core:
        core = 1 - core
    return pair * PAIR + chip, core


def repeat(times, body, carry=None, loop=False):
    if loop or times > SUBLANES:
        return lax.fori_loop(0, times, body, carry)
    for step in range(times):
        carry = body(step, carry)
    return carry


def unfold_store(rows, slot, block):
    height = block.shape[0]
    at = pl.ds(pl.multiple_of(slot * height, SUBLANES), height)
    for tile in range(rows.shape[0]):
        rows[tile, at, :] = block[:, tile * 128 : (tile + 1) * 128].astype(jnp.float32)


def unfold_load(rows, fold, tokens):
    tiles = [rows[tile, pl.ds(fold, tokens, stride=SUBLANES), :] for tile in range(rows.shape[0])]
    return jnp.concatenate([tile.astype(jnp.bfloat16) for tile in tiles], 1)


def rotate_out_kernel(tokens, me_ref, z_ref, y_ref, cz_ref, cy_ref, basis_ref, sq_ref, rows):
    steps, height, width = z_ref.shape
    devices = steps * CORES * PAIR
    me = me_ref[0]
    for ref, chip_bit, core_bit in ((z_ref, 0, 0), (y_ref, 1, 0), (cz_ref, 0, 1), (cy_ref, 1, 1)):

        def put(step, _, ref=ref, chip_bit=chip_bit, core_bit=core_bit):
            chip, core = origin(me, devices, step, chip_bit, core_bit)
            unfold_store(rows, core * (devices // CORES) + chip, ref[step])

        repeat(steps, put)

    def add(fold, total):
        left = unfold_load(rows, fold, devices * tokens)
        right = basis_ref[pl.ds(pl.multiple_of(fold * width, 128), width), :]
        return total + jnp.dot(left, right, preferred_element_type=jnp.float32)

    total = repeat(SUBLANES, add, jnp.zeros(sq_ref.shape, jnp.float32), steps > SUBLANES)
    sq_ref[...] = (total * total).astype(sq_ref.dtype)


def rotate_out(tokens, me, z, y, cz, cy, basis):
    steps, height, width = z.shape
    total = steps * CORES * PAIR * tokens
    return pl.pallas_call(
        functools.partial(rotate_out_kernel, tokens),
        out_shape=jax.ShapeDtypeStruct((total, basis.shape[1]), jnp.bfloat16),
        in_specs=[SMEM] + [VMEM] * 5,
        out_specs=VMEM,
        scratch_shapes=[pltpu.VMEM((width // 128, total * SUBLANES, 128), jnp.float32)],
        compiler_params=pltpu.CompilerParams(vmem_limit_bytes=48 * 2**20),
        cost_estimate=pl.CostEstimate(
            flops=2 * total * basis.shape[0] * basis.shape[1], bytes_accessed=2 * basis.size, transcendentals=0
        ),
        name="rotate_out",
    )(me, z, y, cz, cy, basis)


def rotate_in_kernel(tokens, steps, me_ref, *refs):
    devices = steps * CORES * PAIR
    chips = devices // CORES
    blocks = refs[: CHUNKS * chips]
    mine_ref, theirs_ref, sq_mine_ref, sq_theirs_ref, rows = refs[CHUNKS * chips :]
    height, width = blocks[0].shape
    me = me_ref[0]
    total = jnp.zeros((2 * mine_ref.shape[0], chips * tokens), jnp.float32)
    for chunk in range(CHUNKS):
        for step in range(steps):
            for bit in range(PAIR):
                chip, _ = origin(me, devices, step, bit, 0)
                unfold_store(rows, chip, blocks[(chunk * steps + step) * PAIR + bit][...])

        def add(fold, total, chunk=chunk):
            at = pl.ds(pl.multiple_of((chunk * SUBLANES + fold) * width, 128), width)
            right = unfold_load(rows, fold, chips * tokens)
            left = jnp.concatenate([mine_ref[:, at], theirs_ref[:, at]])
            return total + lax.dot_general(
                left, right, (((1,), (1,)), ((), ())), preferred_element_type=jnp.float32
            )

        total = repeat(SUBLANES, add, total, steps > SUBLANES)
    squares = (total * total).astype(jnp.bfloat16)
    sq_mine_ref[...] = squares[: mine_ref.shape[0]]
    sq_theirs_ref[...] = squares[mine_ref.shape[0] :]


def rotate_in(tokens, steps, me, blocks, mine, theirs):
    chips = steps * PAIR
    height, width = blocks[0].shape
    out = jax.ShapeDtypeStruct((mine.shape[0], chips * tokens), jnp.bfloat16)
    return pl.pallas_call(
        functools.partial(rotate_in_kernel, tokens, steps),
        out_shape=(out, out),
        in_specs=[SMEM] + [VMEM] * (len(blocks) + 2),
        out_specs=(VMEM, VMEM),
        scratch_shapes=[pltpu.VMEM((width // 128, chips * height, 128), jnp.float32)],
        compiler_params=pltpu.CompilerParams(vmem_limit_bytes=48 * 2**20),
        cost_estimate=pl.CostEstimate(
            flops=4 * chips * tokens * mine.size, bytes_accessed=4 * mine.size, transcendentals=0
        ),
        name="rotate_in",
    )(me, *blocks, mine, theirs)


def combine_kernel(me_ref, own_ref, other_ref, z_ref, y_ref, cz_ref, cy_ref, out_ref):
    steps, total_tokens, width = z_ref.shape
    devices = steps * CORES * PAIR
    me = me_ref[0]
    own, other = own_ref[...].astype(jnp.float32), other_ref[...].astype(jnp.float32)
    first = lax.rem(me, CORES) == 0
    left = jnp.concatenate([jnp.where(first, own, other), jnp.where(first, other, own)], 1).astype(jnp.bfloat16)
    for ref, chip_bit, core_bit in ((z_ref, 0, 0), (y_ref, 1, 0), (cz_ref, 0, 1), (cy_ref, 1, 1)):

        def put(step, _, ref=ref, chip_bit=chip_bit, core_bit=core_bit):
            chip, core = origin(me, devices, step, chip_bit, core_bit)
            at = pl.multiple_of((chip * CORES + core) * width, 128)
            total = jnp.dot(left, ref[step], preferred_element_type=jnp.float32)
            out_ref[:, pl.ds(at, width)] = (total / total_tokens).astype(out_ref.dtype)

        repeat(steps, put)


def combine(me, own, other, z, y, cz, cy):
    steps, total_tokens, width = z.shape
    features = steps * CORES * PAIR * width
    return pl.pallas_call(
        combine_kernel,
        out_shape=jax.ShapeDtypeStruct((own.shape[0], features), jnp.bfloat16),
        in_specs=[SMEM] + [VMEM] * 6,
        out_specs=VMEM,
        compiler_params=pltpu.CompilerParams(vmem_limit_bytes=48 * 2**20),
        cost_estimate=pl.CostEstimate(
            flops=2 * own.shape[0] * total_tokens * features, bytes_accessed=4 * own.shape[0] * features, transcendentals=0
        ),
        name="combine",
    )(me, own, other, z, y, cz, cy)


def local(acts, grads, basis_in, basis_out):
    devices = lax.axis_size("wide")
    steps = devices // (CORES * PAIR)
    tokens = acts.shape[0]
    me = lax.axis_index("wide").astype(jnp.int32).reshape(1)

    def everywhere(block):
        z = jnp.stack([block] + [send(block, along(devices, step)) for step in range(1, steps)])
        y = send(z, across(devices))
        return z, y, send(z, swap(devices)), send(y, swap(devices))

    block = grads.reshape(tokens * SUBLANES, -1)
    block, acts, basis_in = lax.optimization_barrier((block, acts, basis_in))
    sq_out = rotate_out(tokens, me, *everywhere(block), basis_out)

    mine = basis_in.T
    theirs = send(mine, swap(devices))
    blocks = []
    width = acts.shape[1] // CHUNKS
    for chunk in range(CHUNKS):
        block = acts[:, chunk * width : (chunk + 1) * width].reshape(tokens * SUBLANES, -1)
        for step in range(steps):
            came = send(block, along(devices, step)) if step else block
            blocks += [came, send(came, across(devices))]
    own, given = rotate_in(tokens, steps, me, blocks, mine, theirs)
    other = send(given, swap(devices))
    return combine(me, own, other, *everywhere(sq_out))


def solution(mesh):
    return jax.shard_map(
        local,
        mesh=mesh,
        in_specs=(
            P(("groups", "wide"), None),
            P(("groups", "wide"), None),
            P("groups", "wide"),
            P("groups", "wide"),
        ),
        out_specs=P(("groups", "wide"), None),
        check_vma=False,
    )
```

```python
import functools

import jax
import jax.numpy as jnp
from jax import lax
from jax.experimental import pallas as pl
from jax.experimental.pallas import tpu as pltpu
from jax.sharding import PartitionSpec as P

CORES = 2
PAIR = 2
SUBLANES = 8
FOLDS = 2
CHUNKS = 2
VMEM = pl.BlockSpec(memory_space=pltpu.VMEM)
ANY = pl.BlockSpec(memory_space=pl.ANY)
SMEM = pl.BlockSpec(memory_space=pltpu.SMEM)


def along(devices, by):
    each = CORES * PAIR
    return [(d, (d + by * each) % devices) for d in range(devices)]


def across(devices):
    return [(d, d ^ CORES) for d in range(devices)]


def swap(devices):
    return [(d, d ^ 1) for d in range(devices)]


def send(block, pairs):
    return lax.ppermute(block, "wide", pairs)


def origin(me, devices, step, other_chip, other_core):
    each = CORES * PAIR
    pair = lax.rem(me // each + devices // each - step, devices // each)
    chip = lax.rem(me // CORES, PAIR)
    core = lax.rem(me, CORES)
    if other_chip:
        chip = 1 - chip
    if other_core:
        core = 1 - core
    return pair * PAIR + chip, core


def repeat(times, body, carry=None, loop=False):
    if loop or times > SUBLANES:
        return lax.fori_loop(0, times, body, carry)
    for step in range(times):
        carry = body(step, carry)
    return carry


def unfold_store(rows, slot, block):
    height = block.shape[0]
    at = pl.ds(pl.multiple_of(slot * height, SUBLANES), height)
    for tile in range(rows.shape[0]):
        rows[tile, at, :] = block[:, tile * 128 : (tile + 1) * 128].astype(jnp.float32)


def unfold_load(rows, fold, tokens):
    tiles = [rows[tile, pl.ds(fold, tokens, stride=SUBLANES), :] for tile in range(rows.shape[0])]
    return jnp.concatenate([tile.astype(jnp.bfloat16) for tile in tiles], 1)


def rotate_out_kernel(tokens, waits, me_ref, z_ref, y_ref, cz_ref, cy_ref, basis_ref, *refs):
    sq_ref, rows, total = refs[waits:]
    steps, height, width = z_ref.shape
    devices = steps * CORES * PAIR
    me = me_ref[0]

    @pl.when(pl.program_id(0) == 0)
    def _():
        for ref, chip_bit, core_bit in ((z_ref, 0, 0), (y_ref, 1, 0), (cz_ref, 0, 1), (cy_ref, 1, 1)):

            def put(step, _, ref=ref, chip_bit=chip_bit, core_bit=core_bit):
                chip, core = origin(me, devices, step, chip_bit, core_bit)
                unfold_store(rows, core * (devices // CORES) + chip, ref[step])

            repeat(steps, put)
        total[...] = jnp.zeros_like(total)

    def add(fold, _):
        left = unfold_load(rows, pl.program_id(0) * FOLDS + fold, devices * tokens)
        right = basis_ref[pl.ds(pl.multiple_of(fold * width, 128), width), :]
        total[...] += jnp.dot(left, right, preferred_element_type=jnp.float32)

    repeat(FOLDS, add, None, steps > SUBLANES)

    @pl.when(pl.program_id(0) == pl.num_programs(0) - 1)
    def _():
        sq_ref[...] = (total[...] * total[...]).astype(sq_ref.dtype)


def rotate_out(tokens, me, z, y, cz, cy, basis, waits):
    steps, height, width = z.shape
    total = steps * CORES * PAIR * tokens
    columns = basis.shape[1]
    return pl.pallas_call(
        functools.partial(rotate_out_kernel, tokens, len(waits)),
        grid=(SUBLANES // FOLDS,),
        out_shape=jax.ShapeDtypeStruct((total, columns), jnp.bfloat16),
        in_specs=[SMEM] + [VMEM] * 4 + [pl.BlockSpec((FOLDS * width, columns), lambda i: (i, 0))] + [ANY] * len(waits),
        out_specs=VMEM,
        scratch_shapes=[
            pltpu.VMEM((width // 128, total * SUBLANES, 128), jnp.float32),
            pltpu.VMEM((total, columns), jnp.float32),
        ],
        compiler_params=pltpu.CompilerParams(vmem_limit_bytes=48 * 2**20),
        cost_estimate=pl.CostEstimate(
            flops=2 * total * basis.shape[0] * columns, bytes_accessed=2 * basis.size, transcendentals=0
        ),
        name="rotate_out",
    )(me, z, y, cz, cy, basis, *waits)


def rotate_in_kernel(tokens, before, me_ref, own_ref, across_ref, z_ref, y_ref, mine_ref, theirs_ref, *refs):
    total_ref, rows = refs[before:]
    height, width = own_ref.shape
    steps = z_ref.shape[0] + 1
    devices = steps * CORES * PAIR
    chips = devices // CORES
    me = me_ref[0]

    @pl.when(pl.program_id(0) == 0)
    def _():
        unfold_store(rows, origin(me, devices, 0, 0, 0)[0], own_ref[...])
        unfold_store(rows, origin(me, devices, 0, 1, 0)[0], across_ref[...])
        for ref, chip_bit in ((z_ref, 0), (y_ref, 1)):

            def put(step, _, ref=ref, chip_bit=chip_bit):
                unfold_store(rows, origin(me, devices, step + 1, chip_bit, 0)[0], ref[step])

            repeat(steps - 1, put)
        total_ref[...] = refs[0][...] if before else jnp.zeros_like(total_ref)

    def add(fold, _):
        at = pl.ds(pl.multiple_of(fold * width, 128), width)
        right = unfold_load(rows, pl.program_id(0) * FOLDS + fold, chips * tokens)
        left = jnp.concatenate([mine_ref[:, at], theirs_ref[:, at]])
        total_ref[...] += lax.dot_general(left, right, (((1,), (1,)), ((), ())), preferred_element_type=jnp.float32)

    repeat(FOLDS, add, None, steps > SUBLANES)


def rotate_in(tokens, chunk, me, own, across, z, y, mine, theirs, before):
    height, width = own.shape
    chips = (z.shape[0] + 1) * PAIR
    basis = pl.BlockSpec((mine.shape[0], FOLDS * width), lambda i: (0, chunk * (SUBLANES // FOLDS) + i))
    return pl.pallas_call(
        functools.partial(rotate_in_kernel, tokens, len(before)),
        grid=(SUBLANES // FOLDS,),
        out_shape=jax.ShapeDtypeStruct((2 * mine.shape[0], chips * tokens), jnp.float32),
        in_specs=[SMEM] + [VMEM] * 4 + [basis] * 2 + [VMEM] * len(before),
        out_specs=VMEM,
        scratch_shapes=[pltpu.VMEM((width // 128, chips * height, 128), jnp.float32)],
        compiler_params=pltpu.CompilerParams(vmem_limit_bytes=48 * 2**20),
        cost_estimate=pl.CostEstimate(
            flops=4 * chips * tokens * mine.shape[0] * SUBLANES * width,
            bytes_accessed=4 * mine.shape[0] * SUBLANES * width,
            transcendentals=0,
        ),
        name="rotate_in",
    )(me, own, across, z, y, mine, theirs, *before)


def pile_kernel(blocks, *refs):
    for step in range(blocks):
        refs[-1][step] = refs[step][...]


def pile(blocks, waits):
    return pl.pallas_call(
        functools.partial(pile_kernel, len(blocks)),
        out_shape=jax.ShapeDtypeStruct((len(blocks), *blocks[0].shape), blocks[0].dtype),
        in_specs=[VMEM] * len(blocks) + [ANY] * len(waits),
        out_specs=VMEM,
        compiler_params=pltpu.CompilerParams(vmem_limit_bytes=48 * 2**20),
        cost_estimate=pl.CostEstimate(flops=0, bytes_accessed=2 * len(blocks) * blocks[0].size, transcendentals=0),
        name="pile",
    )(*blocks, *waits)


def combine_kernel(me_ref, own_ref, other_ref, z_ref, y_ref, cz_ref, cy_ref, out_ref):
    steps, total_tokens, width = z_ref.shape
    devices = steps * CORES * PAIR
    me = me_ref[0]
    own, other = own_ref[...].astype(jnp.float32), other_ref[...].astype(jnp.float32)
    first = lax.rem(me, CORES) == 0
    left = jnp.concatenate([jnp.where(first, own, other), jnp.where(first, other, own)], 1).astype(jnp.bfloat16)
    for ref, chip_bit, core_bit in ((z_ref, 0, 0), (y_ref, 1, 0), (cz_ref, 0, 1), (cy_ref, 1, 1)):

        def put(step, _, ref=ref, chip_bit=chip_bit, core_bit=core_bit):
            chip, core = origin(me, devices, step, chip_bit, core_bit)
            at = pl.multiple_of((chip * CORES + core) * width, 128)
            total = jnp.dot(left, ref[step], preferred_element_type=jnp.float32)
            out_ref[:, pl.ds(at, width)] = (total / total_tokens).astype(out_ref.dtype)

        repeat(steps, put)


def combine(me, own, other, z, y, cz, cy):
    steps, total_tokens, width = z.shape
    features = steps * CORES * PAIR * width
    return pl.pallas_call(
        combine_kernel,
        out_shape=jax.ShapeDtypeStruct((own.shape[0], features), jnp.bfloat16),
        in_specs=[SMEM] + [VMEM] * 6,
        out_specs=VMEM,
        compiler_params=pltpu.CompilerParams(vmem_limit_bytes=48 * 2**20),
        cost_estimate=pl.CostEstimate(
            flops=2 * own.shape[0] * total_tokens * features, bytes_accessed=4 * own.shape[0] * features, transcendentals=0
        ),
        name="combine",
    )(me, own, other, z, y, cz, cy)


def local(acts, grads, basis_in, basis_out):
    devices = lax.axis_size("wide")
    steps = devices // (CORES * PAIR)
    tokens = acts.shape[0]
    me = lax.axis_index("wide").astype(jnp.int32).reshape(1)

    def along_all(block):
        return [send(block, along(devices, step)) for step in range(1, steps)]

    def others(z):
        y = send(z, across(devices))
        return z, y, send(z, swap(devices)), send(y, swap(devices))

    mine = basis_in.T
    theirs = send(mine, swap(devices))
    width = acts.shape[1] // (CHUNKS * SUBLANES)
    folded = acts.reshape(tokens, CHUNKS, SUBLANES, width).transpose(1, 0, 2, 3).reshape(CHUNKS, -1, width)
    folded_across = send(folded, across(devices))
    block = grads.reshape(tokens * SUBLANES, -1)
    grads_z = others(jnp.stack([block] + along_all(block)))

    acts_z = []
    acts_y = []
    for chunk in range(CHUNKS):
        acts_z.append(jnp.stack(along_all(folded[chunk])))
        acts_y.append(send(acts_z[chunk], across(devices)))

    sq_out = rotate_out(tokens, me, *grads_z, basis_out, [acts_y[0]])
    came = along_all(sq_out)

    def part(chunk, before):
        return rotate_in(
            tokens, chunk, me, folded[chunk], folded_across[chunk], acts_z[chunk], acts_y[chunk], mine, theirs, before
        )

    total = part(0, [])
    z = pile([sq_out] + came, [total, acts_z[-1]])
    for chunk in range(1, CHUNKS):
        total = part(chunk, [total])
    squares = (total * total).astype(jnp.bfloat16)
    own, given = squares[: mine.shape[0]], squares[mine.shape[0] :]
    other = send(given, swap(devices))
    return combine(me, own, other, *others(z))


def solution(mesh):
    return jax.shard_map(
        local,
        mesh=mesh,
        in_specs=(
            P(("groups", "wide"), None),
            P(("groups", "wide"), None),
            P("groups", "wide"),
            P("groups", "wide"),
        ),
        out_specs=P(("groups", "wide"), None),
        check_vma=False,
    )
```

```python
import functools

import jax
import jax.numpy as jnp
from jax import lax
from jax.experimental import pallas as pl
from jax.experimental.pallas import tpu as pltpu
from jax.sharding import PartitionSpec as P

CORES = 2
PAIR = 2
SUBLANES = 8
FOLDS = 2
CHUNKS = 2
VMEM = pl.BlockSpec(memory_space=pltpu.VMEM)
ANY = pl.BlockSpec(memory_space=pl.ANY)
SMEM = pl.BlockSpec(memory_space=pltpu.SMEM)


def along(devices, by):
    each = CORES * PAIR
    return [(d, (d + by * each) % devices) for d in range(devices)]


def across(devices):
    return [(d, d ^ CORES) for d in range(devices)]


def swap(devices):
    return [(d, d ^ 1) for d in range(devices)]


def send(block, pairs):
    return lax.ppermute(block, "wide", pairs)


def origin(me, devices, step, other_chip, other_core):
    each = CORES * PAIR
    pair = lax.rem(me // each + devices // each - step, devices // each)
    chip = lax.rem(me // CORES, PAIR)
    core = lax.rem(me, CORES)
    if other_chip:
        chip = 1 - chip
    if other_core:
        core = 1 - core
    return pair * PAIR + chip, core


def repeat(times, body, carry=None, loop=False):
    if loop or times > SUBLANES:
        return lax.fori_loop(0, times, body, carry)
    for step in range(times):
        carry = body(step, carry)
    return carry


def unfold_store(rows, slot, block):
    height = block.shape[0]
    at = pl.ds(pl.multiple_of(slot * height, SUBLANES), height)
    for tile in range(rows.shape[0]):
        rows[tile, at, :] = block[:, tile * 128 : (tile + 1) * 128].astype(jnp.float32)


def unfold_load(rows, fold, tokens):
    tiles = [rows[tile, pl.ds(fold, tokens, stride=SUBLANES), :] for tile in range(rows.shape[0])]
    return jnp.concatenate([tile.astype(jnp.bfloat16) for tile in tiles], 1)


def rotate_out_kernel(tokens, waits, me_ref, z_ref, y_ref, cz_ref, cy_ref, basis_ref, *refs):
    sq_ref, rows, total = refs[waits:]
    steps, height, width = z_ref.shape
    devices = steps * CORES * PAIR
    me = me_ref[0]

    @pl.when(pl.program_id(0) == 0)
    def _():
        for ref, chip_bit, core_bit in ((z_ref, 0, 0), (y_ref, 1, 0), (cz_ref, 0, 1), (cy_ref, 1, 1)):

            def put(step, _, ref=ref, chip_bit=chip_bit, core_bit=core_bit):
                chip, core = origin(me, devices, step, chip_bit, core_bit)
                unfold_store(rows, core * (devices // CORES) + chip, ref[step])

            repeat(steps, put)
        total[...] = jnp.zeros_like(total)

    def add(fold, _):
        left = unfold_load(rows, pl.program_id(0) * FOLDS + fold, devices * tokens)
        right = basis_ref[pl.ds(pl.multiple_of(fold * width, 128), width), :]
        total[...] += jnp.dot(left, right, preferred_element_type=jnp.float32)

    repeat(FOLDS, add, None, steps > SUBLANES)

    @pl.when(pl.program_id(0) == pl.num_programs(0) - 1)
    def _():
        sq_ref[...] = (total[...] * total[...]).astype(sq_ref.dtype)


def rotate_out(tokens, me, z, y, cz, cy, basis, waits):
    steps, height, width = z.shape
    total = steps * CORES * PAIR * tokens
    columns = basis.shape[1]
    return pl.pallas_call(
        functools.partial(rotate_out_kernel, tokens, len(waits)),
        grid=(SUBLANES // FOLDS,),
        out_shape=jax.ShapeDtypeStruct((total, columns), jnp.bfloat16),
        in_specs=[SMEM] + [VMEM] * 4 + [pl.BlockSpec((FOLDS * width, columns), lambda i: (i, 0))] + [ANY] * len(waits),
        out_specs=VMEM,
        scratch_shapes=[
            pltpu.VMEM((width // 128, total * SUBLANES, 128), jnp.float32),
            pltpu.VMEM((total, columns), jnp.float32),
        ],
        compiler_params=pltpu.CompilerParams(vmem_limit_bytes=48 * 2**20),
        cost_estimate=pl.CostEstimate(
            flops=2 * total * basis.shape[0] * columns, bytes_accessed=2 * basis.size, transcendentals=0
        ),
        name="rotate_out",
    )(me, z, y, cz, cy, basis, *waits)


def rotate_in_kernel(tokens, before, me_ref, own_ref, across_ref, z_ref, y_ref, mine_ref, theirs_ref, *refs):
    total_ref, rows = refs[before:]
    height, width = own_ref.shape
    steps = z_ref.shape[0] + 1
    devices = steps * CORES * PAIR
    chips = devices // CORES
    me = me_ref[0]

    @pl.when(pl.program_id(0) == 0)
    def _():
        unfold_store(rows, origin(me, devices, 0, 0, 0)[0], own_ref[...])
        unfold_store(rows, origin(me, devices, 0, 1, 0)[0], across_ref[...])
        for ref, chip_bit in ((z_ref, 0), (y_ref, 1)):

            def put(step, _, ref=ref, chip_bit=chip_bit):
                unfold_store(rows, origin(me, devices, step + 1, chip_bit, 0)[0], ref[step])

            repeat(steps - 1, put)
        total_ref[...] = refs[0][...] if before else jnp.zeros_like(total_ref)

    def add(fold, _):
        at = pl.ds(pl.multiple_of(fold * width, 128), width)
        right = unfold_load(rows, pl.program_id(0) * FOLDS + fold, chips * tokens)
        left = jnp.concatenate([mine_ref[:, at], theirs_ref[:, at]])
        total_ref[...] += lax.dot_general(left, right, (((1,), (1,)), ((), ())), preferred_element_type=jnp.float32)

    repeat(FOLDS, add, None, steps > SUBLANES)


def rotate_in(tokens, chunk, me, own, across, z, y, mine, theirs, before):
    height, width = own.shape
    chips = (z.shape[0] + 1) * PAIR
    basis = pl.BlockSpec((mine.shape[0], FOLDS * width), lambda i: (0, chunk * (SUBLANES // FOLDS) + i))
    return pl.pallas_call(
        functools.partial(rotate_in_kernel, tokens, len(before)),
        grid=(SUBLANES // FOLDS,),
        out_shape=jax.ShapeDtypeStruct((2 * mine.shape[0], chips * tokens), jnp.float32),
        in_specs=[SMEM] + [VMEM] * 4 + [basis] * 2 + [VMEM] * len(before),
        out_specs=VMEM,
        scratch_shapes=[pltpu.VMEM((width // 128, chips * height, 128), jnp.float32)],
        compiler_params=pltpu.CompilerParams(vmem_limit_bytes=48 * 2**20),
        cost_estimate=pl.CostEstimate(
            flops=4 * chips * tokens * mine.shape[0] * SUBLANES * width,
            bytes_accessed=4 * mine.shape[0] * SUBLANES * width,
            transcendentals=0,
        ),
        name="rotate_in",
    )(me, own, across, z, y, mine, theirs, *before)


def pile_kernel(blocks, *refs):
    for step in range(blocks):
        refs[-1][step] = refs[step][...]


def pile(blocks, waits):
    return pl.pallas_call(
        functools.partial(pile_kernel, len(blocks)),
        out_shape=jax.ShapeDtypeStruct((len(blocks), *blocks[0].shape), blocks[0].dtype),
        in_specs=[VMEM] * len(blocks) + [ANY] * len(waits),
        out_specs=VMEM,
        compiler_params=pltpu.CompilerParams(vmem_limit_bytes=48 * 2**20),
        cost_estimate=pl.CostEstimate(flops=0, bytes_accessed=2 * len(blocks) * blocks[0].size, transcendentals=0),
        name="pile",
    )(*blocks, *waits)


def combine_kernel(me_ref, own_ref, other_ref, z_ref, y_ref, cz_ref, cy_ref, out_ref):
    steps, total_tokens, width = z_ref.shape
    devices = steps * CORES * PAIR
    me = me_ref[0]
    own, other = own_ref[...].astype(jnp.float32), other_ref[...].astype(jnp.float32)
    first = lax.rem(me, CORES) == 0
    left = jnp.concatenate([jnp.where(first, own, other), jnp.where(first, other, own)], 1).astype(jnp.bfloat16)
    for ref, chip_bit, core_bit in ((z_ref, 0, 0), (y_ref, 1, 0), (cz_ref, 0, 1), (cy_ref, 1, 1)):

        def put(step, _, ref=ref, chip_bit=chip_bit, core_bit=core_bit):
            chip, core = origin(me, devices, step, chip_bit, core_bit)
            at = pl.multiple_of((chip * CORES + core) * width, 128)
            total = jnp.dot(left, ref[step], preferred_element_type=jnp.float32)
            out_ref[:, pl.ds(at, width)] = (total / total_tokens).astype(out_ref.dtype)

        repeat(steps, put)


def combine(me, own, other, z, y, cz, cy):
    steps, total_tokens, width = z.shape
    features = steps * CORES * PAIR * width
    return pl.pallas_call(
        combine_kernel,
        out_shape=jax.ShapeDtypeStruct((own.shape[0], features), jnp.bfloat16),
        in_specs=[SMEM] + [VMEM] * 6,
        out_specs=VMEM,
        compiler_params=pltpu.CompilerParams(vmem_limit_bytes=48 * 2**20),
        cost_estimate=pl.CostEstimate(
            flops=2 * own.shape[0] * total_tokens * features, bytes_accessed=4 * own.shape[0] * features, transcendentals=0
        ),
        name="combine",
    )(me, own, other, z, y, cz, cy)


def local(acts, grads, basis_in, basis_out):
    devices = lax.axis_size("wide")
    steps = devices // (CORES * PAIR)
    tokens = acts.shape[0]
    me = lax.axis_index("wide").astype(jnp.int32).reshape(1)

    def along_all(block):
        return [send(block, along(devices, step)) for step in range(1, steps)]

    def others(z):
        y = send(z, across(devices))
        return z, y, send(z, swap(devices)), send(y, swap(devices))

    mine = basis_in.T
    theirs = send(mine, swap(devices))
    width = acts.shape[1] // (CHUNKS * SUBLANES)
    folded = acts.reshape(tokens, CHUNKS, SUBLANES, width).transpose(1, 0, 2, 3).reshape(CHUNKS, -1, width)
    folded_across = send(folded, across(devices))
    block = grads.reshape(tokens * SUBLANES, -1)
    grads_z = others(pile([block] + along_all(block), [folded_across]))

    acts_z = []
    acts_y = []
    for chunk in range(CHUNKS):
        acts_z.append(pile(along_all(folded[chunk]), [] if chunk else [grads_z[1]]))
        acts_y.append(send(acts_z[chunk], across(devices)))

    sq_out = rotate_out(tokens, me, *grads_z, basis_out, [acts_z[0]])
    came = along_all(sq_out)

    def part(chunk, before):
        return rotate_in(
            tokens, chunk, me, folded[chunk], folded_across[chunk], acts_z[chunk], acts_y[chunk], mine, theirs, before
        )

    total = part(0, [])
    z = pile([sq_out] + came, [total, acts_z[-1]])
    for chunk in range(1, CHUNKS):
        total = part(chunk, [total])
    squares = (total * total).astype(jnp.bfloat16)
    own, given = squares[: mine.shape[0]], squares[mine.shape[0] :]
    other = send(given, swap(devices))
    return combine(me, own, other, *others(z))


def solution(mesh):
    return jax.shard_map(
        local,
        mesh=mesh,
        in_specs=(
            P(("groups", "wide"), None),
            P(("groups", "wide"), None),
            P("groups", "wide"),
            P("groups", "wide"),
        ),
        out_specs=P(("groups", "wide"), None),
        check_vma=False,
    )
```

```python
import functools

import jax
import jax.numpy as jnp
from jax import lax
from jax.experimental import pallas as pl
from jax.experimental.pallas import tpu as pltpu
from jax.sharding import PartitionSpec as P

CORES = 2
PAIR = 2
SUBLANES = 8
FOLDS = 2
CHUNKS = 2
VMEM = pl.BlockSpec(memory_space=pltpu.VMEM)
ANY = pl.BlockSpec(memory_space=pl.ANY)
SMEM = pl.BlockSpec(memory_space=pltpu.SMEM)


def row(block, devices):
    each = CORES * PAIR
    steps = devices // each
    rows = [[first + each * step for step in range(steps)] for first in range(each)]
    copies = jnp.broadcast_to(block, (steps, *block.shape))
    return lax.all_to_all(copies, "wide", 0, 0, axis_index_groups=rows)


def across(devices):
    return [(d, d ^ CORES) for d in range(devices)]


def swap(devices):
    return [(d, d ^ 1) for d in range(devices)]


def send(block, pairs):
    return lax.ppermute(block, "wide", pairs)


def origin(me, step, other_chip, other_core):
    chip = lax.rem(me // CORES, PAIR)
    core = lax.rem(me, CORES)
    if other_chip:
        chip = 1 - chip
    if other_core:
        core = 1 - core
    return step * PAIR + chip, core


def repeat(times, body, carry=None, loop=False):
    if loop or times > SUBLANES:
        return lax.fori_loop(0, times, body, carry)
    for step in range(times):
        carry = body(step, carry)
    return carry


def unfold_store(rows, slot, block):
    height = block.shape[0]
    at = pl.ds(pl.multiple_of(slot * height, SUBLANES), height)
    for tile in range(rows.shape[0]):
        rows[tile, at, :] = block[:, tile * 128 : (tile + 1) * 128].astype(jnp.float32)


def unfold_load(rows, fold, tokens):
    tiles = [rows[tile, pl.ds(fold, tokens, stride=SUBLANES), :] for tile in range(rows.shape[0])]
    return jnp.concatenate([tile.astype(jnp.bfloat16) for tile in tiles], 1)


def rotate_out_kernel(tokens, waits, me_ref, z_ref, y_ref, cz_ref, cy_ref, basis_ref, *refs):
    sq_ref, rows, total = refs[waits:]
    steps, height, width = z_ref.shape
    devices = steps * CORES * PAIR
    me = me_ref[0]

    @pl.when(pl.program_id(0) == 0)
    def _():
        for ref, chip_bit, core_bit in ((z_ref, 0, 0), (y_ref, 1, 0), (cz_ref, 0, 1), (cy_ref, 1, 1)):

            def put(step, _, ref=ref, chip_bit=chip_bit, core_bit=core_bit):
                chip, core = origin(me, step, chip_bit, core_bit)
                unfold_store(rows, core * (devices // CORES) + chip, ref[step])

            repeat(steps, put)
        total[...] = jnp.zeros_like(total)

    def add(fold, _):
        left = unfold_load(rows, pl.program_id(0) * FOLDS + fold, devices * tokens)
        right = basis_ref[pl.ds(pl.multiple_of(fold * width, 128), width), :]
        total[...] += jnp.dot(left, right, preferred_element_type=jnp.float32)

    repeat(FOLDS, add, None, steps > SUBLANES)

    @pl.when(pl.program_id(0) == pl.num_programs(0) - 1)
    def _():
        sq_ref[...] = (total[...] * total[...]).astype(sq_ref.dtype)


def rotate_out(tokens, me, z, y, cz, cy, basis, waits):
    steps, height, width = z.shape
    total = steps * CORES * PAIR * tokens
    columns = basis.shape[1]
    return pl.pallas_call(
        functools.partial(rotate_out_kernel, tokens, len(waits)),
        grid=(SUBLANES // FOLDS,),
        out_shape=jax.ShapeDtypeStruct((total, columns), jnp.bfloat16),
        in_specs=[SMEM] + [VMEM] * 4 + [pl.BlockSpec((FOLDS * width, columns), lambda i: (i, 0))] + [ANY] * len(waits),
        out_specs=VMEM,
        scratch_shapes=[
            pltpu.VMEM((width // 128, total * SUBLANES, 128), jnp.float32),
            pltpu.VMEM((total, columns), jnp.float32),
        ],
        compiler_params=pltpu.CompilerParams(vmem_limit_bytes=48 * 2**20),
        cost_estimate=pl.CostEstimate(
            flops=2 * total * basis.shape[0] * columns, bytes_accessed=2 * basis.size, transcendentals=0
        ),
        name="rotate_out",
    )(me, z, y, cz, cy, basis, *waits)


def rotate_in_kernel(tokens, before, me_ref, z_ref, y_ref, mine_ref, theirs_ref, *refs):
    total_ref, rows = refs[before:]
    steps, _, width = z_ref.shape
    devices = steps * CORES * PAIR
    chips = devices // CORES
    me = me_ref[0]

    @pl.when(pl.program_id(0) == 0)
    def _():
        for ref, chip_bit in ((z_ref, 0), (y_ref, 1)):

            def put(step, _, ref=ref, chip_bit=chip_bit):
                unfold_store(rows, origin(me, step, chip_bit, 0)[0], ref[step])

            repeat(steps, put)
        total_ref[...] = refs[0][...] if before else jnp.zeros_like(total_ref)

    def add(fold, _):
        at = pl.ds(pl.multiple_of(fold * width, 128), width)
        right = unfold_load(rows, pl.program_id(0) * FOLDS + fold, chips * tokens)
        left = jnp.concatenate([mine_ref[:, at], theirs_ref[:, at]])
        total_ref[...] += lax.dot_general(left, right, (((1,), (1,)), ((), ())), preferred_element_type=jnp.float32)

    repeat(FOLDS, add, None, steps > SUBLANES)


def rotate_in(tokens, chunk, me, z, y, mine, theirs, before):
    steps, height, width = z.shape
    chips = steps * PAIR
    basis = pl.BlockSpec((mine.shape[0], FOLDS * width), lambda i: (0, chunk * (SUBLANES // FOLDS) + i))
    return pl.pallas_call(
        functools.partial(rotate_in_kernel, tokens, len(before)),
        grid=(SUBLANES // FOLDS,),
        out_shape=jax.ShapeDtypeStruct((2 * mine.shape[0], chips * tokens), jnp.float32),
        in_specs=[SMEM] + [VMEM] * 2 + [basis] * 2 + [VMEM] * len(before),
        out_specs=VMEM,
        scratch_shapes=[pltpu.VMEM((width // 128, chips * height, 128), jnp.float32)],
        compiler_params=pltpu.CompilerParams(vmem_limit_bytes=48 * 2**20),
        cost_estimate=pl.CostEstimate(
            flops=4 * chips * tokens * mine.shape[0] * SUBLANES * width,
            bytes_accessed=4 * mine.shape[0] * SUBLANES * width,
            transcendentals=0,
        ),
        name="rotate_in",
    )(me, z, y, mine, theirs, *before)


def combine_kernel(me_ref, own_ref, other_ref, z_ref, y_ref, cz_ref, cy_ref, out_ref):
    steps, total_tokens, width = z_ref.shape
    devices = steps * CORES * PAIR
    me = me_ref[0]
    own, other = own_ref[...].astype(jnp.float32), other_ref[...].astype(jnp.float32)
    first = lax.rem(me, CORES) == 0
    left = jnp.concatenate([jnp.where(first, own, other), jnp.where(first, other, own)], 1).astype(jnp.bfloat16)
    for ref, chip_bit, core_bit in ((z_ref, 0, 0), (y_ref, 1, 0), (cz_ref, 0, 1), (cy_ref, 1, 1)):

        def put(step, _, ref=ref, chip_bit=chip_bit, core_bit=core_bit):
            chip, core = origin(me, step, chip_bit, core_bit)
            at = pl.multiple_of((chip * CORES + core) * width, 128)
            total = jnp.dot(left, ref[step], preferred_element_type=jnp.float32)
            out_ref[:, pl.ds(at, width)] = (total / total_tokens).astype(out_ref.dtype)

        repeat(steps, put)


def combine(me, own, other, z, y, cz, cy):
    steps, total_tokens, width = z.shape
    features = steps * CORES * PAIR * width
    return pl.pallas_call(
        combine_kernel,
        out_shape=jax.ShapeDtypeStruct((own.shape[0], features), jnp.bfloat16),
        in_specs=[SMEM] + [VMEM] * 6,
        out_specs=VMEM,
        compiler_params=pltpu.CompilerParams(vmem_limit_bytes=48 * 2**20),
        cost_estimate=pl.CostEstimate(
            flops=2 * own.shape[0] * total_tokens * features, bytes_accessed=4 * own.shape[0] * features, transcendentals=0
        ),
        name="combine",
    )(me, own, other, z, y, cz, cy)


def local(acts, grads, basis_in, basis_out):
    devices = lax.axis_size("wide")
    tokens = acts.shape[0]
    me = lax.axis_index("wide").astype(jnp.int32).reshape(1)

    def others(z):
        y = send(z, across(devices))
        return z, y, send(z, swap(devices)), send(y, swap(devices))

    mine = basis_in.T
    theirs = send(mine, swap(devices))
    width = acts.shape[1] // (CHUNKS * SUBLANES)
    folded = acts.reshape(tokens, CHUNKS, SUBLANES, width).transpose(1, 0, 2, 3).reshape(CHUNKS, -1, width)
    grads_all = others(row(grads.reshape(tokens * SUBLANES, -1), devices))
    acts_z = [row(folded[chunk], devices) for chunk in range(CHUNKS)]
    acts_y = [send(z, across(devices)) for z in acts_z]

    sq_out = rotate_out(tokens, me, *grads_all, basis_out, [acts_z[0]])

    total = []
    for chunk in range(CHUNKS):
        total = [rotate_in(tokens, chunk, me, acts_z[chunk], acts_y[chunk], mine, theirs, total)]
    squares = (total[0] * total[0]).astype(jnp.bfloat16)
    own, given = squares[: mine.shape[0]], squares[mine.shape[0] :]
    other = send(given, swap(devices))
    return combine(me, own, other, *others(row(sq_out, devices)))


def solution(mesh):
    return jax.shard_map(
        local,
        mesh=mesh,
        in_specs=(
            P(("groups", "wide"), None),
            P(("groups", "wide"), None),
            P("groups", "wide"),
            P("groups", "wide"),
        ),
        out_specs=P(("groups", "wide"), None),
        check_vma=False,
    )
```

```python
import functools

import jax
import jax.numpy as jnp
from jax import lax
from jax.experimental import pallas as pl
from jax.experimental.pallas import tpu as pltpu
from jax.sharding import PartitionSpec as P

CORES = 2
PAIR = 2
SUBLANES = 8
FOLDS = 2
CHUNKS = 2
VMEM = pl.BlockSpec(memory_space=pltpu.VMEM)
ANY = pl.BlockSpec(memory_space=pl.ANY)
SMEM = pl.BlockSpec(memory_space=pltpu.SMEM)


def along(devices, by):
    each = CORES * PAIR
    return [(d, (d + by * each) % devices) for d in range(devices)]


def across(devices):
    return [(d, d ^ CORES) for d in range(devices)]


def swap(devices):
    return [(d, d ^ 1) for d in range(devices)]


def send(block, pairs):
    return lax.ppermute(block, "wide", pairs)


def origin(me, devices, step, other_chip, other_core):
    each = CORES * PAIR
    pair = lax.rem(me // each + devices // each - step, devices // each)
    chip = lax.rem(me // CORES, PAIR)
    core = lax.rem(me, CORES)
    if other_chip:
        chip = 1 - chip
    if other_core:
        core = 1 - core
    return pair * PAIR + chip, core


def repeat(times, body, carry=None, loop=False):
    if loop or times > SUBLANES:
        return lax.fori_loop(0, times, body, carry)
    for step in range(times):
        carry = body(step, carry)
    return carry


def unfold_store(rows, slot, block):
    height = block.shape[0]
    at = pl.ds(pl.multiple_of(slot * height, SUBLANES), height)
    for tile in range(rows.shape[0]):
        rows[tile, at, :] = block[:, tile * 128 : (tile + 1) * 128].astype(jnp.float32)


def unfold_load(rows, fold, tokens):
    tiles = [rows[tile, pl.ds(fold, tokens, stride=SUBLANES), :] for tile in range(rows.shape[0])]
    return jnp.concatenate([tile.astype(jnp.bfloat16) for tile in tiles], 1)


def rotate_out_kernel(tokens, waits, me_ref, z_ref, y_ref, cz_ref, cy_ref, basis_ref, *refs):
    sq_ref, rows, total = refs[waits:]
    steps, height, width = z_ref.shape
    devices = steps * CORES * PAIR
    me = me_ref[0]

    @pl.when(pl.program_id(0) == 0)
    def _():
        for ref, chip_bit, core_bit in ((z_ref, 0, 0), (y_ref, 1, 0), (cz_ref, 0, 1), (cy_ref, 1, 1)):

            def put(step, _, ref=ref, chip_bit=chip_bit, core_bit=core_bit):
                chip, core = origin(me, devices, step, chip_bit, core_bit)
                unfold_store(rows, core * (devices // CORES) + chip, ref[step])

            repeat(steps, put)
        total[...] = jnp.zeros_like(total)

    def add(fold, _):
        left = unfold_load(rows, pl.program_id(0) * FOLDS + fold, devices * tokens)
        right = basis_ref[pl.ds(pl.multiple_of(fold * width, 128), width), :]
        total[...] += jnp.dot(left, right, preferred_element_type=jnp.float32)

    repeat(FOLDS, add, None, steps > SUBLANES)

    @pl.when(pl.program_id(0) == pl.num_programs(0) - 1)
    def _():
        sq_ref[...] = (total[...] * total[...]).astype(sq_ref.dtype)


def rotate_out(tokens, me, z, y, cz, cy, basis, waits):
    steps, height, width = z.shape
    total = steps * CORES * PAIR * tokens
    columns = basis.shape[1]
    return pl.pallas_call(
        functools.partial(rotate_out_kernel, tokens, len(waits)),
        grid=(SUBLANES // FOLDS,),
        out_shape=jax.ShapeDtypeStruct((total, columns), jnp.bfloat16),
        in_specs=[SMEM] + [VMEM] * 4 + [pl.BlockSpec((FOLDS * width, columns), lambda i: (i, 0))] + [ANY] * len(waits),
        out_specs=VMEM,
        scratch_shapes=[
            pltpu.VMEM((width // 128, total * SUBLANES, 128), jnp.float32),
            pltpu.VMEM((total, columns), jnp.float32),
        ],
        compiler_params=pltpu.CompilerParams(vmem_limit_bytes=48 * 2**20),
        cost_estimate=pl.CostEstimate(
            flops=2 * total * basis.shape[0] * columns, bytes_accessed=2 * basis.size, transcendentals=0
        ),
        name="rotate_out",
    )(me, z, y, cz, cy, basis, *waits)


def rotate_in_kernel(tokens, before, me_ref, own_ref, across_ref, z_ref, y_ref, mine_ref, theirs_ref, *refs):
    total_ref, rows = refs[before:]
    height, width = own_ref.shape
    steps = z_ref.shape[0] + 1
    devices = steps * CORES * PAIR
    chips = devices // CORES
    me = me_ref[0]

    @pl.when(pl.program_id(0) == 0)
    def _():
        unfold_store(rows, origin(me, devices, 0, 0, 0)[0], own_ref[...])
        unfold_store(rows, origin(me, devices, 0, 1, 0)[0], across_ref[...])
        for ref, chip_bit in ((z_ref, 0), (y_ref, 1)):

            def put(step, _, ref=ref, chip_bit=chip_bit):
                unfold_store(rows, origin(me, devices, step + 1, chip_bit, 0)[0], ref[step])

            repeat(steps - 1, put)
        total_ref[...] = refs[0][...] if before else jnp.zeros_like(total_ref)

    def add(fold, _):
        at = pl.ds(pl.multiple_of(fold * width, 128), width)
        right = unfold_load(rows, pl.program_id(0) * FOLDS + fold, chips * tokens)
        left = jnp.concatenate([mine_ref[:, at], theirs_ref[:, at]])
        total_ref[...] += lax.dot_general(left, right, (((1,), (1,)), ((), ())), preferred_element_type=jnp.float32)

    repeat(FOLDS, add, None, steps > SUBLANES)


def rotate_in(tokens, chunk, me, own, across, z, y, mine, theirs, before):
    height, width = own.shape
    chips = (z.shape[0] + 1) * PAIR
    basis = pl.BlockSpec((mine.shape[0], FOLDS * width), lambda i: (0, chunk * (SUBLANES // FOLDS) + i))
    return pl.pallas_call(
        functools.partial(rotate_in_kernel, tokens, len(before)),
        grid=(SUBLANES // FOLDS,),
        out_shape=jax.ShapeDtypeStruct((2 * mine.shape[0], chips * tokens), jnp.float32),
        in_specs=[SMEM] + [VMEM] * 4 + [basis] * 2 + [VMEM] * len(before),
        out_specs=VMEM,
        scratch_shapes=[pltpu.VMEM((width // 128, chips * height, 128), jnp.float32)],
        compiler_params=pltpu.CompilerParams(vmem_limit_bytes=48 * 2**20),
        cost_estimate=pl.CostEstimate(
            flops=4 * chips * tokens * mine.shape[0] * SUBLANES * width,
            bytes_accessed=4 * mine.shape[0] * SUBLANES * width,
            transcendentals=0,
        ),
        name="rotate_in",
    )(me, own, across, z, y, mine, theirs, *before)


def pile_kernel(blocks, *refs):
    for step in range(blocks):
        refs[-1][step] = refs[step][...]


def pile(blocks, waits):
    return pl.pallas_call(
        functools.partial(pile_kernel, len(blocks)),
        out_shape=jax.ShapeDtypeStruct((len(blocks), *blocks[0].shape), blocks[0].dtype),
        in_specs=[VMEM] * len(blocks) + [ANY] * len(waits),
        out_specs=VMEM,
        compiler_params=pltpu.CompilerParams(vmem_limit_bytes=48 * 2**20),
        cost_estimate=pl.CostEstimate(flops=0, bytes_accessed=2 * len(blocks) * blocks[0].size, transcendentals=0),
        name="pile",
    )(*blocks, *waits)


def combine_kernel(me_ref, own_ref, other_ref, z_ref, y_ref, cz_ref, cy_ref, out_ref):
    steps, total_tokens, width = z_ref.shape
    devices = steps * CORES * PAIR
    me = me_ref[0]
    own, other = own_ref[...].astype(jnp.float32), other_ref[...].astype(jnp.float32)
    first = lax.rem(me, CORES) == 0
    left = jnp.concatenate([jnp.where(first, own, other), jnp.where(first, other, own)], 1).astype(jnp.bfloat16)
    for ref, chip_bit, core_bit in ((z_ref, 0, 0), (y_ref, 1, 0), (cz_ref, 0, 1), (cy_ref, 1, 1)):

        def put(step, _, ref=ref, chip_bit=chip_bit, core_bit=core_bit):
            chip, core = origin(me, devices, step, chip_bit, core_bit)
            at = pl.multiple_of((chip * CORES + core) * width, 128)
            total = jnp.dot(left, ref[step], preferred_element_type=jnp.float32)
            out_ref[:, pl.ds(at, width)] = (total / total_tokens).astype(out_ref.dtype)

        repeat(steps, put)


def combine(me, own, other, z, y, cz, cy):
    steps, total_tokens, width = z.shape
    features = steps * CORES * PAIR * width
    return pl.pallas_call(
        combine_kernel,
        out_shape=jax.ShapeDtypeStruct((own.shape[0], features), jnp.bfloat16),
        in_specs=[SMEM] + [VMEM] * 6,
        out_specs=VMEM,
        compiler_params=pltpu.CompilerParams(vmem_limit_bytes=48 * 2**20),
        cost_estimate=pl.CostEstimate(
            flops=2 * own.shape[0] * total_tokens * features, bytes_accessed=4 * own.shape[0] * features, transcendentals=0
        ),
        name="combine",
    )(me, own, other, z, y, cz, cy)


def local(acts, grads, basis_in, basis_out):
    devices = lax.axis_size("wide")
    steps = devices // (CORES * PAIR)
    tokens = acts.shape[0]
    me = lax.axis_index("wide").astype(jnp.int32).reshape(1)

    def along_all(block):
        return [send(block, along(devices, step)) for step in range(1, steps)]

    def others(z):
        y = send(z, across(devices))
        return z, y, send(z, swap(devices)), send(y, swap(devices))

    mine = basis_in.T
    theirs = send(mine, swap(devices))
    width = acts.shape[1] // (CHUNKS * SUBLANES)
    folded = acts.reshape(tokens, CHUNKS, SUBLANES, width).transpose(1, 0, 2, 3).reshape(CHUNKS, -1, width)
    folded_across = send(folded, across(devices))
    block = grads.reshape(tokens * SUBLANES, -1)
    grads_z = others(pile([block] + along_all(block), []))

    acts_z = [pile(along_all(folded[0]), [])]
    acts_y = [send(acts_z[0], across(devices))]
    sq_out = rotate_out(tokens, me, *grads_z, basis_out, [acts_z[0]])
    came = along_all(sq_out)
    acts_z.append(pile(along_all(folded[1]), [sq_out]))
    acts_y.append(send(acts_z[1], across(devices)))

    def part(chunk, before):
        return rotate_in(
            tokens, chunk, me, folded[chunk], folded_across[chunk], acts_z[chunk], acts_y[chunk], mine, theirs, before
        )

    total = part(0, [])
    z = pile([sq_out] + came, [total, acts_z[-1]])
    for chunk in range(1, CHUNKS):
        total = part(chunk, [total])
    squares = (total * total).astype(jnp.bfloat16)
    own, given = squares[: mine.shape[0]], squares[mine.shape[0] :]
    other = send(given, swap(devices))
    return combine(me, own, other, *others(z))


def solution(mesh):
    return jax.shard_map(
        local,
        mesh=mesh,
        in_specs=(
            P(("groups", "wide"), None),
            P(("groups", "wide"), None),
            P("groups", "wide"),
            P("groups", "wide"),
        ),
        out_specs=P(("groups", "wide"), None),
        check_vma=False,
    )
```

```python
import functools

import jax
import jax.numpy as jnp
from jax import lax
from jax.experimental import pallas as pl
from jax.experimental.pallas import tpu as pltpu
from jax.sharding import PartitionSpec as P

CORES = 2
PAIR = 2
SUBLANES = 8
FOLDS = 2
SHARES = (14, 14)
VMEM = pl.BlockSpec(memory_space=pltpu.VMEM)
ANY = pl.BlockSpec(memory_space=pl.ANY)
SMEM = pl.BlockSpec(memory_space=pltpu.SMEM)


def along(devices, by):
    each = CORES * PAIR
    return [(d, (d + by * each) % devices) for d in range(devices)]


def across(devices):
    return [(d, d ^ CORES) for d in range(devices)]


def swap(devices):
    return [(d, d ^ 1) for d in range(devices)]


def send(block, pairs):
    return lax.ppermute(block, "wide", pairs)


def origin(me, devices, step, other_chip, other_core):
    each = CORES * PAIR
    pair = lax.rem(me // each + devices // each - step, devices // each)
    chip = lax.rem(me // CORES, PAIR)
    core = lax.rem(me, CORES)
    if other_chip:
        chip = 1 - chip
    if other_core:
        core = 1 - core
    return pair * PAIR + chip, core


def repeat(times, body, carry=None, loop=False):
    if loop or times > SUBLANES:
        return lax.fori_loop(0, times, body, carry)
    for step in range(times):
        carry = body(step, carry)
    return carry


def unfold_store(rows, first, block):
    at = pl.ds(pl.multiple_of(first, SUBLANES), block.shape[0])
    for tile in range(rows.shape[0]):
        rows[tile, at, :] = block[:, tile * 128 : (tile + 1) * 128].astype(jnp.float32)


def unfold_load(rows, fold, tokens):
    tiles = [rows[tile, pl.ds(fold, tokens, stride=SUBLANES), :] for tile in range(rows.shape[0])]
    return jnp.concatenate([tile.astype(jnp.bfloat16) for tile in tiles], 1)


def rotate_out_kernel(tokens, waits, me_ref, z_ref, y_ref, cz_ref, cy_ref, basis_ref, *refs):
    sq_ref, rows, total = refs[waits:]
    steps, height, width = z_ref.shape
    devices = steps * CORES * PAIR
    me = me_ref[0]

    @pl.when(pl.program_id(0) == 0)
    def _():
        for ref, chip_bit, core_bit in ((z_ref, 0, 0), (y_ref, 1, 0), (cz_ref, 0, 1), (cy_ref, 1, 1)):

            def put(step, _, ref=ref, chip_bit=chip_bit, core_bit=core_bit):
                chip, core = origin(me, devices, step, chip_bit, core_bit)
                unfold_store(rows, (core * (devices // CORES) + chip) * height, ref[step])

            repeat(steps, put)
        total[...] = jnp.zeros_like(total)

    def add(fold, _):
        left = unfold_load(rows, pl.program_id(0) * FOLDS + fold, devices * tokens)
        right = basis_ref[pl.ds(pl.multiple_of(fold * width, 128), width), :]
        total[...] += jnp.dot(left, right, preferred_element_type=jnp.float32)

    repeat(FOLDS, add, None, steps > SUBLANES)

    @pl.when(pl.program_id(0) == pl.num_programs(0) - 1)
    def _():
        sq_ref[...] = (total[...] * total[...]).astype(sq_ref.dtype)


def rotate_out(tokens, me, z, y, cz, cy, basis, waits):
    steps, height, width = z.shape
    total = steps * CORES * PAIR * tokens
    columns = basis.shape[1]
    return pl.pallas_call(
        functools.partial(rotate_out_kernel, tokens, len(waits)),
        grid=(SUBLANES // FOLDS,),
        out_shape=jax.ShapeDtypeStruct((total, columns), jnp.bfloat16),
        in_specs=[SMEM] + [VMEM] * 4 + [pl.BlockSpec((FOLDS * width, columns), lambda i: (i, 0))] + [ANY] * len(waits),
        out_specs=VMEM,
        scratch_shapes=[
            pltpu.VMEM((width // 128, total * SUBLANES, 128), jnp.float32),
            pltpu.VMEM((total, columns), jnp.float32),
        ],
        compiler_params=pltpu.CompilerParams(vmem_limit_bytes=24 * 2**20),
        cost_estimate=pl.CostEstimate(
            flops=2 * total * basis.shape[0] * columns, bytes_accessed=2 * basis.size, transcendentals=0
        ),
        name="rotate_out",
    )(me, z, y, cz, cy, basis, *waits)


def rotate_in_kernel(tokens, start, before, me_ref, own_ref, across_ref, z_ref, y_ref, mine_ref, theirs_ref, *refs):
    total_ref, rows = refs[before:]
    height, whole = own_ref.shape
    width = z_ref.shape[2]
    steps = z_ref.shape[0] + 1
    devices = steps * CORES * PAIR
    chips = devices // CORES
    me = me_ref[0]
    unfold_store(rows, origin(me, devices, 0, 0, 0)[0] * height, own_ref[:, start : start + width])
    unfold_store(rows, origin(me, devices, 0, 1, 0)[0] * height, across_ref[:, start : start + width])
    for ref, chip_bit in ((z_ref, 0), (y_ref, 1)):

        def put(step, _, ref=ref, chip_bit=chip_bit):
            unfold_store(rows, origin(me, devices, step + 1, chip_bit, 0)[0] * height, ref[step])

        repeat(steps - 1, put)

    def add(fold, total):
        at = pl.ds(pl.multiple_of(fold * whole + start, 128), width)
        right = unfold_load(rows, fold, chips * tokens)
        left = jnp.concatenate([mine_ref[:, at], theirs_ref[:, at]])
        return total + lax.dot_general(left, right, (((1,), (1,)), ((), ())), preferred_element_type=jnp.float32)

    total = refs[0][...] if before else jnp.zeros(total_ref.shape, jnp.float32)
    total_ref[...] = repeat(SUBLANES, add, total, steps > SUBLANES)


def rotate_in(tokens, start, me, own, across, z, y, mine, theirs, before):
    height, width = z.shape[1:]
    chips = (z.shape[0] + 1) * PAIR
    return pl.pallas_call(
        functools.partial(rotate_in_kernel, tokens, start, len(before)),
        out_shape=jax.ShapeDtypeStruct((2 * mine.shape[0], chips * tokens), jnp.float32),
        in_specs=[SMEM] + [VMEM] * (6 + len(before)),
        out_specs=VMEM,
        scratch_shapes=[pltpu.VMEM((width // 128, chips * height, 128), jnp.float32)],
        compiler_params=pltpu.CompilerParams(vmem_limit_bytes=(28 if chips <= SUBLANES else 48) * 2**20),
        cost_estimate=pl.CostEstimate(
            flops=4 * chips * tokens * mine.shape[0] * SUBLANES * width,
            bytes_accessed=4 * mine.shape[0] * SUBLANES * width,
            transcendentals=0,
        ),
        name="rotate_in",
    )(me, own, across, z, y, mine, theirs, *before)


def pile_kernel(blocks, *refs):
    for step in range(blocks):
        refs[-1][step] = refs[step][...]


def pile(blocks, waits):
    return pl.pallas_call(
        functools.partial(pile_kernel, len(blocks)),
        out_shape=jax.ShapeDtypeStruct((len(blocks), *blocks[0].shape), blocks[0].dtype),
        in_specs=[VMEM] * len(blocks) + [ANY] * len(waits),
        out_specs=VMEM,
        compiler_params=pltpu.CompilerParams(vmem_limit_bytes=24 * 2**20),
        cost_estimate=pl.CostEstimate(flops=0, bytes_accessed=2 * len(blocks) * blocks[0].size, transcendentals=0),
        name="pile",
    )(*blocks, *waits)


def fetch_kernel(from_ref, *refs):
    to_ref, done = refs[-2:]
    copy = pltpu.make_async_copy(from_ref, to_ref, done)
    copy.start()
    copy.wait()


def fetch(array, waits):
    return pl.pallas_call(
        fetch_kernel,
        out_shape=jax.ShapeDtypeStruct(array.shape, array.dtype),
        in_specs=[ANY] * (1 + len(waits)),
        out_specs=VMEM,
        scratch_shapes=[pltpu.SemaphoreType.DMA],
        compiler_params=pltpu.CompilerParams(vmem_limit_bytes=16 * 2**20),
        cost_estimate=pl.CostEstimate(flops=0, bytes_accessed=2 * array.size, transcendentals=0),
        name="fetch",
    )(array, *waits)


def after(arrays, waits):
    return pl.pallas_call(
        lambda *refs: None,
        out_shape=[jax.ShapeDtypeStruct(array.shape, array.dtype) for array in arrays],
        in_specs=[ANY] * (len(arrays) + len(waits)),
        out_specs=[ANY] * len(arrays),
        input_output_aliases={i: i for i in range(len(arrays))},
        compiler_params=pltpu.CompilerParams(vmem_limit_bytes=2**20),
        cost_estimate=pl.CostEstimate(flops=0, bytes_accessed=0, transcendentals=0),
        name="after",
    )(*arrays, *waits)


def pile_kernel(blocks, *refs):
    for step in range(blocks):
        refs[-1][step] = refs[step][...]


def pile(blocks, waits):
    return pl.pallas_call(
        functools.partial(pile_kernel, len(blocks)),
        out_shape=jax.ShapeDtypeStruct((len(blocks), *blocks[0].shape), blocks[0].dtype),
        in_specs=[VMEM] * len(blocks) + [ANY] * len(waits),
        out_specs=VMEM,
        compiler_params=pltpu.CompilerParams(vmem_limit_bytes=24 * 2**20),
        cost_estimate=pl.CostEstimate(flops=0, bytes_accessed=2 * len(blocks) * blocks[0].size, transcendentals=0),
        name="pile",
    )(*blocks, *waits)


def combine_kernel(steps, me_ref, own_ref, other_ref, *refs):
    blocks, out_ref = refs[:-1], refs[-1]
    _, total_tokens, width = blocks[0].shape
    devices = steps * CORES * PAIR
    me = me_ref[0]
    own, other = own_ref[...].astype(jnp.float32), other_ref[...].astype(jnp.float32)
    first = lax.rem(me, CORES) == 0
    left = jnp.concatenate([jnp.where(first, own, other), jnp.where(first, other, own)], 1).astype(jnp.bfloat16)
    for i, block in enumerate(blocks):
        for bit in range(PAIR):
            chip, core = origin(me, devices, i % steps, bit, i // steps)
            at = pl.multiple_of((chip * CORES + core) * width, 128)
            total = jnp.dot(left, block[bit], preferred_element_type=jnp.float32)
            out_ref[:, pl.ds(at, width)] = (total / total_tokens).astype(out_ref.dtype)


def combine(me, own, other, blocks):
    steps = len(blocks) // CORES
    _, total_tokens, width = blocks[0].shape
    features = steps * PAIR * CORES * width
    return pl.pallas_call(
        functools.partial(combine_kernel, steps),
        out_shape=jax.ShapeDtypeStruct((own.shape[0], features), jnp.bfloat16),
        in_specs=[SMEM] + [VMEM] * (2 + len(blocks)),
        out_specs=VMEM,
        compiler_params=pltpu.CompilerParams(vmem_limit_bytes=24 * 2**20),
        cost_estimate=pl.CostEstimate(
            flops=2 * own.shape[0] * total_tokens * features, bytes_accessed=4 * own.shape[0] * features, transcendentals=0
        ),
        name="combine",
    )(me, own, other, *blocks)


def local(acts, grads, basis_in, basis_out):
    devices = lax.axis_size("wide")
    steps = devices // (CORES * PAIR)
    tokens = acts.shape[0]
    me = lax.axis_index("wide").astype(jnp.int32).reshape(1)

    def along_all(block):
        return [send(block, along(devices, step)) for step in range(1, steps)]

    folded = acts.reshape(tokens * SUBLANES, -1)
    folded_across = send(folded, across(devices))
    unit = folded.shape[1] // sum(SHARES)
    starts = [sum(SHARES[:chunk]) * unit for chunk in range(len(SHARES))]

    def chunk_along(chunk, waits):
        acts_s.append(along_all(folded[:, starts[chunk] : starts[chunk] + SHARES[chunk] * unit]))
        z = pile(acts_s[-1], waits)
        acts_z.append(z)
        acts_y.append(send(z, across(devices)))

    def part(chunk, before):
        return rotate_in(
            tokens, starts[chunk], me, folded, folded_across, acts_z[chunk], acts_y[chunk], mine, theirs, before
        )

    acts_s, acts_z, acts_y = [], [], []
    mine = basis_in.T
    theirs = send(mine, swap(devices))
    block = grads.reshape(tokens * SUBLANES, -1)
    grads_z = pile([block] + along_all(block), [folded_across])
    grads_y = send(grads_z, across(devices))
    chunk_along(0, [theirs])
    [grads_y] = after([grads_y], [acts_z[0]])
    grads_cz, grads_cy = send(grads_z, swap(devices)), send(grads_y, swap(devices))
    sq_out = rotate_out(tokens, me, grads_z, grads_y, grads_cz, grads_cy, basis_out, [acts_z[0]])
    sq_pair = pile([sq_out, send(sq_out, across(devices))], [acts_y[0]])
    came = [sq_pair] + along_all(sq_pair)
    chunk_along(1, [sq_pair])
    total = None
    for chunk in range(len(SHARES)):
        total = part(chunk, [total] if chunk else [])
    came[-1:] = after(came[-1:], [total])
    swapped = [send(pair, swap(devices)) for pair in came]
    squares = (total * total).astype(jnp.bfloat16)
    own, given = squares[: mine.shape[0]], squares[mine.shape[0] :]
    other = send(given, swap(devices))
    return combine(me, own, other, came + swapped)


def solution(mesh):
    return jax.shard_map(
        local,
        mesh=mesh,
        in_specs=(
            P(("groups", "wide"), None),
            P(("groups", "wide"), None),
            P("groups", "wide"),
            P("groups", "wide"),
        ),
        out_specs=P(("groups", "wide"), None),
        check_vma=False,
    )
```

```python
import functools

import jax
import jax.numpy as jnp
from jax import lax
from jax.experimental import pallas as pl
from jax.experimental.pallas import tpu as pltpu
from jax.sharding import PartitionSpec as P

CORES = 2
PAIR = 2
SUBLANES = 8
FOLDS = 2
CHUNKS = 2
VMEM = pl.BlockSpec(memory_space=pltpu.VMEM)
ANY = pl.BlockSpec(memory_space=pl.ANY)
SMEM = pl.BlockSpec(memory_space=pltpu.SMEM)


def along(devices, by):
    each = CORES * PAIR
    return [(d, (d + by * each) % devices) for d in range(devices)]


def across(devices):
    return [(d, d ^ CORES) for d in range(devices)]


def swap(devices):
    return [(d, d ^ 1) for d in range(devices)]


def send(block, pairs):
    return lax.ppermute(block, "wide", pairs)


def origin(me, devices, step, other_chip, other_core):
    each = CORES * PAIR
    pair = lax.rem(me // each + devices // each - step, devices // each)
    chip = lax.rem(me // CORES, PAIR)
    core = lax.rem(me, CORES)
    if other_chip:
        chip = 1 - chip
    if other_core:
        core = 1 - core
    return pair * PAIR + chip, core


def repeat(times, body, carry=None, loop=False):
    if loop or times > SUBLANES:
        return lax.fori_loop(0, times, body, carry)
    for step in range(times):
        carry = body(step, carry)
    return carry


def unfold_store(rows, slot, block):
    height = block.shape[0]
    at = pl.ds(pl.multiple_of(slot * height, SUBLANES), height)
    for tile in range(rows.shape[0]):
        rows[tile, at, :] = block[:, tile * 128 : (tile + 1) * 128].astype(jnp.float32)


def unfold_load(rows, fold, tokens):
    tiles = [rows[tile, pl.ds(fold, tokens, stride=SUBLANES), :] for tile in range(rows.shape[0])]
    return jnp.concatenate([tile.astype(jnp.bfloat16) for tile in tiles], 1)


def rotate_out_kernel(tokens, waits, me_ref, z_ref, y_ref, cz_ref, cy_ref, basis_ref, *refs):
    sq_ref, rows, total = refs[waits:]
    steps, height, width = z_ref.shape
    devices = steps * CORES * PAIR
    me = me_ref[0]

    @pl.when(pl.program_id(0) == 0)
    def _():
        for ref, chip_bit, core_bit in ((z_ref, 0, 0), (y_ref, 1, 0), (cz_ref, 0, 1), (cy_ref, 1, 1)):

            def put(step, _, ref=ref, chip_bit=chip_bit, core_bit=core_bit):
                chip, core = origin(me, devices, step, chip_bit, core_bit)
                unfold_store(rows, core * (devices // CORES) + chip, ref[step])

            repeat(steps, put)
        total[...] = jnp.zeros_like(total)

    def add(fold, _):
        left = unfold_load(rows, pl.program_id(0) * FOLDS + fold, devices * tokens)
        right = basis_ref[pl.ds(pl.multiple_of(fold * width, 128), width), :]
        total[...] += jnp.dot(left, right, preferred_element_type=jnp.float32)

    repeat(FOLDS, add, None, steps > SUBLANES)

    @pl.when(pl.program_id(0) == pl.num_programs(0) - 1)
    def _():
        sq_ref[...] = (total[...] * total[...]).astype(sq_ref.dtype)


def rotate_out(tokens, me, z, y, cz, cy, basis, waits):
    steps, height, width = z.shape
    total = steps * CORES * PAIR * tokens
    columns = basis.shape[1]
    return pl.pallas_call(
        functools.partial(rotate_out_kernel, tokens, len(waits)),
        grid=(SUBLANES // FOLDS,),
        out_shape=jax.ShapeDtypeStruct((total, columns), jnp.bfloat16),
        in_specs=[SMEM] + [VMEM] * 4 + [pl.BlockSpec((FOLDS * width, columns), lambda i: (i, 0))] + [ANY] * len(waits),
        out_specs=VMEM,
        scratch_shapes=[
            pltpu.VMEM((width // 128, total * SUBLANES, 128), jnp.float32),
            pltpu.VMEM((total, columns), jnp.float32),
        ],
        compiler_params=pltpu.CompilerParams(vmem_limit_bytes=24 * 2**20),
        cost_estimate=pl.CostEstimate(
            flops=2 * total * basis.shape[0] * columns, bytes_accessed=2 * basis.size, transcendentals=0
        ),
        name="rotate_out",
    )(me, z, y, cz, cy, basis, *waits)


def rotate_in_kernel(tokens, before, me_ref, own_ref, across_ref, z_ref, y_ref, mine_ref, theirs_ref, *refs):
    total_ref, rows = refs[before:]
    height, width = own_ref.shape
    steps = z_ref.shape[0] + 1
    devices = steps * CORES * PAIR
    chips = devices // CORES
    me = me_ref[0]

    @pl.when(pl.program_id(0) == 0)
    def _():
        unfold_store(rows, origin(me, devices, 0, 0, 0)[0], own_ref[...])
        unfold_store(rows, origin(me, devices, 0, 1, 0)[0], across_ref[...])
        for ref, chip_bit in ((z_ref, 0), (y_ref, 1)):

            def put(step, _, ref=ref, chip_bit=chip_bit):
                unfold_store(rows, origin(me, devices, step + 1, chip_bit, 0)[0], ref[step])

            repeat(steps - 1, put)
        total_ref[...] = refs[0][...] if before else jnp.zeros_like(total_ref)

    def add(fold, _):
        at = pl.ds(pl.multiple_of(fold * width, 128), width)
        right = unfold_load(rows, pl.program_id(0) * FOLDS + fold, chips * tokens)
        left = jnp.concatenate([mine_ref[:, at], theirs_ref[:, at]])
        total_ref[...] += lax.dot_general(left, right, (((1,), (1,)), ((), ())), preferred_element_type=jnp.float32)

    repeat(FOLDS, add, None, steps > SUBLANES)


def rotate_in(tokens, chunk, me, own, across, z, y, mine, theirs, before):
    height, width = own.shape
    chips = (z.shape[0] + 1) * PAIR
    basis = pl.BlockSpec((mine.shape[0], FOLDS * width), lambda i: (0, chunk * (SUBLANES // FOLDS) + i))
    return pl.pallas_call(
        functools.partial(rotate_in_kernel, tokens, len(before)),
        grid=(SUBLANES // FOLDS,),
        out_shape=jax.ShapeDtypeStruct((2 * mine.shape[0], chips * tokens), jnp.float32),
        in_specs=[SMEM] + [VMEM] * 4 + [basis] * 2 + [VMEM] * len(before),
        out_specs=VMEM,
        scratch_shapes=[pltpu.VMEM((width // 128, chips * height, 128), jnp.float32)],
        compiler_params=pltpu.CompilerParams(vmem_limit_bytes=24 * 2**20),
        cost_estimate=pl.CostEstimate(
            flops=4 * chips * tokens * mine.shape[0] * SUBLANES * width,
            bytes_accessed=4 * mine.shape[0] * SUBLANES * width,
            transcendentals=0,
        ),
        name="rotate_in",
    )(me, own, across, z, y, mine, theirs, *before)


def pile_kernel(blocks, *refs):
    for step in range(blocks):
        refs[-1][step] = refs[step][...]


def pile(blocks, waits):
    return pl.pallas_call(
        functools.partial(pile_kernel, len(blocks)),
        out_shape=jax.ShapeDtypeStruct((len(blocks), *blocks[0].shape), blocks[0].dtype),
        in_specs=[VMEM] * len(blocks) + [ANY] * len(waits),
        out_specs=VMEM,
        compiler_params=pltpu.CompilerParams(vmem_limit_bytes=24 * 2**20),
        cost_estimate=pl.CostEstimate(flops=0, bytes_accessed=2 * len(blocks) * blocks[0].size, transcendentals=0),
        name="pile",
    )(*blocks, *waits)


def fetch_kernel(from_ref, *refs):
    to_ref, done = refs[-2:]
    copy = pltpu.make_async_copy(from_ref, to_ref, done)
    copy.start()
    copy.wait()


def fetch(array, waits):
    return pl.pallas_call(
        fetch_kernel,
        out_shape=jax.ShapeDtypeStruct(array.shape, array.dtype),
        in_specs=[ANY] * (1 + len(waits)),
        out_specs=VMEM,
        scratch_shapes=[pltpu.SemaphoreType.DMA],
        compiler_params=pltpu.CompilerParams(vmem_limit_bytes=16 * 2**20),
        cost_estimate=pl.CostEstimate(flops=0, bytes_accessed=2 * array.size, transcendentals=0),
        name="fetch",
    )(array, *waits)


def after(arrays, waits):
    return pl.pallas_call(
        lambda *refs: None,
        out_shape=[jax.ShapeDtypeStruct(array.shape, array.dtype) for array in arrays],
        in_specs=[ANY] * (len(arrays) + len(waits)),
        out_specs=[ANY] * len(arrays),
        input_output_aliases={i: i for i in range(len(arrays))},
        compiler_params=pltpu.CompilerParams(vmem_limit_bytes=2**20),
        cost_estimate=pl.CostEstimate(flops=0, bytes_accessed=0, transcendentals=0),
        name="after",
    )(*arrays, *waits)


def combine_kernel(me_ref, own_ref, other_ref, z_ref, y_ref, cz_ref, cy_ref, out_ref):
    steps, total_tokens, width = z_ref.shape
    devices = steps * CORES * PAIR
    me = me_ref[0]
    own, other = own_ref[...].astype(jnp.float32), other_ref[...].astype(jnp.float32)
    first = lax.rem(me, CORES) == 0
    left = jnp.concatenate([jnp.where(first, own, other), jnp.where(first, other, own)], 1).astype(jnp.bfloat16)
    for ref, chip_bit, core_bit in ((z_ref, 0, 0), (y_ref, 1, 0), (cz_ref, 0, 1), (cy_ref, 1, 1)):

        def put(step, _, ref=ref, chip_bit=chip_bit, core_bit=core_bit):
            chip, core = origin(me, devices, step, chip_bit, core_bit)
            at = pl.multiple_of((chip * CORES + core) * width, 128)
            total = jnp.dot(left, ref[step], preferred_element_type=jnp.float32)
            out_ref[:, pl.ds(at, width)] = (total / total_tokens).astype(out_ref.dtype)

        repeat(steps, put)


def combine(me, own, other, z, y, cz, cy):
    steps, total_tokens, width = z.shape
    features = steps * CORES * PAIR * width
    return pl.pallas_call(
        combine_kernel,
        out_shape=jax.ShapeDtypeStruct((own.shape[0], features), jnp.bfloat16),
        in_specs=[SMEM] + [VMEM] * 6,
        out_specs=VMEM,
        compiler_params=pltpu.CompilerParams(vmem_limit_bytes=24 * 2**20),
        cost_estimate=pl.CostEstimate(
            flops=2 * own.shape[0] * total_tokens * features, bytes_accessed=4 * own.shape[0] * features, transcendentals=0
        ),
        name="combine",
    )(me, own, other, z, y, cz, cy)


def local(acts, grads, basis_in, basis_out):
    devices = lax.axis_size("wide")
    steps = devices // (CORES * PAIR)
    tokens = acts.shape[0]
    me = lax.axis_index("wide").astype(jnp.int32).reshape(1)

    def along_all(block):
        return [send(block, along(devices, step)) for step in range(1, steps)]

    def others(z):
        y = send(z, across(devices))
        return z, y, send(z, swap(devices)), send(y, swap(devices))

    mine = basis_in.T
    theirs = send(mine, swap(devices))
    width = acts.shape[1] // (CHUNKS * SUBLANES)
    folded = acts.reshape(tokens, CHUNKS, SUBLANES, width).transpose(1, 0, 2, 3).reshape(CHUNKS, -1, width)
    folded_across = send(folded, across(devices))
    block = grads.reshape(tokens * SUBLANES, -1)
    basis_out = fetch(basis_out, [block])
    grads_z = others(pile([block] + along_all(block), [folded_across, basis_out]))

    acts_z = [pile(along_all(folded[0]), [])]
    acts_y = [send(acts_z[0], across(devices))]
    sq_out = rotate_out(tokens, me, *grads_z, basis_out, [acts_z[0]])
    came = along_all(sq_out)
    acts_z.append(pile(along_all(folded[1]), [sq_out]))
    acts_y.append(send(acts_z[1], across(devices)))

    def part(chunk, before):
        return rotate_in(
            tokens, chunk, me, folded[chunk], folded_across[chunk], acts_z[chunk], acts_y[chunk], mine, theirs, before
        )

    total = part(0, [])
    z = pile([sq_out] + came, [total, acts_z[-1]])
    for chunk in range(1, CHUNKS):
        total = part(chunk, [total])
    squares = (total * total).astype(jnp.bfloat16)
    own, given = squares[: mine.shape[0]], squares[mine.shape[0] :]
    other = send(given, swap(devices))
    return combine(me, own, other, *others(z))


def solution(mesh):
    return jax.shard_map(
        local,
        mesh=mesh,
        in_specs=(
            P(("groups", "wide"), None),
            P(("groups", "wide"), None),
            P("groups", "wide"),
            P("groups", "wide"),
        ),
        out_specs=P(("groups", "wide"), None),
        check_vma=False,
    )
```

```python
import functools

import jax
import jax.numpy as jnp
from jax import lax
from jax.experimental import pallas as pl
from jax.experimental.pallas import tpu as pltpu
from jax.sharding import PartitionSpec as P

CORES = 2
PAIR = 2
SUBLANES = 8
FOLDS = 2
CHUNKS = 2
VMEM = pl.BlockSpec(memory_space=pltpu.VMEM)
ANY = pl.BlockSpec(memory_space=pl.ANY)
SMEM = pl.BlockSpec(memory_space=pltpu.SMEM)


def along(devices, by):
    each = CORES * PAIR
    return [(d, (d + by * each) % devices) for d in range(devices)]


def across(devices):
    return [(d, d ^ CORES) for d in range(devices)]


def swap(devices):
    return [(d, d ^ 1) for d in range(devices)]


def send(block, pairs):
    return lax.ppermute(block, "wide", pairs)


def origin(me, devices, step, other_chip, other_core):
    each = CORES * PAIR
    pair = lax.rem(me // each + devices // each - step, devices // each)
    chip = lax.rem(me // CORES, PAIR)
    core = lax.rem(me, CORES)
    if other_chip:
        chip = 1 - chip
    if other_core:
        core = 1 - core
    return pair * PAIR + chip, core


def room(mib, blocks):
    return mib * 2**20 if blocks <= SUBLANES else 24 * 2**20


def repeat(times, body, carry=None, loop=False):
    if loop or times > SUBLANES:
        return lax.fori_loop(0, times, body, carry)
    for step in range(times):
        carry = body(step, carry)
    return carry


def unfold_store(rows, slot, block):
    height = block.shape[0]
    at = pl.ds(pl.multiple_of(slot * height, SUBLANES), height)
    for tile in range(rows.shape[0]):
        rows[tile, at, :] = block[:, tile * 128 : (tile + 1) * 128].astype(jnp.float32)


def unfold_load(rows, fold, tokens):
    tiles = [rows[tile, pl.ds(fold, tokens, stride=SUBLANES), :] for tile in range(rows.shape[0])]
    return jnp.concatenate([tile.astype(jnp.bfloat16) for tile in tiles], 1)


def rotate_out_kernel(tokens, waits, me_ref, z_ref, y_ref, cz_ref, cy_ref, basis_ref, *refs):
    sq_ref, rows, total = refs[waits:]
    steps, height, width = z_ref.shape
    devices = steps * CORES * PAIR
    me = me_ref[0]

    @pl.when(pl.program_id(0) == 0)
    def _():
        for ref, chip_bit, core_bit in ((z_ref, 0, 0), (y_ref, 1, 0), (cz_ref, 0, 1), (cy_ref, 1, 1)):

            def put(step, _, ref=ref, chip_bit=chip_bit, core_bit=core_bit):
                chip, core = origin(me, devices, step, chip_bit, core_bit)
                unfold_store(rows, core * (devices // CORES) + chip, ref[step])

            repeat(steps, put)
        total[...] = jnp.zeros_like(total)

    def add(fold, _):
        left = unfold_load(rows, pl.program_id(0) * FOLDS + fold, devices * tokens)
        right = basis_ref[pl.ds(pl.multiple_of(fold * width, 128), width), :]
        total[...] += jnp.dot(left, right, preferred_element_type=jnp.float32)

    repeat(FOLDS, add, None, steps > SUBLANES)

    @pl.when(pl.program_id(0) == pl.num_programs(0) - 1)
    def _():
        sq_ref[...] = (total[...] * total[...]).astype(sq_ref.dtype)


def rotate_out(tokens, me, z, y, cz, cy, basis, waits):
    steps, height, width = z.shape
    total = steps * CORES * PAIR * tokens
    columns = basis.shape[1]
    return pl.pallas_call(
        functools.partial(rotate_out_kernel, tokens, len(waits)),
        grid=(SUBLANES // FOLDS,),
        out_shape=jax.ShapeDtypeStruct((total, columns), jnp.bfloat16),
        in_specs=[SMEM] + [VMEM] * 4 + [pl.BlockSpec((FOLDS * width, columns), lambda i: (i, 0))] + [ANY] * len(waits),
        out_specs=VMEM,
        scratch_shapes=[
            pltpu.VMEM((width // 128, total * SUBLANES, 128), jnp.float32),
            pltpu.VMEM((total, columns), jnp.float32),
        ],
        compiler_params=pltpu.CompilerParams(vmem_limit_bytes=room(10, steps)),
        cost_estimate=pl.CostEstimate(
            flops=2 * total * basis.shape[0] * columns, bytes_accessed=2 * basis.size, transcendentals=0
        ),
        name="rotate_out",
    )(me, z, y, cz, cy, basis, *waits)


def rotate_in_kernel(tokens, before, me_ref, own_ref, across_ref, z_ref, y_ref, mine_ref, theirs_ref, *refs):
    total_ref, rows = refs[before:]
    height, width = own_ref.shape
    steps = z_ref.shape[0] + 1
    devices = steps * CORES * PAIR
    chips = devices // CORES
    me = me_ref[0]

    @pl.when(pl.program_id(0) == 0)
    def _():
        unfold_store(rows, origin(me, devices, 0, 0, 0)[0], own_ref[...])
        unfold_store(rows, origin(me, devices, 0, 1, 0)[0], across_ref[...])
        for ref, chip_bit in ((z_ref, 0), (y_ref, 1)):

            def put(step, _, ref=ref, chip_bit=chip_bit):
                unfold_store(rows, origin(me, devices, step + 1, chip_bit, 0)[0], ref[step])

            repeat(steps - 1, put)
        total_ref[...] = refs[0][...] if before else jnp.zeros_like(total_ref)

    def add(fold, _):
        at = pl.ds(pl.multiple_of(fold * width, 128), width)
        right = unfold_load(rows, pl.program_id(0) * FOLDS + fold, chips * tokens)
        left = jnp.concatenate([mine_ref[:, at], theirs_ref[:, at]])
        total_ref[...] += lax.dot_general(left, right, (((1,), (1,)), ((), ())), preferred_element_type=jnp.float32)

    repeat(FOLDS, add, None, steps > SUBLANES)


def rotate_in(tokens, chunk, me, own, across, z, y, mine, theirs, before):
    height, width = own.shape
    chips = (z.shape[0] + 1) * PAIR
    basis = pl.BlockSpec((mine.shape[0], FOLDS * width), lambda i: (0, chunk * (SUBLANES // FOLDS) + i))
    return pl.pallas_call(
        functools.partial(rotate_in_kernel, tokens, len(before)),
        grid=(SUBLANES // FOLDS,),
        out_shape=jax.ShapeDtypeStruct((2 * mine.shape[0], chips * tokens), jnp.float32),
        in_specs=[SMEM] + [VMEM] * 4 + [basis] * 2 + [VMEM] * len(before),
        out_specs=VMEM,
        scratch_shapes=[pltpu.VMEM((width // 128, chips * height, 128), jnp.float32)],
        compiler_params=pltpu.CompilerParams(vmem_limit_bytes=room(9, chips)),
        cost_estimate=pl.CostEstimate(
            flops=4 * chips * tokens * mine.shape[0] * SUBLANES * width,
            bytes_accessed=4 * mine.shape[0] * SUBLANES * width,
            transcendentals=0,
        ),
        name="rotate_in",
    )(me, own, across, z, y, mine, theirs, *before)


def pile_kernel(blocks, *refs):
    for step in range(blocks):
        refs[-1][step] = refs[step][...]


def pile(blocks, waits):
    return pl.pallas_call(
        functools.partial(pile_kernel, len(blocks)),
        out_shape=jax.ShapeDtypeStruct((len(blocks), *blocks[0].shape), blocks[0].dtype),
        in_specs=[VMEM] * len(blocks) + [ANY] * len(waits),
        out_specs=VMEM,
        compiler_params=pltpu.CompilerParams(vmem_limit_bytes=room(3, len(blocks))),
        cost_estimate=pl.CostEstimate(flops=0, bytes_accessed=2 * len(blocks) * blocks[0].size, transcendentals=0),
        name="pile",
    )(*blocks, *waits)


def fetch_kernel(from_ref, *refs):
    to_ref, done = refs[-2:]
    copy = pltpu.make_async_copy(from_ref, to_ref, done)
    copy.start()
    copy.wait()


def fetch(array, waits):
    return pl.pallas_call(
        fetch_kernel,
        out_shape=jax.ShapeDtypeStruct(array.shape, array.dtype),
        in_specs=[pl.BlockSpec(memory_space=pltpu.HBM)] + [ANY] * len(waits),
        out_specs=VMEM,
        scratch_shapes=[pltpu.SemaphoreType.DMA],
        compiler_params=pltpu.CompilerParams(vmem_limit_bytes=2 * 2**20),
        cost_estimate=pl.CostEstimate(flops=0, bytes_accessed=2 * array.size, transcendentals=0),
        name="fetch",
    )(array, *waits)


def combine_kernel(me_ref, own_ref, other_ref, z_ref, y_ref, cz_ref, cy_ref, out_ref):
    steps, total_tokens, width = z_ref.shape
    devices = steps * CORES * PAIR
    me = me_ref[0]
    own, other = own_ref[...].astype(jnp.float32), other_ref[...].astype(jnp.float32)
    first = lax.rem(me, CORES) == 0
    left = jnp.concatenate([jnp.where(first, own, other), jnp.where(first, other, own)], 1).astype(jnp.bfloat16)
    for ref, chip_bit, core_bit in ((z_ref, 0, 0), (y_ref, 1, 0), (cz_ref, 0, 1), (cy_ref, 1, 1)):

        def put(step, _, ref=ref, chip_bit=chip_bit, core_bit=core_bit):
            chip, core = origin(me, devices, step, chip_bit, core_bit)
            at = pl.multiple_of((chip * CORES + core) * width, 128)
            total = jnp.dot(left, ref[step], preferred_element_type=jnp.float32)
            out_ref[:, pl.ds(at, width)] = (total / total_tokens).astype(out_ref.dtype)

        repeat(steps, put)


def combine(me, own, other, z, y, cz, cy):
    steps, total_tokens, width = z.shape
    features = steps * CORES * PAIR * width
    return pl.pallas_call(
        combine_kernel,
        out_shape=jax.ShapeDtypeStruct((own.shape[0], features), jnp.bfloat16),
        in_specs=[SMEM] + [VMEM] * 6,
        out_specs=VMEM,
        compiler_params=pltpu.CompilerParams(vmem_limit_bytes=room(6, steps)),
        cost_estimate=pl.CostEstimate(
            flops=2 * own.shape[0] * total_tokens * features, bytes_accessed=4 * own.shape[0] * features, transcendentals=0
        ),
        name="combine",
    )(me, own, other, z, y, cz, cy)


def local(acts, grads, basis_in, basis_out):
    devices = lax.axis_size("wide")
    steps = devices // (CORES * PAIR)
    tokens = acts.shape[0]
    me = lax.axis_index("wide").astype(jnp.int32).reshape(1)

    def along_all(block):
        return [send(block, along(devices, step)) for step in range(1, steps)]

    def others(z):
        y = send(z, across(devices))
        return z, y, send(z, swap(devices)), send(y, swap(devices))

    mine = basis_in.T
    theirs = send(mine, swap(devices))
    width = acts.shape[1] // (CHUNKS * SUBLANES)
    folded = acts.reshape(tokens, CHUNKS, SUBLANES, width).transpose(1, 0, 2, 3).reshape(CHUNKS, -1, width)
    folded_across = send(folded, across(devices))
    block = grads.reshape(tokens * SUBLANES, -1)
    basis_out = fetch(basis_out, [block])
    grads_z = others(pile([block] + along_all(block), [folded_across, basis_out]))

    acts_z = [pile(along_all(folded[0]), [])]
    acts_y = [send(acts_z[0], across(devices))]
    sq_out = rotate_out(tokens, me, *grads_z, basis_out, [acts_z[0]])
    came = along_all(sq_out)
    acts_z.append(pile(along_all(folded[1]), [sq_out]))
    acts_y.append(send(acts_z[1], across(devices)))

    def part(chunk, before):
        return rotate_in(
            tokens, chunk, me, folded[chunk], folded_across[chunk], acts_z[chunk], acts_y[chunk], mine, theirs, before
        )

    total = part(0, [])
    z = pile([sq_out] + came, [total, acts_z[-1]])
    for chunk in range(1, CHUNKS):
        total = part(chunk, [total])
    squares = (total * total).astype(jnp.bfloat16)
    own, given = squares[: mine.shape[0]], squares[mine.shape[0] :]
    other = send(given, swap(devices))
    return combine(me, own, other, *others(z))


def solution(mesh):
    return jax.shard_map(
        local,
        mesh=mesh,
        in_specs=(
            P(("groups", "wide"), None),
            P(("groups", "wide"), None),
            P("groups", "wide"),
            P("groups", "wide"),
        ),
        out_specs=P(("groups", "wide"), None),
        check_vma=False,
    )
```

```python
import functools

import jax
import jax.numpy as jnp
from jax import lax
from jax.experimental import pallas as pl
from jax.experimental.pallas import tpu as pltpu
from jax.sharding import PartitionSpec as P

CORES = 2
PAIR = 2
SUBLANES = 8
FOLDS = 2
CHUNKS = 2
VMEM = pl.BlockSpec(memory_space=pltpu.VMEM)
ANY = pl.BlockSpec(memory_space=pl.ANY)


def along(devices, by):
    each = CORES * PAIR
    return [(d, (d + by * each) % devices) for d in range(devices)]


def across(devices):
    return [(d, d ^ CORES) for d in range(devices)]


def swap(devices):
    return [(d, d ^ 1) for d in range(devices)]


def send(block, pairs):
    return lax.ppermute(block, "wide", pairs)


def origin(me, devices, step, other_chip, other_core):
    each = CORES * PAIR
    pair = lax.rem(me // each + devices // each - step, devices // each)
    chip = lax.rem(me // CORES, PAIR)
    core = lax.rem(me, CORES)
    if other_chip:
        chip = 1 - chip
    if other_core:
        core = 1 - core
    return pair * PAIR + chip, core


def room(mib, blocks):
    return mib * 2**20 if blocks <= SUBLANES else 24 * 2**20


def repeat(times, body, carry=None, loop=False):
    if loop or times > SUBLANES:
        return lax.fori_loop(0, times, body, carry)
    for step in range(times):
        carry = body(step, carry)
    return carry


def unfold_store(rows, slot, block):
    height = block.shape[0]
    at = pl.ds(pl.multiple_of(slot * height, SUBLANES), height)
    for tile in range(rows.shape[0]):
        rows[tile, at, :] = block[:, tile * 128 : (tile + 1) * 128].astype(jnp.float32)


def unfold_load(rows, fold, tokens):
    tiles = [rows[tile, pl.ds(fold, tokens, stride=SUBLANES), :] for tile in range(rows.shape[0])]
    return jnp.concatenate([tile.astype(jnp.bfloat16) for tile in tiles], 1)


def rotate_out_kernel(tokens, waits, z_ref, y_ref, cz_ref, cy_ref, basis_ref, *refs):
    sq_ref, rows, total = refs[waits:]
    steps, height, width = z_ref.shape
    devices = steps * CORES * PAIR
    me = lax.axis_index("wide")

    @pl.when(pl.program_id(0) == 0)
    def _():
        for ref, chip_bit, core_bit in ((z_ref, 0, 0), (y_ref, 1, 0), (cz_ref, 0, 1), (cy_ref, 1, 1)):

            def put(step, _, ref=ref, chip_bit=chip_bit, core_bit=core_bit):
                chip, core = origin(me, devices, step, chip_bit, core_bit)
                unfold_store(rows, core * (devices // CORES) + chip, ref[step])

            repeat(steps, put)
        total[...] = jnp.zeros_like(total)

    def add(fold, _):
        left = unfold_load(rows, pl.program_id(0) * FOLDS + fold, devices * tokens)
        right = basis_ref[pl.ds(pl.multiple_of(fold * width, 128), width), :]
        total[...] += jnp.dot(left, right, preferred_element_type=jnp.float32)

    repeat(FOLDS, add, None, steps > SUBLANES)

    @pl.when(pl.program_id(0) == pl.num_programs(0) - 1)
    def _():
        sq_ref[...] = (total[...] * total[...]).astype(sq_ref.dtype)


def rotate_out(tokens, z, y, cz, cy, basis, waits):
    steps, height, width = z.shape
    total = steps * CORES * PAIR * tokens
    columns = basis.shape[1]
    return pl.pallas_call(
        functools.partial(rotate_out_kernel, tokens, len(waits)),
        grid=(SUBLANES // FOLDS,),
        out_shape=jax.ShapeDtypeStruct((total, columns), jnp.bfloat16),
        in_specs=[VMEM] * 4 + [pl.BlockSpec((FOLDS * width, columns), lambda i: (i, 0))] + [ANY] * len(waits),
        out_specs=VMEM,
        scratch_shapes=[
            pltpu.VMEM((width // 128, total * SUBLANES, 128), jnp.float32),
            pltpu.VMEM((total, columns), jnp.float32),
        ],
        compiler_params=pltpu.CompilerParams(vmem_limit_bytes=room(10, steps)),
        cost_estimate=pl.CostEstimate(
            flops=2 * total * basis.shape[0] * columns, bytes_accessed=2 * basis.size, transcendentals=0
        ),
        name="rotate_out",
    )(z, y, cz, cy, basis, *waits)


def rotate_in_kernel(tokens, chunk, before, last, own_ref, across_ref, z_ref, y_ref, mine_ref, theirs_ref, *refs):
    outs, (total, rows) = refs[before:-2], refs[-2:]
    height, width = own_ref.shape
    steps = z_ref.shape[0] + 1
    devices = steps * CORES * PAIR
    chips = devices // CORES
    me = lax.axis_index("wide")

    def put(chip, block):
        unfold_store(rows, chip, block)

    @pl.when(pl.program_id(0) == 0)
    def _():
        put(origin(me, devices, 0, 0, 0)[0], own_ref[...])
        put(origin(me, devices, 0, 1, 0)[0], across_ref[chunk])
        for ref, chip_bit in ((z_ref, 0), (y_ref, 1)):

            def put_far(step, _, ref=ref, chip_bit=chip_bit):
                put(origin(me, devices, step + 1, chip_bit, 0)[0], ref[step])

            repeat(steps - 1, put_far)
        total[...] = refs[0][...] if before else jnp.zeros_like(total)

    def add(fold, _):
        at = pl.ds(pl.multiple_of(fold * width, 128), width)
        right = unfold_load(rows, pl.program_id(0) * FOLDS + fold, chips * tokens)
        left = jnp.concatenate([mine_ref[:, at], theirs_ref[:, at]])
        total[...] += lax.dot_general(left, right, (((1,), (1,)), ((), ())), preferred_element_type=jnp.float32)

    repeat(FOLDS, add, None, steps > SUBLANES)

    @pl.when(pl.program_id(0) == pl.num_programs(0) - 1)
    def _():
        if last:
            squares = (total[...] * total[...]).astype(jnp.bfloat16)
            outs[0][...] = squares[: outs[0].shape[0]]
            outs[1][...] = squares[outs[0].shape[0] :]
        else:
            outs[0][...] = total[...]


def rotate_in(tokens, chunk, own, across, z, y, mine, theirs, before):
    height, width = own.shape
    chips = (z.shape[0] + 1) * PAIR
    last = chunk == CHUNKS - 1
    basis = pl.BlockSpec((mine.shape[0], FOLDS * width), lambda i: (0, chunk * (SUBLANES // FOLDS) + i))
    whole = jax.ShapeDtypeStruct((2 * mine.shape[0], chips * tokens), jnp.float32)
    half = jax.ShapeDtypeStruct((mine.shape[0], chips * tokens), jnp.bfloat16)
    return pl.pallas_call(
        functools.partial(rotate_in_kernel, tokens, chunk, len(before), last),
        grid=(SUBLANES // FOLDS,),
        out_shape=(half, half) if last else (whole,),
        in_specs=[VMEM] * 4 + [basis] * 2 + [VMEM] * len(before),
        out_specs=(VMEM, VMEM) if last else (VMEM,),
        scratch_shapes=[
            pltpu.VMEM(whole.shape, jnp.float32),
            pltpu.VMEM((width // 128, chips * height, 128), jnp.float32),
        ],
        compiler_params=pltpu.CompilerParams(vmem_limit_bytes=room(9, chips)),
        cost_estimate=pl.CostEstimate(
            flops=4 * chips * tokens * mine.shape[0] * SUBLANES * width,
            bytes_accessed=4 * mine.shape[0] * SUBLANES * width,
            transcendentals=0,
        ),
        name="rotate_in",
    )(own, across, z, y, mine, theirs, *before)


def fold_kernel(waits, from_ref, *refs):
    outs, rows = refs[waits:-1], refs[-1]
    tokens = from_ref.shape[0]
    chunks = max(1, len(outs) - 1)
    tiles = from_ref.shape[1] // (chunks * SUBLANES * 128)
    for chunk in range(chunks):
        for tile in range(tiles):
            for fold in range(SUBLANES):
                at = ((chunk * SUBLANES + fold) * tiles + tile) * 128
                rows[tile, pl.ds(fold, tokens, stride=SUBLANES), :] = from_ref[:, at : at + 128].astype(jnp.float32)
        for tile in range(tiles):
            block = rows[tile].astype(jnp.bfloat16)
            outs[chunk][:, tile * 128 : (tile + 1) * 128] = block
            if chunks > 1:
                outs[-1][chunk, :, tile * 128 : (tile + 1) * 128] = block


def folded(array, chunks, waits):
    shape = (array.shape[0] * SUBLANES, array.shape[1] // (chunks * SUBLANES))
    outs = [jax.ShapeDtypeStruct(shape, array.dtype)] * chunks
    if chunks > 1:
        outs.append(jax.ShapeDtypeStruct((chunks, *shape), array.dtype))
    return pl.pallas_call(
        functools.partial(fold_kernel, len(waits)),
        out_shape=outs,
        in_specs=[VMEM] + [ANY] * len(waits),
        out_specs=[VMEM] * len(outs),
        scratch_shapes=[pltpu.VMEM((shape[1] // 128, shape[0], 128), jnp.float32)],
        compiler_params=pltpu.CompilerParams(vmem_limit_bytes=4 * 2**20),
        cost_estimate=pl.CostEstimate(flops=0, bytes_accessed=4 * array.size, transcendentals=0),
        name="fold",
    )(array, *waits)


def pile_kernel(blocks, *refs):
    for step in range(blocks):
        refs[-1][step] = refs[step][...]


def pile(blocks, waits):
    return pl.pallas_call(
        functools.partial(pile_kernel, len(blocks)),
        out_shape=jax.ShapeDtypeStruct((len(blocks), *blocks[0].shape), blocks[0].dtype),
        in_specs=[VMEM] * len(blocks) + [ANY] * len(waits),
        out_specs=VMEM,
        compiler_params=pltpu.CompilerParams(vmem_limit_bytes=room(3, len(blocks))),
        cost_estimate=pl.CostEstimate(flops=0, bytes_accessed=2 * len(blocks) * blocks[0].size, transcendentals=0),
        name="pile",
    )(*blocks, *waits)


def after(arrays, waits):
    return pl.pallas_call(
        lambda *refs: None,
        out_shape=[jax.ShapeDtypeStruct(array.shape, array.dtype) for array in arrays],
        in_specs=[ANY] * (len(arrays) + len(waits)),
        out_specs=[ANY] * len(arrays),
        input_output_aliases={i: i for i in range(len(arrays))},
        compiler_params=pltpu.CompilerParams(vmem_limit_bytes=2**20),
        cost_estimate=pl.CostEstimate(flops=0, bytes_accessed=0, transcendentals=0),
        name="after",
    )(*arrays, *waits)


def combine_kernel(own_ref, other_ref, z_ref, y_ref, cz_ref, cy_ref, out_ref):
    steps, total_tokens, width = z_ref.shape
    devices = steps * CORES * PAIR
    me = lax.axis_index("wide")
    own, other = own_ref[...].astype(jnp.float32), other_ref[...].astype(jnp.float32)
    first = lax.rem(me, CORES) == 0
    left = jnp.concatenate([jnp.where(first, own, other), jnp.where(first, other, own)], 1).astype(jnp.bfloat16)
    for ref, chip_bit, core_bit in ((z_ref, 0, 0), (y_ref, 1, 0), (cz_ref, 0, 1), (cy_ref, 1, 1)):

        def put(step, _, ref=ref, chip_bit=chip_bit, core_bit=core_bit):
            chip, core = origin(me, devices, step, chip_bit, core_bit)
            at = pl.multiple_of((chip * CORES + core) * width, 128)
            total = jnp.dot(left, ref[step], preferred_element_type=jnp.float32)
            out_ref[:, pl.ds(at, width)] = (total / total_tokens).astype(out_ref.dtype)

        repeat(steps, put)


def combine(own, other, z, y, cz, cy):
    steps, total_tokens, width = z.shape
    features = steps * CORES * PAIR * width
    return pl.pallas_call(
        combine_kernel,
        out_shape=jax.ShapeDtypeStruct((own.shape[0], features), jnp.bfloat16),
        in_specs=[VMEM] * 6,
        out_specs=VMEM,
        compiler_params=pltpu.CompilerParams(vmem_limit_bytes=room(6, steps)),
        cost_estimate=pl.CostEstimate(
            flops=2 * own.shape[0] * total_tokens * features, bytes_accessed=4 * own.shape[0] * features, transcendentals=0
        ),
        name="combine",
    )(own, other, z, y, cz, cy)


def local(acts, grads, basis_in, basis_out):
    devices = lax.axis_size("wide")
    steps = devices // (CORES * PAIR)
    tokens = acts.shape[0]

    def along_all(block):
        return [send(block, along(devices, step)) for step in range(1, steps)]

    def others(z):
        y = send(z, across(devices))
        return z, y, send(z, swap(devices)), send(y, swap(devices))

    [block] = folded(grads, 1, [])
    mine = basis_in.T
    theirs = send(mine, swap(devices))
    *own, every = folded(acts, CHUNKS, [block])
    own_across = send(every, across(devices))
    grads_all = others(pile([block] + along_all(block), [own_across]))

    acts_z, acts_y = [], []

    def chunk_along(chunk, waits):
        acts_z.append(pile(along_all(own[chunk]), waits))
        acts_y.append(send(acts_z[-1], across(devices)))

    def part(chunk, before):
        return rotate_in(tokens, chunk, own[chunk], own_across, acts_z[chunk], acts_y[chunk], mine, theirs, before)

    chunk_along(0, [])
    sq_out = rotate_out(tokens, *grads_all, basis_out, [acts_z[0]])
    came = along_all(sq_out)
    for chunk in range(1, CHUNKS):
        chunk_along(chunk, [sq_out])
    total = part(0, [])
    z = pile([sq_out] + came, [*total, acts_z[-1]])
    y = send(z, across(devices))
    for chunk in range(1, CHUNKS):
        total = part(chunk, total)
    sq_in, given = total
    [y] = after([y], [sq_in])
    return combine(sq_in, send(given, swap(devices)), z, y, send(z, swap(devices)), send(y, swap(devices)))


def solution(mesh):
    return jax.shard_map(
        local,
        mesh=mesh,
        in_specs=(
            P(("groups", "wide"), None),
            P(("groups", "wide"), None),
            P("groups", "wide"),
            P("groups", "wide"),
        ),
        out_specs=P(("groups", "wide"), None),
        check_vma=False,
    )
```

```python
import functools

import jax
import jax.numpy as jnp
from jax import lax
from jax.experimental import pallas as pl
from jax.experimental.pallas import tpu as pltpu
from jax.sharding import PartitionSpec as P

CORES = 2
PAIR = 2
SUBLANES = 8
FOLDS = 2
CHUNKS = 2
VMEM = pl.BlockSpec(memory_space=pltpu.VMEM)
ANY = pl.BlockSpec(memory_space=pl.ANY)


def along(devices, by):
    each = CORES * PAIR
    return [(d, (d + by * each) % devices) for d in range(devices)]


def across(devices):
    return [(d, d ^ CORES) for d in range(devices)]


def swap(devices):
    return [(d, d ^ 1) for d in range(devices)]


def send(block, pairs):
    return lax.ppermute(block, "wide", pairs)


def origin(me, devices, step, other_chip, other_core):
    each = CORES * PAIR
    pair = lax.rem(me // each + devices // each - step, devices // each)
    chip = lax.rem(me // CORES, PAIR)
    core = lax.rem(me, CORES)
    if other_chip:
        chip = 1 - chip
    if other_core:
        core = 1 - core
    return pair * PAIR + chip, core


def room(mib, blocks):
    return mib * 2**20 if blocks <= SUBLANES else 24 * 2**20


def repeat(times, body, carry=None, loop=False):
    if loop or times > SUBLANES:
        return lax.fori_loop(0, times, body, carry)
    for step in range(times):
        carry = body(step, carry)
    return carry


def unfold_store(rows, slot, block):
    height = block.shape[0]
    at = pl.ds(pl.multiple_of(slot * height, SUBLANES), height)
    for tile in range(rows.shape[0]):
        rows[tile, at, :] = block[:, tile * 128 : (tile + 1) * 128].astype(jnp.float32)


def unfold_load(rows, fold, tokens):
    tiles = [rows[tile, pl.ds(fold, tokens, stride=SUBLANES), :] for tile in range(rows.shape[0])]
    return jnp.concatenate([tile.astype(jnp.bfloat16) for tile in tiles], 1)


def rotate_out_kernel(tokens, waits, z_ref, y_ref, cz_ref, cy_ref, basis_ref, *refs):
    sq_ref, rows, total = refs[waits:]
    steps, height, width = z_ref.shape
    devices = steps * CORES * PAIR
    me = lax.axis_index("wide")

    @pl.when(pl.program_id(0) == 0)
    def _():
        for ref, chip_bit, core_bit in ((z_ref, 0, 0), (y_ref, 1, 0), (cz_ref, 0, 1), (cy_ref, 1, 1)):

            def put(step, _, ref=ref, chip_bit=chip_bit, core_bit=core_bit):
                chip, core = origin(me, devices, step, chip_bit, core_bit)
                unfold_store(rows, core * (devices // CORES) + chip, ref[step])

            repeat(steps, put)
        total[...] = jnp.zeros_like(total)

    def add(fold, _):
        left = unfold_load(rows, pl.program_id(0) * FOLDS + fold, devices * tokens)
        right = basis_ref[pl.ds(pl.multiple_of(fold * width, 128), width), :]
        total[...] += jnp.dot(left, right, preferred_element_type=jnp.float32)

    repeat(FOLDS, add, None, steps > SUBLANES)

    @pl.when(pl.program_id(0) == pl.num_programs(0) - 1)
    def _():
        sq_ref[...] = (total[...] * total[...]).astype(sq_ref.dtype)


def rotate_out(tokens, z, y, cz, cy, basis, waits):
    steps, height, width = z.shape
    total = steps * CORES * PAIR * tokens
    columns = basis.shape[1]
    return pl.pallas_call(
        functools.partial(rotate_out_kernel, tokens, len(waits)),
        grid=(SUBLANES // FOLDS,),
        out_shape=jax.ShapeDtypeStruct((total, columns), jnp.bfloat16),
        in_specs=[VMEM] * 4 + [pl.BlockSpec((FOLDS * width, columns), lambda i: (i, 0))] + [ANY] * len(waits),
        out_specs=VMEM,
        scratch_shapes=[
            pltpu.VMEM((width // 128, total * SUBLANES, 128), jnp.float32),
            pltpu.VMEM((total, columns), jnp.float32),
        ],
        compiler_params=pltpu.CompilerParams(vmem_limit_bytes=room(10, steps)),
        cost_estimate=pl.CostEstimate(
            flops=2 * total * basis.shape[0] * columns, bytes_accessed=2 * basis.size, transcendentals=0
        ),
        name="rotate_out",
    )(z, y, cz, cy, basis, *waits)


def rotate_in_kernel(tokens, before, last, z_ref, y_ref, mine_ref, theirs_ref, *refs):
    outs, (total, rows) = refs[before:-2], refs[-2:]
    steps, height, width = z_ref.shape
    devices = steps * CORES * PAIR
    chips = devices // CORES
    me = lax.axis_index("wide")

    @pl.when(pl.program_id(0) == 0)
    def _():
        for ref, chip_bit in ((z_ref, 0), (y_ref, 1)):

            def put(step, _, ref=ref, chip_bit=chip_bit):
                unfold_store(rows, origin(me, devices, step, chip_bit, 0)[0], ref[step])

            repeat(steps, put)
        total[...] = refs[0][...] if before else jnp.zeros_like(total)

    def add(fold, _):
        at = pl.ds(pl.multiple_of(fold * width, 128), width)
        right = unfold_load(rows, pl.program_id(0) * FOLDS + fold, chips * tokens)
        left = jnp.concatenate([mine_ref[:, at], theirs_ref[:, at]])
        total[...] += lax.dot_general(left, right, (((1,), (1,)), ((), ())), preferred_element_type=jnp.float32)

    repeat(FOLDS, add, None, steps > SUBLANES)

    @pl.when(pl.program_id(0) == pl.num_programs(0) - 1)
    def _():
        if last:
            squares = (total[...] * total[...]).astype(jnp.bfloat16)
            outs[0][...] = squares[: outs[0].shape[0]]
            outs[1][...] = squares[outs[0].shape[0] :]
        else:
            outs[0][...] = total[...]


def rotate_in(tokens, chunk, z, y, mine, theirs, before):
    steps, height, width = z.shape
    chips = steps * PAIR
    last = chunk == CHUNKS - 1
    basis = pl.BlockSpec((mine.shape[0], FOLDS * width), lambda i: (0, chunk * (SUBLANES // FOLDS) + i))
    whole = jax.ShapeDtypeStruct((2 * mine.shape[0], chips * tokens), jnp.float32)
    half = jax.ShapeDtypeStruct((mine.shape[0], chips * tokens), jnp.bfloat16)
    return pl.pallas_call(
        functools.partial(rotate_in_kernel, tokens, len(before), last),
        grid=(SUBLANES // FOLDS,),
        out_shape=(half, half) if last else (whole,),
        in_specs=[VMEM] * 2 + [basis] * 2 + [VMEM] * len(before),
        out_specs=(VMEM, VMEM) if last else (VMEM,),
        scratch_shapes=[
            pltpu.VMEM(whole.shape, jnp.float32),
            pltpu.VMEM((width // 128, chips * height, 128), jnp.float32),
        ],
        compiler_params=pltpu.CompilerParams(vmem_limit_bytes=room(9, chips)),
        cost_estimate=pl.CostEstimate(
            flops=4 * chips * tokens * mine.shape[0] * SUBLANES * width,
            bytes_accessed=4 * mine.shape[0] * SUBLANES * width,
            transcendentals=0,
        ),
        name="rotate_in",
    )(z, y, mine, theirs, *before)


def fold_kernel(waits, from_ref, *refs):
    outs, rows = refs[waits:-1], refs[-1]
    tokens = from_ref.shape[0]
    tiles = rows.shape[0]
    for chunk, out_ref in enumerate(outs):
        for tile in range(tiles):
            for fold in range(SUBLANES):
                at = ((chunk * SUBLANES + fold) * tiles + tile) * 128
                rows[tile, pl.ds(fold, tokens, stride=SUBLANES), :] = from_ref[:, at : at + 128].astype(jnp.float32)
        for tile in range(tiles):
            out_ref[:, tile * 128 : (tile + 1) * 128] = rows[tile].astype(jnp.bfloat16)


def folded(array, chunks, waits):
    shape = (array.shape[0] * SUBLANES, array.shape[1] // (chunks * SUBLANES))
    return pl.pallas_call(
        functools.partial(fold_kernel, len(waits)),
        out_shape=[jax.ShapeDtypeStruct(shape, array.dtype)] * chunks,
        in_specs=[VMEM] + [ANY] * len(waits),
        out_specs=[VMEM] * chunks,
        scratch_shapes=[pltpu.VMEM((shape[1] // 128, shape[0], 128), jnp.float32)],
        compiler_params=pltpu.CompilerParams(vmem_limit_bytes=4 * 2**20),
        cost_estimate=pl.CostEstimate(flops=0, bytes_accessed=4 * array.size, transcendentals=0),
        name="fold",
    )(array, *waits)


def pile_kernel(blocks, *refs):
    for step in range(blocks):
        refs[-1][step] = refs[step][...]


def pile(blocks, waits):
    return pl.pallas_call(
        functools.partial(pile_kernel, len(blocks)),
        out_shape=jax.ShapeDtypeStruct((len(blocks), *blocks[0].shape), blocks[0].dtype),
        in_specs=[VMEM] * len(blocks) + [ANY] * len(waits),
        out_specs=VMEM,
        compiler_params=pltpu.CompilerParams(vmem_limit_bytes=room(3, len(blocks))),
        cost_estimate=pl.CostEstimate(flops=0, bytes_accessed=2 * len(blocks) * blocks[0].size, transcendentals=0),
        name="pile",
    )(*blocks, *waits)


def fetch_kernel(from_ref, *refs):
    to_ref, done = refs[-2:]
    copy = pltpu.make_async_copy(from_ref, to_ref, done)
    copy.start()
    copy.wait()


def fetch(array, waits):
    return pl.pallas_call(
        fetch_kernel,
        out_shape=jax.ShapeDtypeStruct(array.shape, array.dtype),
        in_specs=[ANY] * (1 + len(waits)),
        out_specs=VMEM,
        scratch_shapes=[pltpu.SemaphoreType.DMA],
        compiler_params=pltpu.CompilerParams(vmem_limit_bytes=2**20),
        cost_estimate=pl.CostEstimate(flops=0, bytes_accessed=2 * array.size, transcendentals=0),
        name="fetch",
    )(array, *waits)


def after(arrays, waits):
    return pl.pallas_call(
        lambda *refs: None,
        out_shape=[jax.ShapeDtypeStruct(array.shape, array.dtype) for array in arrays],
        in_specs=[ANY] * (len(arrays) + len(waits)),
        out_specs=[ANY] * len(arrays),
        input_output_aliases={i: i for i in range(len(arrays))},
        compiler_params=pltpu.CompilerParams(vmem_limit_bytes=2**20),
        cost_estimate=pl.CostEstimate(flops=0, bytes_accessed=0, transcendentals=0),
        name="after",
    )(*arrays, *waits)


def combine_kernel(own_ref, other_ref, z_ref, y_ref, cz_ref, cy_ref, out_ref):
    steps, total_tokens, width = z_ref.shape
    devices = steps * CORES * PAIR
    me = lax.axis_index("wide")
    own, other = own_ref[...].astype(jnp.float32), other_ref[...].astype(jnp.float32)
    first = lax.rem(me, CORES) == 0
    left = jnp.concatenate([jnp.where(first, own, other), jnp.where(first, other, own)], 1).astype(jnp.bfloat16)
    for ref, chip_bit, core_bit in ((z_ref, 0, 0), (y_ref, 1, 0), (cz_ref, 0, 1), (cy_ref, 1, 1)):

        def put(step, _, ref=ref, chip_bit=chip_bit, core_bit=core_bit):
            chip, core = origin(me, devices, step, chip_bit, core_bit)
            at = pl.multiple_of((chip * CORES + core) * width, 128)
            total = jnp.dot(left, ref[step], preferred_element_type=jnp.float32)
            out_ref[:, pl.ds(at, width)] = (total / total_tokens).astype(out_ref.dtype)

        repeat(steps, put)


def combine(own, other, z, y, cz, cy):
    steps, total_tokens, width = z.shape
    features = steps * CORES * PAIR * width
    return pl.pallas_call(
        combine_kernel,
        out_shape=jax.ShapeDtypeStruct((own.shape[0], features), jnp.bfloat16),
        in_specs=[VMEM] * 6,
        out_specs=VMEM,
        compiler_params=pltpu.CompilerParams(vmem_limit_bytes=room(6, steps)),
        cost_estimate=pl.CostEstimate(
            flops=2 * own.shape[0] * total_tokens * features, bytes_accessed=4 * own.shape[0] * features, transcendentals=0
        ),
        name="combine",
    )(own, other, z, y, cz, cy)


def local(acts, grads, basis_in, basis_out):
    devices = lax.axis_size("wide")
    steps = devices // (CORES * PAIR)
    tokens = acts.shape[0]

    def along_all(block):
        return [send(block, along(devices, step)) for step in range(1, steps)]

    def others(z):
        y = send(z, across(devices))
        return z, y, send(z, swap(devices)), send(y, swap(devices))

    [block] = folded(grads, 1, [])
    fetched = fetch(basis_out, [block])
    mine = basis_in.T
    theirs = send(mine, swap(devices))
    own = folded(acts, CHUNKS, [block])
    first = along_all(own[0])
    grads_all = others(pile([block] + along_all(block), [fetched, first[0]]))

    acts_z, acts_y = [], []

    def chunk_along(chunk, waits):
        acts_z.append(pile([own[chunk]] + (along_all(own[chunk]) if chunk else first), waits))
        acts_y.append(send(acts_z[-1], across(devices)))

    def part(chunk, before):
        return rotate_in(tokens, chunk, acts_z[chunk], acts_y[chunk], mine, theirs, before)

    chunk_along(0, [])
    sq_out = rotate_out(tokens, *grads_all, fetched, [acts_z[0]])
    came = along_all(sq_out)
    for chunk in range(1, CHUNKS):
        chunk_along(chunk, [sq_out])
    total = part(0, [])
    z = pile([sq_out] + came, [*total, acts_z[-1]])
    y = send(z, across(devices))
    for chunk in range(1, CHUNKS):
        total = part(chunk, total)
    sq_in, given = total
    [y] = after([y], [sq_in])
    return combine(sq_in, send(given, swap(devices)), z, y, send(z, swap(devices)), send(y, swap(devices)))


def solution(mesh):
    return jax.shard_map(
        local,
        mesh=mesh,
        in_specs=(
            P(("groups", "wide"), None),
            P(("groups", "wide"), None),
            P("groups", "wide"),
            P("groups", "wide"),
        ),
        out_specs=P(("groups", "wide"), None),
        check_vma=False,
    )
```

```python
import functools

import jax
import jax.numpy as jnp
from jax import lax
from jax.experimental import pallas as pl
from jax.experimental.pallas import tpu as pltpu
from jax.sharding import PartitionSpec as P

CORES = 2
PAIR = 2
SUBLANES = 8
FOLDS = 2
CHUNKS = 2
VMEM = pl.BlockSpec(memory_space=pltpu.VMEM)
ANY = pl.BlockSpec(memory_space=pl.ANY)


def along(devices, by):
    each = CORES * PAIR
    return [(d, (d + by * each) % devices) for d in range(devices)]


def across(devices):
    return [(d, d ^ CORES) for d in range(devices)]


def swap(devices):
    return [(d, d ^ 1) for d in range(devices)]


def send(block, pairs):
    return lax.ppermute(block, "wide", pairs)


def origin(me, devices, step, other_chip, other_core):
    each = CORES * PAIR
    pair = lax.rem(me // each + devices // each - step, devices // each)
    chip = lax.rem(me // CORES, PAIR)
    core = lax.rem(me, CORES)
    if other_chip:
        chip = 1 - chip
    if other_core:
        core = 1 - core
    return pair * PAIR + chip, core


def room(mib, blocks):
    return mib * 2**20 if blocks <= SUBLANES else 24 * 2**20


def repeat(times, body, carry=None, loop=False):
    if loop or times > SUBLANES:
        return lax.fori_loop(0, times, body, carry)
    for step in range(times):
        carry = body(step, carry)
    return carry


def unfold_store(rows, slot, block):
    height = block.shape[0]
    at = pl.ds(pl.multiple_of(slot * height, SUBLANES), height)
    for tile in range(rows.shape[0]):
        rows[tile, at, :] = block[:, tile * 128 : (tile + 1) * 128].astype(jnp.float32)


def unfold_load(rows, fold, tokens):
    tiles = [rows[tile, pl.ds(fold, tokens, stride=SUBLANES), :] for tile in range(rows.shape[0])]
    return jnp.concatenate([tile.astype(jnp.bfloat16) for tile in tiles], 1)


def rotate_out_kernel(tokens, waits, z_ref, y_ref, cz_ref, cy_ref, basis_ref, *refs):
    sq_ref, rows, total = refs[waits:]
    steps, height, width = z_ref.shape
    devices = steps * CORES * PAIR
    me = lax.axis_index("wide")

    @pl.when(pl.program_id(0) == 0)
    def _():
        for ref, chip_bit, core_bit in ((z_ref, 0, 0), (y_ref, 1, 0), (cz_ref, 0, 1), (cy_ref, 1, 1)):

            def put(step, _, ref=ref, chip_bit=chip_bit, core_bit=core_bit):
                chip, core = origin(me, devices, step, chip_bit, core_bit)
                unfold_store(rows, core * (devices // CORES) + chip, ref[step])

            repeat(steps, put)
        total[...] = jnp.zeros_like(total)

    def add(fold, _):
        left = unfold_load(rows, pl.program_id(0) * FOLDS + fold, devices * tokens)
        right = basis_ref[pl.ds(pl.multiple_of(fold * width, 128), width), :]
        total[...] += jnp.dot(left, right, preferred_element_type=jnp.float32)

    repeat(FOLDS, add, None, steps > SUBLANES)

    @pl.when(pl.program_id(0) == pl.num_programs(0) - 1)
    def _():
        sq_ref[...] = (total[...] * total[...]).astype(sq_ref.dtype)


def rotate_out(tokens, z, y, cz, cy, basis, waits):
    steps, height, width = z.shape
    total = steps * CORES * PAIR * tokens
    columns = basis.shape[1]
    return pl.pallas_call(
        functools.partial(rotate_out_kernel, tokens, len(waits)),
        grid=(SUBLANES // FOLDS,),
        out_shape=jax.ShapeDtypeStruct((total, columns), jnp.bfloat16),
        in_specs=[VMEM] * 4 + [pl.BlockSpec((FOLDS * width, columns), lambda i: (i, 0))] + [ANY] * len(waits),
        out_specs=VMEM,
        scratch_shapes=[
            pltpu.VMEM((width // 128, total * SUBLANES, 128), jnp.float32),
            pltpu.VMEM((total, columns), jnp.float32),
        ],
        compiler_params=pltpu.CompilerParams(vmem_limit_bytes=room(10, steps)),
        cost_estimate=pl.CostEstimate(
            flops=2 * total * basis.shape[0] * columns, bytes_accessed=2 * basis.size, transcendentals=0
        ),
        name="rotate_out",
    )(z, y, cz, cy, basis, *waits)


def rotate_in_kernel(tokens, chunk, before, last, own_ref, across_ref, z_ref, y_ref, mine_ref, theirs_ref, *refs):
    outs, (total, rows) = refs[before:-2], refs[-2:]
    height, width = own_ref.shape
    steps = z_ref.shape[0] + 1
    devices = steps * CORES * PAIR
    chips = devices // CORES
    me = lax.axis_index("wide")

    def put(chip, block):
        unfold_store(rows, chip, block)

    @pl.when(pl.program_id(0) == 0)
    def _():
        put(origin(me, devices, 0, 0, 0)[0], own_ref[...])
        put(origin(me, devices, 0, 1, 0)[0], across_ref[chunk])
        for ref, chip_bit in ((z_ref, 0), (y_ref, 1)):

            def put_far(step, _, ref=ref, chip_bit=chip_bit):
                put(origin(me, devices, step + 1, chip_bit, 0)[0], ref[step])

            repeat(steps - 1, put_far)
        total[...] = refs[0][...] if before else jnp.zeros_like(total)

    def add(fold, _):
        at = pl.ds(pl.multiple_of(fold * width, 128), width)
        right = unfold_load(rows, pl.program_id(0) * FOLDS + fold, chips * tokens)
        left = jnp.concatenate([mine_ref[:, at], theirs_ref[:, at]])
        total[...] += lax.dot_general(left, right, (((1,), (1,)), ((), ())), preferred_element_type=jnp.float32)

    repeat(FOLDS, add, None, steps > SUBLANES)

    @pl.when(pl.program_id(0) == pl.num_programs(0) - 1)
    def _():
        if last:
            squares = (total[...] * total[...]).astype(jnp.bfloat16)
            outs[0][...] = squares[: outs[0].shape[0]]
            outs[1][...] = squares[outs[0].shape[0] :]
        else:
            outs[0][...] = total[...]


def rotate_in(tokens, chunk, own, across, z, y, mine, theirs, before):
    height, width = own.shape
    chips = (z.shape[0] + 1) * PAIR
    last = chunk == CHUNKS - 1
    basis = pl.BlockSpec((mine.shape[0], FOLDS * width), lambda i: (0, chunk * (SUBLANES // FOLDS) + i))
    whole = jax.ShapeDtypeStruct((2 * mine.shape[0], chips * tokens), jnp.float32)
    half = jax.ShapeDtypeStruct((mine.shape[0], chips * tokens), jnp.bfloat16)
    return pl.pallas_call(
        functools.partial(rotate_in_kernel, tokens, chunk, len(before), last),
        grid=(SUBLANES // FOLDS,),
        out_shape=(half, half) if last else (whole,),
        in_specs=[VMEM] * 4 + [basis] * 2 + [VMEM] * len(before),
        out_specs=(VMEM, VMEM) if last else (VMEM,),
        scratch_shapes=[
            pltpu.VMEM(whole.shape, jnp.float32),
            pltpu.VMEM((width // 128, chips * height, 128), jnp.float32),
        ],
        compiler_params=pltpu.CompilerParams(vmem_limit_bytes=room(9, chips)),
        cost_estimate=pl.CostEstimate(
            flops=4 * chips * tokens * mine.shape[0] * SUBLANES * width,
            bytes_accessed=4 * mine.shape[0] * SUBLANES * width,
            transcendentals=0,
        ),
        name="rotate_in",
    )(own, across, z, y, mine, theirs, *before)


def fold_one(from_ref, start, out_refs, rows):
    tokens = from_ref.shape[0]
    tiles = out_refs[0].shape[1] // 128
    for tile in range(tiles):
        for fold in range(SUBLANES):
            at = start + (fold * tiles + tile) * 128
            rows[tile, pl.ds(fold, tokens, stride=SUBLANES), :] = from_ref[:, at : at + 128].astype(jnp.float32)
    for tile in range(tiles):
        block = rows[tile].astype(jnp.bfloat16)
        for out_ref in out_refs:
            out_ref[:, tile * 128 : (tile + 1) * 128] = block


def fold_kernel(grads_ref, acts_ref, block_ref, *refs):
    own, every_ref, rows = refs[:-2], refs[-2], refs[-1]
    fold_one(grads_ref, 0, [block_ref], rows)
    for chunk, out_ref in enumerate(own):
        fold_one(acts_ref, chunk * SUBLANES * out_ref.shape[1], [out_ref, every_ref.at[chunk]], rows)


def folded(grads, acts):
    height = grads.shape[0] * SUBLANES
    width = acts.shape[1] // (CHUNKS * SUBLANES)
    shapes = [(height, grads.shape[1] // SUBLANES)] + [(height, width)] * CHUNKS + [(CHUNKS, height, width)]
    tiles = max(shape[-1] for shape in shapes) // 128
    return pl.pallas_call(
        fold_kernel,
        out_shape=[jax.ShapeDtypeStruct(shape, acts.dtype) for shape in shapes],
        in_specs=[VMEM] * 2,
        out_specs=[VMEM] * len(shapes),
        scratch_shapes=[pltpu.VMEM((tiles, height, 128), jnp.float32)],
        compiler_params=pltpu.CompilerParams(vmem_limit_bytes=4 * 2**20),
        cost_estimate=pl.CostEstimate(flops=0, bytes_accessed=4 * acts.size, transcendentals=0),
        name="fold",
    )(grads, acts)


def pile_kernel(blocks, *refs):
    for step in range(blocks):
        refs[-1][step] = refs[step][...]


def pile(blocks, waits):
    return pl.pallas_call(
        functools.partial(pile_kernel, len(blocks)),
        out_shape=jax.ShapeDtypeStruct((len(blocks), *blocks[0].shape), blocks[0].dtype),
        in_specs=[VMEM] * len(blocks) + [ANY] * len(waits),
        out_specs=VMEM,
        compiler_params=pltpu.CompilerParams(vmem_limit_bytes=room(3, len(blocks))),
        cost_estimate=pl.CostEstimate(flops=0, bytes_accessed=2 * len(blocks) * blocks[0].size, transcendentals=0),
        name="pile",
    )(*blocks, *waits)


def fetch_kernel(from_ref, *refs):
    to_ref, done = refs[-2:]
    copy = pltpu.make_async_copy(from_ref, to_ref, done)
    copy.start()
    copy.wait()


def fetch(array, waits):
    return pl.pallas_call(
        fetch_kernel,
        out_shape=jax.ShapeDtypeStruct(array.shape, array.dtype),
        in_specs=[ANY] * (1 + len(waits)),
        out_specs=VMEM,
        scratch_shapes=[pltpu.SemaphoreType.DMA],
        compiler_params=pltpu.CompilerParams(vmem_limit_bytes=16 * 2**20),
        cost_estimate=pl.CostEstimate(flops=0, bytes_accessed=2 * array.size, transcendentals=0),
        name="fetch",
    )(array, *waits)


def after(arrays, waits):
    return pl.pallas_call(
        lambda *refs: None,
        out_shape=[jax.ShapeDtypeStruct(array.shape, array.dtype) for array in arrays],
        in_specs=[ANY] * (len(arrays) + len(waits)),
        out_specs=[ANY] * len(arrays),
        input_output_aliases={i: i for i in range(len(arrays))},
        compiler_params=pltpu.CompilerParams(vmem_limit_bytes=2**20),
        cost_estimate=pl.CostEstimate(flops=0, bytes_accessed=0, transcendentals=0),
        name="after",
    )(*arrays, *waits)


def both_classes(own_ref, other_ref):
    own, other = own_ref[...].astype(jnp.float32), other_ref[...].astype(jnp.float32)
    first = lax.rem(lax.axis_index("wide"), CORES) == 0
    left = jnp.concatenate([jnp.where(first, own, other), jnp.where(first, other, own)], 1)
    return left.astype(jnp.bfloat16)


def eigenvalues(left, block):
    total = jnp.dot(left, block, preferred_element_type=jnp.float32)
    return (total / block.shape[0]).astype(jnp.bfloat16)


def combine_kernel(own_ref, other_ref, z_ref, y_ref, cz_ref, out_ref):
    steps, _, width = z_ref.shape
    devices = steps * CORES * PAIR
    me = lax.axis_index("wide")
    left = both_classes(own_ref, other_ref)
    for ref, chip_bit, core_bit in ((z_ref, 0, 0), (y_ref, 1, 0), (cz_ref, 0, 1)):

        def put(step, _, ref=ref, chip_bit=chip_bit, core_bit=core_bit):
            chip, core = origin(me, devices, step, chip_bit, core_bit)
            at = pl.multiple_of((chip * CORES + core) * width, 128)
            out_ref[:, pl.ds(at, width)] = eigenvalues(left, ref[step])

        repeat(steps, put)


def combine(own, other, z, y, cz):
    steps, total_tokens, width = z.shape
    features = steps * CORES * PAIR * width
    return pl.pallas_call(
        combine_kernel,
        out_shape=jax.ShapeDtypeStruct((own.shape[0], features), jnp.bfloat16),
        in_specs=[VMEM] * 5,
        out_specs=VMEM,
        compiler_params=pltpu.CompilerParams(vmem_limit_bytes=room(6, steps)),
        cost_estimate=pl.CostEstimate(
            flops=2 * own.shape[0] * total_tokens * features, bytes_accessed=4 * own.shape[0] * features, transcendentals=0
        ),
        name="combine",
    )(own, other, z, y, cz)


def finish_kernel(own_ref, other_ref, cy_ref, _, out_ref, blocks, done):
    steps, _, width = cy_ref.shape
    devices = steps * CORES * PAIR
    me = lax.axis_index("wide")
    left = both_classes(own_ref, other_ref)
    copies = []
    for step in range(steps):
        chip, core = origin(me, devices, step, 1, 1)
        at = pl.multiple_of((chip * CORES + core) * width, 128)
        blocks[step] = eigenvalues(left, cy_ref[step])
        copies.append(pltpu.make_async_copy(blocks.at[step], out_ref.at[:, pl.ds(at, width)], done.at[step]))
        copies[-1].start()
    for copy in copies:
        copy.wait()


def finish(own, other, cy, result):
    steps, total_tokens, width = cy.shape
    return pl.pallas_call(
        finish_kernel,
        out_shape=jax.ShapeDtypeStruct(result.shape, result.dtype),
        in_specs=[VMEM] * 3 + [ANY],
        out_specs=ANY,
        scratch_shapes=[
            pltpu.VMEM((steps, own.shape[0], width), result.dtype),
            pltpu.SemaphoreType.DMA((steps,)),
        ],
        input_output_aliases={3: 0},
        compiler_params=pltpu.CompilerParams(vmem_limit_bytes=room(4, steps)),
        cost_estimate=pl.CostEstimate(
            flops=2 * own.shape[0] * total_tokens * steps * width, bytes_accessed=4 * cy.size, transcendentals=0
        ),
        name="finish",
    )(own, other, cy, result)


def local(acts, grads, basis_in, basis_out):
    devices = lax.axis_size("wide")
    steps = devices // (CORES * PAIR)
    tokens = acts.shape[0]

    def along_all(block):
        return [send(block, along(devices, step)) for step in range(1, steps)]

    def others(z):
        y = send(z, across(devices))
        return z, y, send(z, swap(devices)), send(y, swap(devices))

    block, *own, every = folded(grads, acts)
    fetched = fetch(basis_out, [block])
    mine = basis_in.T
    theirs = send(mine, swap(devices))
    own_across = send(every, across(devices))
    grads_all = others(pile([block] + along_all(block), [own_across, fetched]))

    acts_z, acts_y = [], []

    def chunk_along(chunk, waits):
        acts_z.append(pile(along_all(own[chunk]), waits))
        acts_y.append(send(acts_z[-1], across(devices)))

    def part(chunk, before):
        return rotate_in(tokens, chunk, own[chunk], own_across, acts_z[chunk], acts_y[chunk], mine, theirs, before)

    chunk_along(0, [])
    sq_out = rotate_out(tokens, *grads_all, fetched, [acts_z[0]])
    came = along_all(sq_out)
    for chunk in range(1, CHUNKS):
        chunk_along(chunk, [sq_out])
    total = part(0, [])
    z = pile([sq_out] + came, [*total, acts_z[-1]])
    y = send(z, across(devices))
    for chunk in range(1, CHUNKS):
        total = part(chunk, total)
    sq_in, given = total
    other = send(given, swap(devices))
    [y] = after([y], [other])
    cz, cy = send(z, swap(devices)), send(y, swap(devices))
    return finish(sq_in, other, cy, combine(sq_in, other, z, y, cz))


def solution(mesh):
    return jax.shard_map(
        local,
        mesh=mesh,
        in_specs=(
            P(("groups", "wide"), None),
            P(("groups", "wide"), None),
            P("groups", "wide"),
            P("groups", "wide"),
        ),
        out_specs=P(("groups", "wide"), None),
        check_vma=False,
    )
```

```python
import functools

import jax
import jax.numpy as jnp
from jax import lax
from jax.experimental import pallas as pl
from jax.experimental.pallas import tpu as pltpu
from jax.sharding import PartitionSpec as P

CORES = 2
PAIR = 2
SUBLANES = 8
FOLDS = 2
CHUNKS = 2
VMEM = pl.BlockSpec(memory_space=pltpu.VMEM)
ANY = pl.BlockSpec(memory_space=pl.ANY)


def along(devices, by):
    each = CORES * PAIR
    return [(d, (d + by * each) % devices) for d in range(devices)]


def across(devices):
    return [(d, d ^ CORES) for d in range(devices)]


def swap(devices):
    return [(d, d ^ 1) for d in range(devices)]


def send(block, pairs):
    return lax.ppermute(block, "wide", pairs)


def origin(me, devices, step, other_chip, other_core):
    each = CORES * PAIR
    pair = lax.rem(me // each + devices // each - step, devices // each)
    chip = lax.rem(me // CORES, PAIR)
    core = lax.rem(me, CORES)
    if other_chip:
        chip = 1 - chip
    if other_core:
        core = 1 - core
    return pair * PAIR + chip, core


def room(mib, blocks):
    return mib * 2**20 if blocks <= SUBLANES else 24 * 2**20


def repeat(times, body, carry=None, loop=False):
    if loop or times > SUBLANES:
        return lax.fori_loop(0, times, body, carry)
    for step in range(times):
        carry = body(step, carry)
    return carry


def unfold_store(rows, slot, block):
    height = block.shape[0]
    at = pl.ds(pl.multiple_of(slot * height, SUBLANES), height)
    for tile in range(rows.shape[0]):
        rows[tile, at, :] = block[:, tile * 128 : (tile + 1) * 128].astype(jnp.float32)


def unfold_load(rows, fold, tokens):
    tiles = [rows[tile, pl.ds(fold, tokens, stride=SUBLANES), :] for tile in range(rows.shape[0])]
    return jnp.concatenate([tile.astype(jnp.bfloat16) for tile in tiles], 1)


def rotate_out_kernel(tokens, waits, z_ref, y_ref, cz_ref, cy_ref, basis_ref, *refs):
    sq_ref, rows, total = refs[waits:]
    steps, height, width = z_ref.shape
    devices = steps * CORES * PAIR
    me = lax.axis_index("wide")

    @pl.when(pl.program_id(0) == 0)
    def _():
        for ref, chip_bit, core_bit in ((z_ref, 0, 0), (y_ref, 1, 0), (cz_ref, 0, 1), (cy_ref, 1, 1)):

            def put(step, _, ref=ref, chip_bit=chip_bit, core_bit=core_bit):
                chip, core = origin(me, devices, step, chip_bit, core_bit)
                unfold_store(rows, core * (devices // CORES) + chip, ref[step])

            repeat(steps, put)
        total[...] = jnp.zeros_like(total)

    def add(fold, _):
        left = unfold_load(rows, pl.program_id(0) * FOLDS + fold, devices * tokens)
        right = basis_ref[pl.ds(pl.multiple_of(fold * width, 128), width), :]
        total[...] += jnp.dot(left, right, preferred_element_type=jnp.float32)

    repeat(FOLDS, add, None, steps > SUBLANES)

    @pl.when(pl.program_id(0) == pl.num_programs(0) - 1)
    def _():
        sq_ref[...] = (total[...] * total[...]).astype(sq_ref.dtype)


def rotate_out(tokens, z, y, cz, cy, basis, waits):
    steps, height, width = z.shape
    total = steps * CORES * PAIR * tokens
    columns = basis.shape[1]
    return pl.pallas_call(
        functools.partial(rotate_out_kernel, tokens, len(waits)),
        grid=(SUBLANES // FOLDS,),
        out_shape=jax.ShapeDtypeStruct((total, columns), jnp.bfloat16),
        in_specs=[VMEM] * 4 + [pl.BlockSpec((FOLDS * width, columns), lambda i: (i, 0))] + [ANY] * len(waits),
        out_specs=VMEM,
        scratch_shapes=[
            pltpu.VMEM((width // 128, total * SUBLANES, 128), jnp.float32),
            pltpu.VMEM((total, columns), jnp.float32),
        ],
        compiler_params=pltpu.CompilerParams(vmem_limit_bytes=room(10, steps)),
        cost_estimate=pl.CostEstimate(
            flops=2 * total * basis.shape[0] * columns, bytes_accessed=2 * basis.size, transcendentals=0
        ),
        name="rotate_out",
    )(z, y, cz, cy, basis, *waits)


def rotate_in_kernel(tokens, chunk, before, last, own_ref, across_ref, z_ref, y_ref, mine_ref, theirs_ref, *refs):
    outs, (total, rows) = refs[before:-2], refs[-2:]
    height, width = own_ref.shape
    steps = z_ref.shape[0] + 1
    devices = steps * CORES * PAIR
    chips = devices // CORES
    me = lax.axis_index("wide")

    def put(chip, block):
        unfold_store(rows, chip, block)

    @pl.when(pl.program_id(0) == 0)
    def _():
        put(origin(me, devices, 0, 0, 0)[0], own_ref[...])
        put(origin(me, devices, 0, 1, 0)[0], across_ref[chunk])
        for ref, chip_bit in ((z_ref, 0), (y_ref, 1)):

            def put_far(step, _, ref=ref, chip_bit=chip_bit):
                put(origin(me, devices, step + 1, chip_bit, 0)[0], ref[step])

            repeat(steps - 1, put_far)
        total[...] = refs[0][...] if before else jnp.zeros_like(total)

    def add(fold, _):
        at = pl.ds(pl.multiple_of(fold * width, 128), width)
        right = unfold_load(rows, pl.program_id(0) * FOLDS + fold, chips * tokens)
        left = jnp.concatenate([mine_ref[:, at], theirs_ref[:, at]])
        total[...] += lax.dot_general(left, right, (((1,), (1,)), ((), ())), preferred_element_type=jnp.float32)

    repeat(FOLDS, add, None, steps > SUBLANES)

    @pl.when(pl.program_id(0) == pl.num_programs(0) - 1)
    def _():
        if last:
            squares = (total[...] * total[...]).astype(jnp.bfloat16)
            outs[0][...] = squares[: outs[0].shape[0]]
            outs[1][...] = squares[outs[0].shape[0] :]
        else:
            outs[0][...] = total[...]


def rotate_in(tokens, chunk, own, across, z, y, mine, theirs, before):
    height, width = own.shape
    chips = (z.shape[0] + 1) * PAIR
    last = chunk == CHUNKS - 1
    basis = pl.BlockSpec((mine.shape[0], FOLDS * width), lambda i: (0, chunk * (SUBLANES // FOLDS) + i))
    whole = jax.ShapeDtypeStruct((2 * mine.shape[0], chips * tokens), jnp.float32)
    half = jax.ShapeDtypeStruct((mine.shape[0], chips * tokens), jnp.bfloat16)
    return pl.pallas_call(
        functools.partial(rotate_in_kernel, tokens, chunk, len(before), last),
        grid=(SUBLANES // FOLDS,),
        out_shape=(half, half) if last else (whole,),
        in_specs=[VMEM] * 4 + [basis] * 2 + [VMEM] * len(before),
        out_specs=(VMEM, VMEM) if last else (VMEM,),
        scratch_shapes=[
            pltpu.VMEM(whole.shape, jnp.float32),
            pltpu.VMEM((width // 128, chips * height, 128), jnp.float32),
        ],
        compiler_params=pltpu.CompilerParams(vmem_limit_bytes=room(9, chips)),
        cost_estimate=pl.CostEstimate(
            flops=4 * chips * tokens * mine.shape[0] * SUBLANES * width,
            bytes_accessed=4 * mine.shape[0] * SUBLANES * width,
            transcendentals=0,
        ),
        name="rotate_in",
    )(own, across, z, y, mine, theirs, *before)


def fold_one(from_ref, start, out_refs, rows):
    tokens = from_ref.shape[0]
    tiles = out_refs[0].shape[1] // 128
    for tile in range(tiles):
        for fold in range(SUBLANES):
            at = start + (fold * tiles + tile) * 128
            rows[tile, pl.ds(fold, tokens, stride=SUBLANES), :] = from_ref[:, at : at + 128].astype(jnp.float32)
    for tile in range(tiles):
        block = rows[tile].astype(jnp.bfloat16)
        for out_ref in out_refs:
            out_ref[:, tile * 128 : (tile + 1) * 128] = block


def fold_kernel(grads_ref, acts_ref, block_ref, *refs):
    own, every_ref, rows = refs[:-2], refs[-2], refs[-1]
    fold_one(grads_ref, 0, [block_ref], rows)
    for chunk, out_ref in enumerate(own):
        fold_one(acts_ref, chunk * SUBLANES * out_ref.shape[1], [out_ref, every_ref.at[chunk]], rows)


def folded(grads, acts):
    height = grads.shape[0] * SUBLANES
    width = acts.shape[1] // (CHUNKS * SUBLANES)
    shapes = [(height, grads.shape[1] // SUBLANES)] + [(height, width)] * CHUNKS + [(CHUNKS, height, width)]
    tiles = max(shape[-1] for shape in shapes) // 128
    return pl.pallas_call(
        fold_kernel,
        out_shape=[jax.ShapeDtypeStruct(shape, acts.dtype) for shape in shapes],
        in_specs=[VMEM] * 2,
        out_specs=[VMEM] * len(shapes),
        scratch_shapes=[pltpu.VMEM((tiles, height, 128), jnp.float32)],
        compiler_params=pltpu.CompilerParams(vmem_limit_bytes=4 * 2**20),
        cost_estimate=pl.CostEstimate(flops=0, bytes_accessed=4 * acts.size, transcendentals=0),
        name="fold",
    )(grads, acts)


def pile_kernel(blocks, *refs):
    for step in range(blocks):
        refs[-1][step] = refs[step][...]


def pile(blocks, waits):
    return pl.pallas_call(
        functools.partial(pile_kernel, len(blocks)),
        out_shape=jax.ShapeDtypeStruct((len(blocks), *blocks[0].shape), blocks[0].dtype),
        in_specs=[VMEM] * len(blocks) + [ANY] * len(waits),
        out_specs=VMEM,
        compiler_params=pltpu.CompilerParams(vmem_limit_bytes=room(3, len(blocks))),
        cost_estimate=pl.CostEstimate(flops=0, bytes_accessed=2 * len(blocks) * blocks[0].size, transcendentals=0),
        name="pile",
    )(*blocks, *waits)


def fetch_kernel(from_ref, *refs):
    to_ref, done = refs[-2:]
    copy = pltpu.make_async_copy(from_ref, to_ref, done)
    copy.start()
    copy.wait()


def fetch(array, waits):
    return pl.pallas_call(
        fetch_kernel,
        out_shape=jax.ShapeDtypeStruct(array.shape, array.dtype),
        in_specs=[ANY] * (1 + len(waits)),
        out_specs=VMEM,
        scratch_shapes=[pltpu.SemaphoreType.DMA],
        compiler_params=pltpu.CompilerParams(vmem_limit_bytes=16 * 2**20),
        cost_estimate=pl.CostEstimate(flops=0, bytes_accessed=2 * array.size, transcendentals=0),
        name="fetch",
    )(array, *waits)


def after(arrays, waits):
    return pl.pallas_call(
        lambda *refs: None,
        out_shape=[jax.ShapeDtypeStruct(array.shape, array.dtype) for array in arrays],
        in_specs=[ANY] * (len(arrays) + len(waits)),
        out_specs=[ANY] * len(arrays),
        input_output_aliases={i: i for i in range(len(arrays))},
        compiler_params=pltpu.CompilerParams(vmem_limit_bytes=2**20),
        cost_estimate=pl.CostEstimate(flops=0, bytes_accessed=0, transcendentals=0),
        name="after",
    )(*arrays, *waits)


def both_classes(own_ref, other_ref):
    own, other = own_ref[...].astype(jnp.float32), other_ref[...].astype(jnp.float32)
    first = lax.rem(lax.axis_index("wide"), CORES) == 0
    left = jnp.concatenate([jnp.where(first, own, other), jnp.where(first, other, own)], 1)
    return left.astype(jnp.bfloat16)


def eigenvalues(left, block):
    total = jnp.dot(left, block, preferred_element_type=jnp.float32)
    return (total / block.shape[0]).astype(jnp.bfloat16)


def combine_kernel(own_ref, other_ref, z_ref, y_ref, cz_ref, out_ref):
    steps, _, width = z_ref.shape
    devices = steps * CORES * PAIR
    me = lax.axis_index("wide")
    left = both_classes(own_ref, other_ref)
    for ref, chip_bit, core_bit in ((z_ref, 0, 0), (y_ref, 1, 0), (cz_ref, 0, 1)):

        def put(step, _, ref=ref, chip_bit=chip_bit, core_bit=core_bit):
            chip, core = origin(me, devices, step, chip_bit, core_bit)
            at = pl.multiple_of((chip * CORES + core) * width, 128)
            out_ref[:, pl.ds(at, width)] = eigenvalues(left, ref[step])

        repeat(steps, put)


def combine(own, other, z, y, cz):
    steps, total_tokens, width = z.shape
    features = steps * CORES * PAIR * width
    return pl.pallas_call(
        combine_kernel,
        out_shape=jax.ShapeDtypeStruct((own.shape[0], features), jnp.bfloat16),
        in_specs=[VMEM] * 5,
        out_specs=VMEM,
        compiler_params=pltpu.CompilerParams(vmem_limit_bytes=room(6, steps)),
        cost_estimate=pl.CostEstimate(
            flops=2 * own.shape[0] * total_tokens * features, bytes_accessed=4 * own.shape[0] * features, transcendentals=0
        ),
        name="combine",
    )(own, other, z, y, cz)


def finish_kernel(own_ref, other_ref, cy_ref, _, out_ref, blocks, done):
    steps, _, width = cy_ref.shape
    devices = steps * CORES * PAIR
    me = lax.axis_index("wide")
    left = both_classes(own_ref, other_ref)
    copies = []
    for step in range(steps):
        chip, core = origin(me, devices, step, 1, 1)
        at = pl.multiple_of((chip * CORES + core) * width, 128)
        blocks[step] = eigenvalues(left, cy_ref[step])
        copies.append(pltpu.make_async_copy(blocks.at[step], out_ref.at[:, pl.ds(at, width)], done.at[step]))
        copies[-1].start()
    for copy in copies:
        copy.wait()


def finish(own, other, cy, result):
    steps, total_tokens, width = cy.shape
    return pl.pallas_call(
        finish_kernel,
        out_shape=jax.ShapeDtypeStruct(result.shape, result.dtype),
        in_specs=[VMEM] * 3 + [ANY],
        out_specs=ANY,
        scratch_shapes=[
            pltpu.VMEM((steps, own.shape[0], width), result.dtype),
            pltpu.SemaphoreType.DMA((steps,)),
        ],
        input_output_aliases={3: 0},
        compiler_params=pltpu.CompilerParams(vmem_limit_bytes=room(4, steps)),
        cost_estimate=pl.CostEstimate(
            flops=2 * own.shape[0] * total_tokens * steps * width, bytes_accessed=4 * cy.size, transcendentals=0
        ),
        name="finish",
    )(own, other, cy, result)


def local(acts, grads, basis_in, basis_out):
    devices = lax.axis_size("wide")
    steps = devices // (CORES * PAIR)
    tokens = acts.shape[0]

    def along_all(block):
        return [send(block, along(devices, step)) for step in range(1, steps)]

    def others(z):
        y = send(z, across(devices))
        return z, y, send(z, swap(devices)), send(y, swap(devices))

    block, *own, every = folded(grads, acts)
    fetched = fetch(basis_out, [block])
    mine = basis_in.T
    theirs = send(mine, swap(devices))
    own_across = send(every, across(devices))
    grads_z = pile([block] + along_all(block), [own_across, fetched, theirs])
    grads_y = send(grads_z, across(devices))

    acts_z, acts_y = [], []

    sent = [along_all(block) for block in own]

    def chunk_along(chunk, waits):
        acts_z.append(pile(sent[chunk], waits))
        acts_y.append(send(acts_z[-1], across(devices)))

    def part(chunk, before):
        return rotate_in(tokens, chunk, own[chunk], own_across, acts_z[chunk], acts_y[chunk], mine, theirs, before)

    chunk_along(0, [sent[1][0]])
    grads_cz, grads_cy = send(grads_z, swap(devices)), send(grads_y, swap(devices))
    sq_out = rotate_out(tokens, grads_z, grads_y, grads_cz, grads_cy, fetched, [acts_z[0]])
    came = along_all(sq_out)
    for chunk in range(1, CHUNKS):
        chunk_along(chunk, [sq_out])
    total = part(0, [])
    z = pile([sq_out] + came, [*total, acts_z[-1]])
    y = send(z, across(devices))
    for chunk in range(1, CHUNKS):
        total = part(chunk, total)
    sq_in, given = total
    other = send(given, swap(devices))
    [y] = after([y], [other])
    cz, cy = send(z, swap(devices)), send(y, swap(devices))
    return finish(sq_in, other, cy, combine(sq_in, other, z, y, cz))


def solution(mesh):
    return jax.shard_map(
        local,
        mesh=mesh,
        in_specs=(
            P(("groups", "wide"), None),
            P(("groups", "wide"), None),
            P("groups", "wide"),
            P("groups", "wide"),
        ),
        out_specs=P(("groups", "wide"), None),
        check_vma=False,
    )
```

```python
import functools

import jax
import jax.numpy as jnp
from jax import lax
from jax.experimental import pallas as pl
from jax.experimental.pallas import tpu as pltpu
from jax.sharding import PartitionSpec as P

CORES = 2
PAIR = 2
SUBLANES = 8
FOLDS = 2
CHUNKS = 2
VMEM = pl.BlockSpec(memory_space=pltpu.VMEM)
ANY = pl.BlockSpec(memory_space=pl.ANY)


def along(devices, by):
    each = CORES * PAIR
    return [(d, (d + by * each) % devices) for d in range(devices)]


def across(devices):
    return [(d, d ^ CORES) for d in range(devices)]


def swap(devices):
    return [(d, d ^ 1) for d in range(devices)]


def send(block, pairs):
    return lax.ppermute(block, "wide", pairs)


def origin(me, devices, step, other_chip, other_core):
    each = CORES * PAIR
    pair = lax.rem(me // each + devices // each - step, devices // each)
    chip = lax.rem(me // CORES, PAIR)
    core = lax.rem(me, CORES)
    if other_chip:
        chip = 1 - chip
    if other_core:
        core = 1 - core
    return pair * PAIR + chip, core


def room(mib, blocks):
    return mib * 2**20 if blocks <= SUBLANES else 24 * 2**20


def repeat(times, body, carry=None, loop=False):
    if loop or times > SUBLANES:
        return lax.fori_loop(0, times, body, carry)
    for step in range(times):
        carry = body(step, carry)
    return carry


def unfold_store(rows, slot, block):
    height = block.shape[0]
    at = pl.ds(pl.multiple_of(slot * height, SUBLANES), height)
    for tile in range(rows.shape[0]):
        rows[tile, at, :] = block[:, tile * 128 : (tile + 1) * 128].astype(jnp.float32)


def unfold_load(rows, fold, tokens):
    tiles = [rows[tile, pl.ds(fold, tokens, stride=SUBLANES), :] for tile in range(rows.shape[0])]
    return jnp.concatenate([tile.astype(jnp.bfloat16) for tile in tiles], 1)


def rotate_out_kernel(tokens, waits, z_ref, y_ref, cz_ref, cy_ref, basis_ref, *refs):
    sq_ref, rows, total = refs[waits:]
    steps, height, width = z_ref.shape
    devices = steps * CORES * PAIR
    me = lax.axis_index("wide")

    @pl.when(pl.program_id(0) == 0)
    def _():
        for ref, chip_bit, core_bit in ((z_ref, 0, 0), (y_ref, 1, 0), (cz_ref, 0, 1), (cy_ref, 1, 1)):

            def put(step, _, ref=ref, chip_bit=chip_bit, core_bit=core_bit):
                chip, core = origin(me, devices, step, chip_bit, core_bit)
                unfold_store(rows, core * (devices // CORES) + chip, ref[step])

            repeat(steps, put)
        total[...] = jnp.zeros_like(total)

    def add(fold, _):
        left = unfold_load(rows, pl.program_id(0) * FOLDS + fold, devices * tokens)
        right = basis_ref[pl.ds(pl.multiple_of(fold * width, 128), width), :]
        total[...] += jnp.dot(left, right, preferred_element_type=jnp.float32)

    repeat(FOLDS, add, None, steps > SUBLANES)

    @pl.when(pl.program_id(0) == pl.num_programs(0) - 1)
    def _():
        sq_ref[...] = (total[...] * total[...]).astype(sq_ref.dtype)


def rotate_out(tokens, z, y, cz, cy, basis, waits):
    steps, height, width = z.shape
    total = steps * CORES * PAIR * tokens
    columns = basis.shape[1]
    return pl.pallas_call(
        functools.partial(rotate_out_kernel, tokens, len(waits)),
        grid=(SUBLANES // FOLDS,),
        out_shape=jax.ShapeDtypeStruct((total, columns), jnp.bfloat16),
        in_specs=[VMEM] * 4 + [pl.BlockSpec((FOLDS * width, columns), lambda i: (i, 0))] + [ANY] * len(waits),
        out_specs=VMEM,
        scratch_shapes=[
            pltpu.VMEM((width // 128, total * SUBLANES, 128), jnp.float32),
            pltpu.VMEM((total, columns), jnp.float32),
        ],
        compiler_params=pltpu.CompilerParams(vmem_limit_bytes=room(10, steps)),
        cost_estimate=pl.CostEstimate(
            flops=2 * total * basis.shape[0] * columns, bytes_accessed=2 * basis.size, transcendentals=0
        ),
        name="rotate_out",
    )(z, y, cz, cy, basis, *waits)


def rotate_in_kernel(tokens, chunk, before, last, own_ref, across_ref, z_ref, y_ref, mine_ref, theirs_ref, *refs):
    outs, (total, rows) = refs[before:-2], refs[-2:]
    height, width = own_ref.shape
    steps = z_ref.shape[0] + 1
    devices = steps * CORES * PAIR
    chips = devices // CORES
    me = lax.axis_index("wide")

    def put(chip, block):
        unfold_store(rows, chip, block)

    @pl.when(pl.program_id(0) == 0)
    def _():
        put(origin(me, devices, 0, 0, 0)[0], own_ref[...])
        put(origin(me, devices, 0, 1, 0)[0], across_ref[chunk])
        for ref, chip_bit in ((z_ref, 0), (y_ref, 1)):

            def put_far(step, _, ref=ref, chip_bit=chip_bit):
                put(origin(me, devices, step + 1, chip_bit, 0)[0], ref[step])

            repeat(steps - 1, put_far)
        total[...] = refs[0][...] if before else jnp.zeros_like(total)

    def add(fold, _):
        at = pl.ds(pl.multiple_of(fold * width, 128), width)
        right = unfold_load(rows, pl.program_id(0) * FOLDS + fold, chips * tokens)
        left = jnp.concatenate([mine_ref[:, at], theirs_ref[:, at]])
        total[...] += lax.dot_general(left, right, (((1,), (1,)), ((), ())), preferred_element_type=jnp.float32)

    repeat(FOLDS, add, None, steps > SUBLANES)

    @pl.when(pl.program_id(0) == pl.num_programs(0) - 1)
    def _():
        if last:
            squares = (total[...] * total[...]).astype(jnp.bfloat16)
            outs[0][...] = squares[: outs[0].shape[0]]
            outs[1][...] = squares[outs[0].shape[0] :]
        else:
            outs[0][...] = total[...]


def rotate_in(tokens, chunk, own, across, z, y, mine, theirs, before):
    height, width = own.shape
    chips = (z.shape[0] + 1) * PAIR
    last = chunk == CHUNKS - 1
    basis = pl.BlockSpec((mine.shape[0], FOLDS * width), lambda i: (0, chunk * (SUBLANES // FOLDS) + i))
    whole = jax.ShapeDtypeStruct((2 * mine.shape[0], chips * tokens), jnp.float32)
    half = jax.ShapeDtypeStruct((mine.shape[0], chips * tokens), jnp.bfloat16)
    return pl.pallas_call(
        functools.partial(rotate_in_kernel, tokens, chunk, len(before), last),
        grid=(SUBLANES // FOLDS,),
        out_shape=(half, half) if last else (whole,),
        in_specs=[VMEM] * 4 + [basis] * 2 + [VMEM] * len(before),
        out_specs=(VMEM, VMEM) if last else (VMEM,),
        scratch_shapes=[
            pltpu.VMEM(whole.shape, jnp.float32),
            pltpu.VMEM((width // 128, chips * height, 128), jnp.float32),
        ],
        compiler_params=pltpu.CompilerParams(vmem_limit_bytes=room(9, chips)),
        cost_estimate=pl.CostEstimate(
            flops=4 * chips * tokens * mine.shape[0] * SUBLANES * width,
            bytes_accessed=4 * mine.shape[0] * SUBLANES * width,
            transcendentals=0,
        ),
        name="rotate_in",
    )(own, across, z, y, mine, theirs, *before)


def fold_one(from_ref, start, out_refs, rows):
    tokens = from_ref.shape[0]
    tiles = out_refs[0].shape[1] // 128
    for tile in range(tiles):
        for fold in range(SUBLANES):
            at = start + (fold * tiles + tile) * 128
            rows[tile, pl.ds(fold, tokens, stride=SUBLANES), :] = from_ref[:, at : at + 128].astype(jnp.float32)
    for tile in range(tiles):
        block = rows[tile].astype(jnp.bfloat16)
        for out_ref in out_refs:
            out_ref[:, tile * 128 : (tile + 1) * 128] = block


def fold_kernel(grads_ref, acts_ref, block_ref, *refs):
    own, every_ref, rows = refs[:-2], refs[-2], refs[-1]
    fold_one(grads_ref, 0, [block_ref], rows)
    for chunk, out_ref in enumerate(own):
        fold_one(acts_ref, chunk * SUBLANES * out_ref.shape[1], [out_ref, every_ref.at[chunk]], rows)


def folded(grads, acts):
    height = grads.shape[0] * SUBLANES
    width = acts.shape[1] // (CHUNKS * SUBLANES)
    shapes = [(height, grads.shape[1] // SUBLANES)] + [(height, width)] * CHUNKS + [(CHUNKS, height, width)]
    tiles = max(shape[-1] for shape in shapes) // 128
    return pl.pallas_call(
        fold_kernel,
        out_shape=[jax.ShapeDtypeStruct(shape, acts.dtype) for shape in shapes],
        in_specs=[VMEM] * 2,
        out_specs=[VMEM] * len(shapes),
        scratch_shapes=[pltpu.VMEM((tiles, height, 128), jnp.float32)],
        compiler_params=pltpu.CompilerParams(vmem_limit_bytes=4 * 2**20),
        cost_estimate=pl.CostEstimate(flops=0, bytes_accessed=4 * acts.size, transcendentals=0),
        name="fold",
    )(grads, acts)


def pile_kernel(blocks, *refs):
    for step in range(blocks):
        refs[-1][step] = refs[step][...]


def pile(blocks, waits):
    return pl.pallas_call(
        functools.partial(pile_kernel, len(blocks)),
        out_shape=jax.ShapeDtypeStruct((len(blocks), *blocks[0].shape), blocks[0].dtype),
        in_specs=[VMEM] * len(blocks) + [ANY] * len(waits),
        out_specs=VMEM,
        compiler_params=pltpu.CompilerParams(vmem_limit_bytes=room(3, len(blocks))),
        cost_estimate=pl.CostEstimate(flops=0, bytes_accessed=2 * len(blocks) * blocks[0].size, transcendentals=0),
        name="pile",
    )(*blocks, *waits)


def fetch_kernel(from_ref, *refs):
    to_ref, done = refs[-2:]
    copy = pltpu.make_async_copy(from_ref, to_ref, done)
    copy.start()
    copy.wait()


def fetch(array, waits):
    return pl.pallas_call(
        fetch_kernel,
        out_shape=jax.ShapeDtypeStruct(array.shape, array.dtype),
        in_specs=[ANY] * (1 + len(waits)),
        out_specs=VMEM,
        scratch_shapes=[pltpu.SemaphoreType.DMA],
        compiler_params=pltpu.CompilerParams(vmem_limit_bytes=16 * 2**20),
        cost_estimate=pl.CostEstimate(flops=0, bytes_accessed=2 * array.size, transcendentals=0),
        name="fetch",
    )(array, *waits)


def after(arrays, waits):
    return pl.pallas_call(
        lambda *refs: None,
        out_shape=[jax.ShapeDtypeStruct(array.shape, array.dtype) for array in arrays],
        in_specs=[ANY] * (len(arrays) + len(waits)),
        out_specs=[ANY] * len(arrays),
        input_output_aliases={i: i for i in range(len(arrays))},
        compiler_params=pltpu.CompilerParams(vmem_limit_bytes=2**20),
        cost_estimate=pl.CostEstimate(flops=0, bytes_accessed=0, transcendentals=0),
        name="after",
    )(*arrays, *waits)


def both_classes(own_ref, other_ref):
    own, other = own_ref[...].astype(jnp.float32), other_ref[...].astype(jnp.float32)
    first = lax.rem(lax.axis_index("wide"), CORES) == 0
    left = jnp.concatenate([jnp.where(first, own, other), jnp.where(first, other, own)], 1)
    return left.astype(jnp.bfloat16)


def eigenvalues(left, block):
    total = jnp.dot(left, block, preferred_element_type=jnp.float32)
    return (total / block.shape[0]).astype(jnp.bfloat16)


def put_all(left, out_ref, steps, pieces):
    devices = steps * CORES * PAIR
    me = lax.axis_index("wide")
    for ref, first, chip_bit, core_bit in pieces:

        def put(step, _, ref=ref, first=first, chip_bit=chip_bit, core_bit=core_bit):
            chip, core = origin(me, devices, step + first, chip_bit, core_bit)
            width = ref.shape[2]
            at = pl.multiple_of((chip * CORES + core) * width, 128)
            out_ref[:, pl.ds(at, width)] = eigenvalues(left, ref[step])

        repeat(ref.shape[0], put)


def combine_kernel(own_ref, other_ref, near_ref, swapped_ref, z_ref, y_ref, cz_ref, out_ref):
    left = both_classes(own_ref, other_ref)
    pieces = [(ref.at[bit : bit + 1], 0, bit, core) for core, ref in enumerate((near_ref, swapped_ref)) for bit in range(PAIR)]
    put_all(left, out_ref, z_ref.shape[0] + 1, pieces + [(z_ref, 1, 0, 0), (y_ref, 1, 1, 0), (cz_ref, 1, 0, 1)])


def combine(own, other, near, swapped, z, y, cz):
    blocks, total_tokens, width = z.shape
    features = (blocks + 1) * CORES * PAIR * width
    return pl.pallas_call(
        combine_kernel,
        out_shape=jax.ShapeDtypeStruct((own.shape[0], features), jnp.bfloat16),
        in_specs=[VMEM] * 7,
        out_specs=VMEM,
        compiler_params=pltpu.CompilerParams(vmem_limit_bytes=room(6, blocks)),
        cost_estimate=pl.CostEstimate(
            flops=2 * own.shape[0] * total_tokens * features, bytes_accessed=4 * own.shape[0] * features, transcendentals=0
        ),
        name="combine",
    )(own, other, near, swapped, z, y, cz)


def finish_kernel(own_ref, other_ref, cy_ref, _, out_ref, blocks, done):
    steps, _, width = cy_ref.shape
    devices = (steps + 1) * CORES * PAIR
    me = lax.axis_index("wide")
    left = both_classes(own_ref, other_ref)
    copies = []
    for step in range(steps):
        chip, core = origin(me, devices, step + 1, 1, 1)
        at = pl.multiple_of((chip * CORES + core) * width, 128)
        blocks[step] = eigenvalues(left, cy_ref[step])
        copies.append(pltpu.make_async_copy(blocks.at[step], out_ref.at[:, pl.ds(at, width)], done.at[step]))
        copies[-1].start()
    for copy in copies:
        copy.wait()


def finish(own, other, cy, result):
    steps, total_tokens, width = cy.shape
    return pl.pallas_call(
        finish_kernel,
        out_shape=jax.ShapeDtypeStruct(result.shape, result.dtype),
        in_specs=[VMEM] * 3 + [ANY],
        out_specs=ANY,
        scratch_shapes=[
            pltpu.VMEM((steps, own.shape[0], width), result.dtype),
            pltpu.SemaphoreType.DMA((steps,)),
        ],
        input_output_aliases={3: 0},
        compiler_params=pltpu.CompilerParams(vmem_limit_bytes=room(4, steps)),
        cost_estimate=pl.CostEstimate(
            flops=2 * own.shape[0] * total_tokens * steps * width, bytes_accessed=4 * cy.size, transcendentals=0
        ),
        name="finish",
    )(own, other, cy, result)


def local(acts, grads, basis_in, basis_out):
    devices = lax.axis_size("wide")
    steps = devices // (CORES * PAIR)
    tokens = acts.shape[0]

    def along_all(block):
        return [send(block, along(devices, step)) for step in range(1, steps)]

    def others(z):
        y = send(z, across(devices))
        return z, y, send(z, swap(devices)), send(y, swap(devices))

    block, *own, every = folded(grads, acts)
    fetched = fetch(basis_out, [block])
    mine = basis_in.T
    theirs = send(mine, swap(devices))
    own_across = send(every, across(devices))
    grads_z = pile([block] + along_all(block), [own_across, fetched, theirs])
    grads_y = send(grads_z, across(devices))

    acts_z, acts_y = [], []

    def chunk_along(chunk, waits):
        acts_z.append(pile(along_all(own[chunk]), waits))
        acts_y.append(send(acts_z[-1], across(devices)))

    def part(chunk, before):
        return rotate_in(tokens, chunk, own[chunk], own_across, acts_z[chunk], acts_y[chunk], mine, theirs, before)

    chunk_along(0, [])
    [grads_y] = after([grads_y], [acts_z[0]])
    grads_cz, grads_cy = send(grads_z, swap(devices)), send(grads_y, swap(devices))
    sq_out = rotate_out(tokens, grads_z, grads_y, grads_cz, grads_cy, fetched, [acts_z[0]])
    near = pile([sq_out, send(sq_out, across(devices))], [])
    swapped = send(near, swap(devices))
    came = along_all(sq_out)
    for chunk in range(1, CHUNKS):
        chunk_along(chunk, [came[0]])
    total = part(0, [])
    z = pile(came, [*total, acts_z[-1], near])
    y = send(z, across(devices))
    for chunk in range(1, CHUNKS):
        total = part(chunk, total)
    sq_in, given = total
    other = send(given, swap(devices))
    [y] = after([y], [other, swapped])
    cz, cy = send(z, swap(devices)), send(y, swap(devices))
    return finish(sq_in, other, cy, combine(sq_in, other, near, swapped, z, y, cz))


def solution(mesh):
    return jax.shard_map(
        local,
        mesh=mesh,
        in_specs=(
            P(("groups", "wide"), None),
            P(("groups", "wide"), None),
            P("groups", "wide"),
            P("groups", "wide"),
        ),
        out_specs=P(("groups", "wide"), None),
        check_vma=False,
    )
```

```python
import functools

import jax
import jax.numpy as jnp
from jax import lax
from jax.experimental import pallas as pl
from jax.experimental.pallas import tpu as pltpu
from jax.sharding import PartitionSpec as P

CORES = 2
PAIR = 2
SUBLANES = 8
FOLDS = 2
CHUNKS = 2
VMEM = pl.BlockSpec(memory_space=pltpu.VMEM)
ANY = pl.BlockSpec(memory_space=pl.ANY)


def along(devices, by):
    each = CORES * PAIR
    return [(d, (d + by * each) % devices) for d in range(devices)]


def across(devices):
    return [(d, d ^ CORES) for d in range(devices)]


def swap(devices):
    return [(d, d ^ 1) for d in range(devices)]


def send(block, pairs):
    return lax.ppermute(block, "wide", pairs)


def origin(me, devices, step, other_chip, other_core):
    each = CORES * PAIR
    pair = lax.rem(me // each + devices // each - step, devices // each)
    chip = lax.rem(me // CORES, PAIR)
    core = lax.rem(me, CORES)
    if other_chip:
        chip = 1 - chip
    if other_core:
        core = 1 - core
    return pair * PAIR + chip, core


def room(mib, blocks):
    return mib * 2**20 if blocks <= SUBLANES else 24 * 2**20


def repeat(times, body, carry=None, loop=False):
    if loop or times > SUBLANES:
        return lax.fori_loop(0, times, body, carry)
    for step in range(times):
        carry = body(step, carry)
    return carry


def unfold_store(rows, slot, block):
    height = block.shape[0]
    at = pl.ds(pl.multiple_of(slot * height, SUBLANES), height)
    for tile in range(rows.shape[0]):
        rows[tile, at, :] = block[:, tile * 128 : (tile + 1) * 128].astype(jnp.float32)


def unfold_load(rows, fold, tokens):
    tiles = [rows[tile, pl.ds(fold, tokens, stride=SUBLANES), :] for tile in range(rows.shape[0])]
    return jnp.concatenate([tile.astype(jnp.bfloat16) for tile in tiles], 1)


def rotate_out_kernel(tokens, waits, z_ref, y_ref, cz_ref, cy_ref, basis_ref, *refs):
    sq_ref, rows, total = refs[waits:]
    steps, height, width = z_ref.shape
    devices = steps * CORES * PAIR
    me = lax.axis_index("wide")

    @pl.when(pl.program_id(0) == 0)
    def _():
        for ref, chip_bit, core_bit in ((z_ref, 0, 0), (y_ref, 1, 0), (cz_ref, 0, 1), (cy_ref, 1, 1)):

            def put(step, _, ref=ref, chip_bit=chip_bit, core_bit=core_bit):
                chip, core = origin(me, devices, step, chip_bit, core_bit)
                unfold_store(rows, core * (devices // CORES) + chip, ref[step])

            repeat(steps, put)
        total[...] = jnp.zeros_like(total)

    def add(fold, _):
        left = unfold_load(rows, pl.program_id(0) * FOLDS + fold, devices * tokens)
        right = basis_ref[pl.ds(pl.multiple_of(fold * width, 128), width), :]
        total[...] += jnp.dot(left, right, preferred_element_type=jnp.float32)

    repeat(FOLDS, add, None, steps > SUBLANES)

    @pl.when(pl.program_id(0) == pl.num_programs(0) - 1)
    def _():
        sq_ref[...] = (total[...] * total[...]).astype(sq_ref.dtype)


def rotate_out(tokens, z, y, cz, cy, basis, waits):
    steps, height, width = z.shape
    total = steps * CORES * PAIR * tokens
    columns = basis.shape[1]
    return pl.pallas_call(
        functools.partial(rotate_out_kernel, tokens, len(waits)),
        grid=(SUBLANES // FOLDS,),
        out_shape=jax.ShapeDtypeStruct((total, columns), jnp.bfloat16),
        in_specs=[VMEM] * 4 + [pl.BlockSpec((FOLDS * width, columns), lambda i: (i, 0))] + [ANY] * len(waits),
        out_specs=VMEM,
        scratch_shapes=[
            pltpu.VMEM((width // 128, total * SUBLANES, 128), jnp.float32),
            pltpu.VMEM((total, columns), jnp.float32),
        ],
        compiler_params=pltpu.CompilerParams(vmem_limit_bytes=room(10, steps)),
        cost_estimate=pl.CostEstimate(
            flops=2 * total * basis.shape[0] * columns, bytes_accessed=2 * basis.size, transcendentals=0
        ),
        name="rotate_out",
    )(z, y, cz, cy, basis, *waits)


def rotate_in_kernel(tokens, chunk, before, last, own_ref, across_ref, z_ref, y_ref, mine_ref, theirs_ref, *refs):
    outs, (total, rows) = refs[before:-2], refs[-2:]
    height, width = own_ref.shape
    steps = z_ref.shape[0] + 1
    devices = steps * CORES * PAIR
    chips = devices // CORES
    me = lax.axis_index("wide")

    def put(chip, block):
        unfold_store(rows, chip, block)

    @pl.when(pl.program_id(0) == 0)
    def _():
        put(origin(me, devices, 0, 0, 0)[0], own_ref[...])
        put(origin(me, devices, 0, 1, 0)[0], across_ref[chunk])
        for ref, chip_bit in ((z_ref, 0), (y_ref, 1)):

            def put_far(step, _, ref=ref, chip_bit=chip_bit):
                put(origin(me, devices, step + 1, chip_bit, 0)[0], ref[step])

            repeat(steps - 1, put_far)
        total[...] = refs[0][...] if before else jnp.zeros_like(total)

    def add(fold, _):
        at = pl.ds(pl.multiple_of(fold * width, 128), width)
        right = unfold_load(rows, pl.program_id(0) * FOLDS + fold, chips * tokens)
        left = jnp.concatenate([mine_ref[:, at], theirs_ref[:, at]])
        total[...] += lax.dot_general(left, right, (((1,), (1,)), ((), ())), preferred_element_type=jnp.float32)

    repeat(FOLDS, add, None, steps > SUBLANES)

    @pl.when(pl.program_id(0) == pl.num_programs(0) - 1)
    def _():
        if last:
            squares = (total[...] * total[...]).astype(jnp.bfloat16)
            outs[0][...] = squares[: outs[0].shape[0]]
            outs[1][...] = squares[outs[0].shape[0] :]
        else:
            outs[0][...] = total[...]


def rotate_in(tokens, chunk, own, across, z, y, mine, theirs, before):
    height, width = own.shape
    chips = (z.shape[0] + 1) * PAIR
    last = chunk == CHUNKS - 1
    basis = pl.BlockSpec((mine.shape[0], FOLDS * width), lambda i: (0, chunk * (SUBLANES // FOLDS) + i))
    whole = jax.ShapeDtypeStruct((2 * mine.shape[0], chips * tokens), jnp.float32)
    half = jax.ShapeDtypeStruct((mine.shape[0], chips * tokens), jnp.bfloat16)
    return pl.pallas_call(
        functools.partial(rotate_in_kernel, tokens, chunk, len(before), last),
        grid=(SUBLANES // FOLDS,),
        out_shape=(half, half) if last else (whole,),
        in_specs=[VMEM] * 4 + [basis] * 2 + [VMEM] * len(before),
        out_specs=(VMEM, VMEM) if last else (VMEM,),
        scratch_shapes=[
            pltpu.VMEM(whole.shape, jnp.float32),
            pltpu.VMEM((width // 128, chips * height, 128), jnp.float32),
        ],
        compiler_params=pltpu.CompilerParams(vmem_limit_bytes=room(9, chips)),
        cost_estimate=pl.CostEstimate(
            flops=4 * chips * tokens * mine.shape[0] * SUBLANES * width,
            bytes_accessed=4 * mine.shape[0] * SUBLANES * width,
            transcendentals=0,
        ),
        name="rotate_in",
    )(own, across, z, y, mine, theirs, *before)


def fold_one(from_ref, start, out_refs, rows):
    tokens = from_ref.shape[0]
    tiles = out_refs[0].shape[1] // 128
    for tile in range(tiles):
        for fold in range(SUBLANES):
            at = start + (fold * tiles + tile) * 128
            rows[tile, pl.ds(fold, tokens, stride=SUBLANES), :] = from_ref[:, at : at + 128].astype(jnp.float32)
    for tile in range(tiles):
        block = rows[tile].astype(jnp.bfloat16)
        for out_ref in out_refs:
            out_ref[:, tile * 128 : (tile + 1) * 128] = block


def fold_kernel(grads_ref, acts_ref, block_ref, *refs):
    own, every_ref, rows = refs[:-2], refs[-2], refs[-1]
    fold_one(grads_ref, 0, [block_ref], rows)
    for chunk, out_ref in enumerate(own):
        fold_one(acts_ref, chunk * SUBLANES * out_ref.shape[1], [out_ref, every_ref.at[chunk]], rows)


def folded(grads, acts):
    height = grads.shape[0] * SUBLANES
    width = acts.shape[1] // (CHUNKS * SUBLANES)
    shapes = [(height, grads.shape[1] // SUBLANES)] + [(height, width)] * CHUNKS + [(CHUNKS, height, width)]
    tiles = max(shape[-1] for shape in shapes) // 128
    return pl.pallas_call(
        fold_kernel,
        out_shape=[jax.ShapeDtypeStruct(shape, acts.dtype) for shape in shapes],
        in_specs=[VMEM] * 2,
        out_specs=[VMEM] * len(shapes),
        scratch_shapes=[pltpu.VMEM((tiles, height, 128), jnp.float32)],
        compiler_params=pltpu.CompilerParams(vmem_limit_bytes=4 * 2**20),
        cost_estimate=pl.CostEstimate(flops=0, bytes_accessed=4 * acts.size, transcendentals=0),
        name="fold",
    )(grads, acts)


def pile_kernel(blocks, *refs):
    for step in range(blocks):
        refs[-1][step] = refs[step][...]


def pile(blocks, waits):
    return pl.pallas_call(
        functools.partial(pile_kernel, len(blocks)),
        out_shape=jax.ShapeDtypeStruct((len(blocks), *blocks[0].shape), blocks[0].dtype),
        in_specs=[VMEM] * len(blocks) + [ANY] * len(waits),
        out_specs=VMEM,
        compiler_params=pltpu.CompilerParams(vmem_limit_bytes=room(3, len(blocks))),
        cost_estimate=pl.CostEstimate(flops=0, bytes_accessed=2 * len(blocks) * blocks[0].size, transcendentals=0),
        name="pile",
    )(*blocks, *waits)


def fetch_kernel(from_ref, *refs):
    to_ref, done = refs[-2:]
    copy = pltpu.make_async_copy(from_ref, to_ref, done)
    copy.start()
    copy.wait()


def fetch(array, waits):
    return pl.pallas_call(
        fetch_kernel,
        out_shape=jax.ShapeDtypeStruct(array.shape, array.dtype),
        in_specs=[ANY] * (1 + len(waits)),
        out_specs=VMEM,
        scratch_shapes=[pltpu.SemaphoreType.DMA],
        compiler_params=pltpu.CompilerParams(vmem_limit_bytes=16 * 2**20),
        cost_estimate=pl.CostEstimate(flops=0, bytes_accessed=2 * array.size, transcendentals=0),
        name="fetch",
    )(array, *waits)


def after(arrays, waits):
    return pl.pallas_call(
        lambda *refs: None,
        out_shape=[jax.ShapeDtypeStruct(array.shape, array.dtype) for array in arrays],
        in_specs=[ANY] * (len(arrays) + len(waits)),
        out_specs=[ANY] * len(arrays),
        input_output_aliases={i: i for i in range(len(arrays))},
        compiler_params=pltpu.CompilerParams(vmem_limit_bytes=2**20),
        cost_estimate=pl.CostEstimate(flops=0, bytes_accessed=0, transcendentals=0),
        name="after",
    )(*arrays, *waits)


def both_classes(own_ref, other_ref):
    own, other = own_ref[...].astype(jnp.float32), other_ref[...].astype(jnp.float32)
    first = lax.rem(lax.axis_index("wide"), CORES) == 0
    left = jnp.concatenate([jnp.where(first, own, other), jnp.where(first, other, own)], 1)
    return left.astype(jnp.bfloat16)


def eigenvalues(left, block):
    total = jnp.dot(left, block, preferred_element_type=jnp.float32)
    return (total / block.shape[0]).astype(jnp.bfloat16)


def put_all(left, out_ref, steps, pieces):
    devices = steps * CORES * PAIR
    me = lax.axis_index("wide")
    for ref, first, chip_bit, core_bit in pieces:

        def put(step, _, ref=ref, first=first, chip_bit=chip_bit, core_bit=core_bit):
            chip, core = origin(me, devices, step + first, chip_bit, core_bit)
            width = ref.shape[2]
            at = pl.multiple_of((chip * CORES + core) * width, 128)
            out_ref[:, pl.ds(at, width)] = eigenvalues(left, ref[step])

        repeat(ref.shape[0], put)


def combine_kernel(own_ref, other_ref, near_ref, swapped_ref, z_ref, y_ref, cz_ref, out_ref):
    left = both_classes(own_ref, other_ref)
    pieces = [(ref.at[bit : bit + 1], 0, bit, core) for core, ref in enumerate((near_ref, swapped_ref)) for bit in range(PAIR)]
    put_all(left, out_ref, z_ref.shape[0] + 1, pieces + [(z_ref, 1, 0, 0), (y_ref, 1, 1, 0), (cz_ref, 1, 0, 1)])


def combine(own, other, near, swapped, z, y, cz):
    blocks, total_tokens, width = z.shape
    features = (blocks + 1) * CORES * PAIR * width
    return pl.pallas_call(
        combine_kernel,
        out_shape=jax.ShapeDtypeStruct((own.shape[0], features), jnp.bfloat16),
        in_specs=[VMEM] * 7,
        out_specs=VMEM,
        compiler_params=pltpu.CompilerParams(vmem_limit_bytes=room(6, blocks)),
        cost_estimate=pl.CostEstimate(
            flops=2 * own.shape[0] * total_tokens * features, bytes_accessed=4 * own.shape[0] * features, transcendentals=0
        ),
        name="combine",
    )(own, other, near, swapped, z, y, cz)


def finish_kernel(own_ref, other_ref, cy_ref, _, out_ref, blocks, done):
    steps, _, width = cy_ref.shape
    devices = (steps + 1) * CORES * PAIR
    me = lax.axis_index("wide")
    left = both_classes(own_ref, other_ref)
    copies = []
    for step in range(steps):
        chip, core = origin(me, devices, step + 1, 1, 1)
        at = pl.multiple_of((chip * CORES + core) * width, 128)
        blocks[step] = eigenvalues(left, cy_ref[step])
        copies.append(pltpu.make_async_copy(blocks.at[step], out_ref.at[:, pl.ds(at, width)], done.at[step]))
        copies[-1].start()
    for copy in copies:
        copy.wait()


def finish(own, other, cy, result):
    steps, total_tokens, width = cy.shape
    return pl.pallas_call(
        finish_kernel,
        out_shape=jax.ShapeDtypeStruct(result.shape, result.dtype),
        in_specs=[VMEM] * 3 + [ANY],
        out_specs=ANY,
        scratch_shapes=[
            pltpu.VMEM((steps, own.shape[0], width), result.dtype),
            pltpu.SemaphoreType.DMA((steps,)),
        ],
        input_output_aliases={3: 0},
        compiler_params=pltpu.CompilerParams(vmem_limit_bytes=room(4, steps)),
        cost_estimate=pl.CostEstimate(
            flops=2 * own.shape[0] * total_tokens * steps * width, bytes_accessed=4 * cy.size, transcendentals=0
        ),
        name="finish",
    )(own, other, cy, result)


def local(acts, grads, basis_in, basis_out):
    devices = lax.axis_size("wide")
    steps = devices // (CORES * PAIR)
    tokens = acts.shape[0]

    def along_all(block):
        return [send(block, along(devices, step)) for step in range(1, steps)]

    def others(z):
        y = send(z, across(devices))
        return z, y, send(z, swap(devices)), send(y, swap(devices))

    block, *own, every = folded(grads, acts)
    fetched = fetch(basis_out, [block])
    mine = basis_in.T
    theirs = send(mine, swap(devices))
    own_across = send(every, across(devices))
    grads_z = pile([block] + along_all(block), [own_across, fetched, theirs])
    grads_y = send(grads_z, across(devices))

    acts_z, acts_y = [], []

    def chunk_along(chunk, waits):
        acts_z.append(pile(along_all(own[chunk]), waits))
        acts_y.append(send(acts_z[-1], across(devices)))

    def part(chunk, before):
        return rotate_in(tokens, chunk, own[chunk], own_across, acts_z[chunk], acts_y[chunk], mine, theirs, before)

    chunk_along(0, [])
    [grads_y] = after([grads_y], [acts_z[0]])
    grads_cz, grads_cy = send(grads_z, swap(devices)), send(grads_y, swap(devices))
    sq_out = rotate_out(tokens, grads_z, grads_y, grads_cz, grads_cy, fetched, [acts_z[0]])
    near = pile([sq_out, send(sq_out, across(devices))], [])
    swapped = send(near, swap(devices))
    came = along_all(sq_out)
    for chunk in range(1, CHUNKS):
        chunk_along(chunk, [sq_out])
    total = part(0, [])
    z = pile(came, [*total, acts_z[-1], near])
    y = send(z, across(devices))
    for chunk in range(1, CHUNKS):
        total = part(chunk, total)
    sq_in, given = total
    other = send(given, swap(devices))
    [y] = after([y], [other, swapped])
    cz, cy = send(z, swap(devices)), send(y, swap(devices))
    return finish(sq_in, other, cy, combine(sq_in, other, near, swapped, z, y, cz))


def solution(mesh):
    return jax.shard_map(
        local,
        mesh=mesh,
        in_specs=(
            P(("groups", "wide"), None),
            P(("groups", "wide"), None),
            P("groups", "wide"),
            P("groups", "wide"),
        ),
        out_specs=P(("groups", "wide"), None),
        check_vma=False,
    )
```

```python
import functools

import jax
import jax.numpy as jnp
from jax import lax
from jax.experimental import pallas as pl
from jax.experimental.pallas import tpu as pltpu
from jax.sharding import PartitionSpec as P

CORES = 2
PAIR = 2
SUBLANES = 8
FOLDS = 2
CHUNKS = 2
VMEM = pl.BlockSpec(memory_space=pltpu.VMEM)
ANY = pl.BlockSpec(memory_space=pl.ANY)


def along(devices, by):
    each = CORES * PAIR
    return [(d, (d + by * each) % devices) for d in range(devices)]


def across(devices):
    return [(d, d ^ CORES) for d in range(devices)]


def swap(devices):
    return [(d, d ^ 1) for d in range(devices)]


def send(block, pairs):
    return lax.ppermute(block, "wide", pairs)


def origin(me, devices, step, other_chip, other_core):
    each = CORES * PAIR
    pair = lax.rem(me // each + devices // each - step, devices // each)
    chip = lax.rem(me // CORES, PAIR)
    core = lax.rem(me, CORES)
    if other_chip:
        chip = 1 - chip
    if other_core:
        core = 1 - core
    return pair * PAIR + chip, core


def room(mib, blocks):
    return mib * 2**20 if blocks <= SUBLANES else 24 * 2**20


def repeat(times, body, carry=None, loop=False):
    if loop or times > SUBLANES:
        return lax.fori_loop(0, times, body, carry)
    for step in range(times):
        carry = body(step, carry)
    return carry


def unfold_store(rows, slot, block):
    height = block.shape[0]
    at = pl.ds(pl.multiple_of(slot * height, SUBLANES), height)
    for tile in range(rows.shape[0]):
        rows[tile, at, :] = block[:, tile * 128 : (tile + 1) * 128].astype(jnp.float32)


def unfold_load(rows, fold, tokens):
    tiles = [rows[tile, pl.ds(fold, tokens, stride=SUBLANES), :] for tile in range(rows.shape[0])]
    return jnp.concatenate([tile.astype(jnp.bfloat16) for tile in tiles], 1)


def rotate_out_kernel(tokens, waits, z_ref, y_ref, cz_ref, cy_ref, basis_ref, *refs):
    sq_ref, rows, total = refs[waits:]
    steps, height, width = z_ref.shape
    devices = steps * CORES * PAIR
    me = lax.axis_index("wide")

    @pl.when(pl.program_id(0) == 0)
    def _():
        for ref, chip_bit, core_bit in ((z_ref, 0, 0), (y_ref, 1, 0), (cz_ref, 0, 1), (cy_ref, 1, 1)):

            def put(step, _, ref=ref, chip_bit=chip_bit, core_bit=core_bit):
                chip, core = origin(me, devices, step, chip_bit, core_bit)
                unfold_store(rows, core * (devices // CORES) + chip, ref[step])

            repeat(steps, put)
        total[...] = jnp.zeros_like(total)

    def add(fold, _):
        left = unfold_load(rows, pl.program_id(0) * FOLDS + fold, devices * tokens)
        right = basis_ref[pl.ds(pl.multiple_of(fold * width, 128), width), :]
        total[...] += jnp.dot(left, right, preferred_element_type=jnp.float32)

    repeat(FOLDS, add, None, steps > SUBLANES)

    @pl.when(pl.program_id(0) == pl.num_programs(0) - 1)
    def _():
        sq_ref[...] = (total[...] * total[...]).astype(sq_ref.dtype)


def rotate_out(tokens, z, y, cz, cy, basis, waits):
    steps, height, width = z.shape
    total = steps * CORES * PAIR * tokens
    columns = basis.shape[1]
    return pl.pallas_call(
        functools.partial(rotate_out_kernel, tokens, len(waits)),
        grid=(SUBLANES // FOLDS,),
        out_shape=jax.ShapeDtypeStruct((total, columns), jnp.bfloat16),
        in_specs=[VMEM] * 4 + [pl.BlockSpec((FOLDS * width, columns), lambda i: (i, 0))] + [ANY] * len(waits),
        out_specs=VMEM,
        scratch_shapes=[
            pltpu.VMEM((width // 128, total * SUBLANES, 128), jnp.float32),
            pltpu.VMEM((total, columns), jnp.float32),
        ],
        compiler_params=pltpu.CompilerParams(vmem_limit_bytes=room(10, steps)),
        cost_estimate=pl.CostEstimate(
            flops=2 * total * basis.shape[0] * columns, bytes_accessed=2 * basis.size, transcendentals=0
        ),
        name="rotate_out",
    )(z, y, cz, cy, basis, *waits)


def rotate_in_kernel(tokens, chunk, before, last, own_ref, across_ref, z_ref, y_ref, mine_ref, theirs_ref, *refs):
    outs, (total, rows) = refs[before:-2], refs[-2:]
    height, width = own_ref.shape
    steps = z_ref.shape[0] + 1
    devices = steps * CORES * PAIR
    chips = devices // CORES
    me = lax.axis_index("wide")

    def put(chip, block):
        unfold_store(rows, chip, block)

    @pl.when(pl.program_id(0) == 0)
    def _():
        put(origin(me, devices, 0, 0, 0)[0], own_ref[...])
        put(origin(me, devices, 0, 1, 0)[0], across_ref[chunk])
        for ref, chip_bit in ((z_ref, 0), (y_ref, 1)):

            def put_far(step, _, ref=ref, chip_bit=chip_bit):
                put(origin(me, devices, step + 1, chip_bit, 0)[0], ref[step])

            repeat(steps - 1, put_far)
        total[...] = refs[0][...] if before else jnp.zeros_like(total)

    def add(fold, _):
        at = pl.ds(pl.multiple_of(fold * width, 128), width)
        right = unfold_load(rows, pl.program_id(0) * FOLDS + fold, chips * tokens)
        left = jnp.concatenate([mine_ref[:, at], theirs_ref[:, at]])
        total[...] += lax.dot_general(left, right, (((1,), (1,)), ((), ())), preferred_element_type=jnp.float32)

    repeat(FOLDS, add, None, steps > SUBLANES)

    @pl.when(pl.program_id(0) == pl.num_programs(0) - 1)
    def _():
        if last:
            squares = (total[...] * total[...]).astype(jnp.bfloat16)
            outs[0][...] = squares[: outs[0].shape[0]]
            outs[1][...] = squares[outs[0].shape[0] :]
        else:
            outs[0][...] = total[...]


def rotate_in(tokens, chunk, own, across, z, y, mine, theirs, before):
    height, width = own.shape
    chips = (z.shape[0] + 1) * PAIR
    last = chunk == CHUNKS - 1
    basis = pl.BlockSpec((mine.shape[0], FOLDS * width), lambda i: (0, chunk * (SUBLANES // FOLDS) + i))
    whole = jax.ShapeDtypeStruct((2 * mine.shape[0], chips * tokens), jnp.float32)
    half = jax.ShapeDtypeStruct((mine.shape[0], chips * tokens), jnp.bfloat16)
    return pl.pallas_call(
        functools.partial(rotate_in_kernel, tokens, chunk, len(before), last),
        grid=(SUBLANES // FOLDS,),
        out_shape=(half, half) if last else (whole,),
        in_specs=[VMEM] * 4 + [basis] * 2 + [VMEM] * len(before),
        out_specs=(VMEM, VMEM) if last else (VMEM,),
        scratch_shapes=[
            pltpu.VMEM(whole.shape, jnp.float32),
            pltpu.VMEM((width // 128, chips * height, 128), jnp.float32),
        ],
        compiler_params=pltpu.CompilerParams(vmem_limit_bytes=room(9, chips)),
        cost_estimate=pl.CostEstimate(
            flops=4 * chips * tokens * mine.shape[0] * SUBLANES * width,
            bytes_accessed=4 * mine.shape[0] * SUBLANES * width,
            transcendentals=0,
        ),
        name="rotate_in",
    )(own, across, z, y, mine, theirs, *before)


def fold_one(from_ref, start, out_refs, rows):
    tokens = from_ref.shape[0]
    tiles = out_refs[0].shape[1] // 128
    for tile in range(tiles):
        for fold in range(SUBLANES):
            at = start + (fold * tiles + tile) * 128
            rows[tile, pl.ds(fold, tokens, stride=SUBLANES), :] = from_ref[:, at : at + 128].astype(jnp.float32)
    for tile in range(tiles):
        block = rows[tile].astype(jnp.bfloat16)
        for out_ref in out_refs:
            out_ref[:, tile * 128 : (tile + 1) * 128] = block


def fold_kernel(waits, chunks, from_ref, *refs):
    outs, rows = refs[waits:-1], refs[-1]
    for chunk in range(chunks):
        width = outs[chunk].shape[1]
        also = [outs[chunks].at[chunk]] if chunks > 1 else []
        fold_one(from_ref, chunk * SUBLANES * width, [outs[chunk], *also], rows)


def folded(array, chunks, waits):
    shape = (array.shape[0] * SUBLANES, array.shape[1] // (chunks * SUBLANES))
    shapes = [shape] * chunks + ([(chunks, *shape)] if chunks > 1 else [])
    return pl.pallas_call(
        functools.partial(fold_kernel, len(waits), chunks),
        out_shape=[jax.ShapeDtypeStruct(shape, array.dtype) for shape in shapes],
        in_specs=[VMEM] + [ANY] * len(waits),
        out_specs=[VMEM] * len(shapes),
        scratch_shapes=[pltpu.VMEM((shape[1] // 128, shape[0], 128), jnp.float32)],
        compiler_params=pltpu.CompilerParams(vmem_limit_bytes=4 * 2**20),
        cost_estimate=pl.CostEstimate(flops=0, bytes_accessed=4 * array.size, transcendentals=0),
        name="fold",
    )(array, *waits)


def pile_kernel(blocks, *refs):
    for step in range(blocks):
        refs[-1][step] = refs[step][...]


def pile(blocks, waits):
    return pl.pallas_call(
        functools.partial(pile_kernel, len(blocks)),
        out_shape=jax.ShapeDtypeStruct((len(blocks), *blocks[0].shape), blocks[0].dtype),
        in_specs=[VMEM] * len(blocks) + [ANY] * len(waits),
        out_specs=VMEM,
        compiler_params=pltpu.CompilerParams(vmem_limit_bytes=room(3, len(blocks))),
        cost_estimate=pl.CostEstimate(flops=0, bytes_accessed=2 * len(blocks) * blocks[0].size, transcendentals=0),
        name="pile",
    )(*blocks, *waits)


def fetch_kernel(from_ref, *refs):
    to_ref, done = refs[-2:]
    copy = pltpu.make_async_copy(from_ref, to_ref, done)
    copy.start()
    copy.wait()


def fetch(array, waits):
    return pl.pallas_call(
        fetch_kernel,
        out_shape=jax.ShapeDtypeStruct(array.shape, array.dtype),
        in_specs=[ANY] * (1 + len(waits)),
        out_specs=VMEM,
        scratch_shapes=[pltpu.SemaphoreType.DMA],
        compiler_params=pltpu.CompilerParams(vmem_limit_bytes=16 * 2**20),
        cost_estimate=pl.CostEstimate(flops=0, bytes_accessed=2 * array.size, transcendentals=0),
        name="fetch",
    )(array, *waits)


def after(arrays, waits):
    return pl.pallas_call(
        lambda *refs: None,
        out_shape=[jax.ShapeDtypeStruct(array.shape, array.dtype) for array in arrays],
        in_specs=[ANY] * (len(arrays) + len(waits)),
        out_specs=[ANY] * len(arrays),
        input_output_aliases={i: i for i in range(len(arrays))},
        compiler_params=pltpu.CompilerParams(vmem_limit_bytes=2**20),
        cost_estimate=pl.CostEstimate(flops=0, bytes_accessed=0, transcendentals=0),
        name="after",
    )(*arrays, *waits)


def both_classes(own_ref, other_ref):
    own, other = own_ref[...].astype(jnp.float32), other_ref[...].astype(jnp.float32)
    first = lax.rem(lax.axis_index("wide"), CORES) == 0
    left = jnp.concatenate([jnp.where(first, own, other), jnp.where(first, other, own)], 1)
    return left.astype(jnp.bfloat16)


def eigenvalues(left, block):
    total = jnp.dot(left, block, preferred_element_type=jnp.float32)
    return (total / block.shape[0]).astype(jnp.bfloat16)


def combine_kernel(own_ref, other_ref, z_ref, y_ref, cz_ref, out_ref):
    steps, _, width = z_ref.shape
    devices = steps * CORES * PAIR
    me = lax.axis_index("wide")
    left = both_classes(own_ref, other_ref)
    for ref, chip_bit, core_bit in ((z_ref, 0, 0), (y_ref, 1, 0), (cz_ref, 0, 1)):

        def put(step, _, ref=ref, chip_bit=chip_bit, core_bit=core_bit):
            chip, core = origin(me, devices, step, chip_bit, core_bit)
            at = pl.multiple_of((chip * CORES + core) * width, 128)
            out_ref[:, pl.ds(at, width)] = eigenvalues(left, ref[step])

        repeat(steps, put)


def combine(own, other, z, y, cz):
    steps, total_tokens, width = z.shape
    features = steps * CORES * PAIR * width
    return pl.pallas_call(
        combine_kernel,
        out_shape=jax.ShapeDtypeStruct((own.shape[0], features), jnp.bfloat16),
        in_specs=[VMEM] * 5,
        out_specs=VMEM,
        compiler_params=pltpu.CompilerParams(vmem_limit_bytes=room(6, steps)),
        cost_estimate=pl.CostEstimate(
            flops=2 * own.shape[0] * total_tokens * features, bytes_accessed=4 * own.shape[0] * features, transcendentals=0
        ),
        name="combine",
    )(own, other, z, y, cz)


def finish_kernel(own_ref, other_ref, cy_ref, _, out_ref, blocks, done):
    steps, _, width = cy_ref.shape
    devices = steps * CORES * PAIR
    me = lax.axis_index("wide")
    left = both_classes(own_ref, other_ref)
    copies = []
    for step in range(steps):
        chip, core = origin(me, devices, step, 1, 1)
        at = pl.multiple_of((chip * CORES + core) * width, 128)
        blocks[step] = eigenvalues(left, cy_ref[step])
        copies.append(pltpu.make_async_copy(blocks.at[step], out_ref.at[:, pl.ds(at, width)], done.at[step]))
        copies[-1].start()
    for copy in copies:
        copy.wait()


def finish(own, other, cy, result):
    steps, total_tokens, width = cy.shape
    return pl.pallas_call(
        finish_kernel,
        out_shape=jax.ShapeDtypeStruct(result.shape, result.dtype),
        in_specs=[VMEM] * 3 + [ANY],
        out_specs=ANY,
        scratch_shapes=[
            pltpu.VMEM((steps, own.shape[0], width), result.dtype),
            pltpu.SemaphoreType.DMA((steps,)),
        ],
        input_output_aliases={3: 0},
        compiler_params=pltpu.CompilerParams(vmem_limit_bytes=room(4, steps)),
        cost_estimate=pl.CostEstimate(
            flops=2 * own.shape[0] * total_tokens * steps * width, bytes_accessed=4 * cy.size, transcendentals=0
        ),
        name="finish",
    )(own, other, cy, result)


def local(acts, grads, basis_in, basis_out):
    devices = lax.axis_size("wide")
    steps = devices // (CORES * PAIR)
    tokens = acts.shape[0]

    def along_all(block):
        return [send(block, along(devices, step)) for step in range(1, steps)]

    def others(z):
        y = send(z, across(devices))
        return z, y, send(z, swap(devices)), send(y, swap(devices))

    [block] = folded(grads, 1, [])
    *own, every = folded(acts, CHUNKS, [block])
    fetched = fetch(basis_out, [block])
    mine = basis_in.T
    theirs = send(mine, swap(devices))
    own_across = send(every, across(devices))
    grads_all = others(pile([block] + along_all(block), [fetched, theirs, every]))

    acts_z, acts_y = [], []

    def chunk_along(chunk, waits):
        acts_z.append(pile(along_all(own[chunk]), waits))
        acts_y.append(send(acts_z[-1], across(devices)))

    def part(chunk, before):
        return rotate_in(tokens, chunk, own[chunk], own_across, acts_z[chunk], acts_y[chunk], mine, theirs, before)

    chunk_along(0, [])
    sq_out = rotate_out(tokens, *grads_all, fetched, [acts_z[0], own_across])
    came = along_all(sq_out)
    for chunk in range(1, CHUNKS):
        chunk_along(chunk, [sq_out])
    total = part(0, [])
    z = pile([sq_out] + came, [*total, acts_z[-1]])
    y = send(z, across(devices))
    for chunk in range(1, CHUNKS):
        total = part(chunk, total)
    sq_in, given = total
    other = send(given, swap(devices))
    [y] = after([y], [other])
    cz, cy = send(z, swap(devices)), send(y, swap(devices))
    return finish(sq_in, other, cy, combine(sq_in, other, z, y, cz))


def solution(mesh):
    return jax.shard_map(
        local,
        mesh=mesh,
        in_specs=(
            P(("groups", "wide"), None),
            P(("groups", "wide"), None),
            P("groups", "wide"),
            P("groups", "wide"),
        ),
        out_specs=P(("groups", "wide"), None),
        check_vma=False,
    )
```

```python
import functools

import jax
import jax.numpy as jnp
from jax import lax
from jax.experimental import pallas as pl
from jax.experimental.pallas import tpu as pltpu
from jax.sharding import PartitionSpec as P

CORES = 2
PAIR = 2
SUBLANES = 8
FOLDS = 2
CHUNKS = 2
VMEM = pl.BlockSpec(memory_space=pltpu.VMEM)
ANY = pl.BlockSpec(memory_space=pl.ANY)


def along(devices, by):
    each = CORES * PAIR
    return [(d, (d + by * each) % devices) for d in range(devices)]


def across(devices):
    return [(d, d ^ CORES) for d in range(devices)]


def swap(devices):
    return [(d, d ^ 1) for d in range(devices)]


def send(block, pairs):
    return lax.ppermute(block, "wide", pairs)


def origin(me, devices, step, other_chip, other_core):
    each = CORES * PAIR
    pair = lax.rem(me // each + devices // each - step, devices // each)
    chip = lax.rem(me // CORES, PAIR)
    core = lax.rem(me, CORES)
    if other_chip:
        chip = 1 - chip
    if other_core:
        core = 1 - core
    return pair * PAIR + chip, core


def room(mib, blocks):
    return mib * 2**20 if blocks <= SUBLANES else 24 * 2**20


def repeat(times, body, carry=None, loop=False):
    if loop or times > SUBLANES:
        return lax.fori_loop(0, times, body, carry)
    for step in range(times):
        carry = body(step, carry)
    return carry


def unfold_store(rows, slot, block):
    height = block.shape[0]
    at = pl.ds(pl.multiple_of(slot * height, SUBLANES), height)
    for tile in range(rows.shape[0]):
        rows[tile, at, :] = block[:, tile * 128 : (tile + 1) * 128].astype(jnp.float32)


def unfold_load(rows, fold, tokens):
    tiles = [rows[tile, pl.ds(fold, tokens, stride=SUBLANES), :] for tile in range(rows.shape[0])]
    return jnp.concatenate([tile.astype(jnp.bfloat16) for tile in tiles], 1)


def rotate_out_kernel(tokens, waits, z_ref, y_ref, cz_ref, cy_ref, basis_ref, *refs):
    sq_ref, rows, total = refs[waits:]
    steps, height, width = z_ref.shape
    devices = steps * CORES * PAIR
    me = lax.axis_index("wide")

    @pl.when(pl.program_id(0) == 0)
    def _():
        for ref, chip_bit, core_bit in ((z_ref, 0, 0), (y_ref, 1, 0), (cz_ref, 0, 1), (cy_ref, 1, 1)):

            def put(step, _, ref=ref, chip_bit=chip_bit, core_bit=core_bit):
                chip, core = origin(me, devices, step, chip_bit, core_bit)
                unfold_store(rows, core * (devices // CORES) + chip, ref[step])

            repeat(steps, put)
        total[...] = jnp.zeros_like(total)

    def add(fold, _):
        left = unfold_load(rows, pl.program_id(0) * FOLDS + fold, devices * tokens)
        right = basis_ref[pl.ds(pl.multiple_of(fold * width, 128), width), :]
        total[...] += jnp.dot(left, right, preferred_element_type=jnp.float32)

    repeat(FOLDS, add, None, steps > SUBLANES)

    @pl.when(pl.program_id(0) == pl.num_programs(0) - 1)
    def _():
        sq_ref[...] = (total[...] * total[...]).astype(sq_ref.dtype)


def rotate_out(tokens, z, y, cz, cy, basis, waits):
    steps, height, width = z.shape
    total = steps * CORES * PAIR * tokens
    columns = basis.shape[1]
    return pl.pallas_call(
        functools.partial(rotate_out_kernel, tokens, len(waits)),
        grid=(SUBLANES // FOLDS,),
        out_shape=jax.ShapeDtypeStruct((total, columns), jnp.bfloat16),
        in_specs=[VMEM] * 4 + [pl.BlockSpec((FOLDS * width, columns), lambda i: (i, 0))] + [ANY] * len(waits),
        out_specs=VMEM,
        scratch_shapes=[
            pltpu.VMEM((width // 128, total * SUBLANES, 128), jnp.float32),
            pltpu.VMEM((total, columns), jnp.float32),
        ],
        compiler_params=pltpu.CompilerParams(vmem_limit_bytes=room(10, steps)),
        cost_estimate=pl.CostEstimate(
            flops=2 * total * basis.shape[0] * columns, bytes_accessed=2 * basis.size, transcendentals=0
        ),
        name="rotate_out",
    )(z, y, cz, cy, basis, *waits)


def rotate_in_kernel(tokens, chunk, before, last, own_ref, across_ref, z_ref, y_ref, mine_ref, theirs_ref, *refs):
    outs, (total, rows) = refs[before:-2], refs[-2:]
    height, width = own_ref.shape
    steps = z_ref.shape[0] + 1
    devices = steps * CORES * PAIR
    chips = devices // CORES
    me = lax.axis_index("wide")

    def put(chip, block):
        unfold_store(rows, chip, block)

    @pl.when(pl.program_id(0) == 0)
    def _():
        put(origin(me, devices, 0, 0, 0)[0], own_ref[...])
        put(origin(me, devices, 0, 1, 0)[0], across_ref[chunk])
        for ref, chip_bit in ((z_ref, 0), (y_ref, 1)):

            def put_far(step, _, ref=ref, chip_bit=chip_bit):
                put(origin(me, devices, step + 1, chip_bit, 0)[0], ref[step])

            repeat(steps - 1, put_far)
        total[...] = refs[0][...] if before else jnp.zeros_like(total)

    def add(fold, _):
        at = pl.ds(pl.multiple_of(fold * width, 128), width)
        right = unfold_load(rows, pl.program_id(0) * FOLDS + fold, chips * tokens)
        left = jnp.concatenate([mine_ref[:, at], theirs_ref[:, at]])
        total[...] += lax.dot_general(left, right, (((1,), (1,)), ((), ())), preferred_element_type=jnp.float32)

    repeat(FOLDS, add, None, steps > SUBLANES)

    @pl.when(pl.program_id(0) == pl.num_programs(0) - 1)
    def _():
        if last:
            squares = (total[...] * total[...]).astype(jnp.bfloat16)
            outs[0][...] = squares[: outs[0].shape[0]]
            outs[1][...] = squares[outs[0].shape[0] :]
        else:
            outs[0][...] = total[...]


def rotate_in(tokens, chunk, own, across, z, y, mine, theirs, before):
    height, width = own.shape
    chips = (z.shape[0] + 1) * PAIR
    last = chunk == CHUNKS - 1
    basis = pl.BlockSpec((mine.shape[0], FOLDS * width), lambda i: (0, chunk * (SUBLANES // FOLDS) + i))
    whole = jax.ShapeDtypeStruct((2 * mine.shape[0], chips * tokens), jnp.float32)
    half = jax.ShapeDtypeStruct((mine.shape[0], chips * tokens), jnp.bfloat16)
    return pl.pallas_call(
        functools.partial(rotate_in_kernel, tokens, chunk, len(before), last),
        grid=(SUBLANES // FOLDS,),
        out_shape=(half, half) if last else (whole,),
        in_specs=[VMEM] * 4 + [basis] * 2 + [VMEM] * len(before),
        out_specs=(VMEM, VMEM) if last else (VMEM,),
        scratch_shapes=[
            pltpu.VMEM(whole.shape, jnp.float32),
            pltpu.VMEM((width // 128, chips * height, 128), jnp.float32),
        ],
        compiler_params=pltpu.CompilerParams(vmem_limit_bytes=room(9, chips)),
        cost_estimate=pl.CostEstimate(
            flops=4 * chips * tokens * mine.shape[0] * SUBLANES * width,
            bytes_accessed=4 * mine.shape[0] * SUBLANES * width,
            transcendentals=0,
        ),
        name="rotate_in",
    )(own, across, z, y, mine, theirs, *before)


def fold_one(from_ref, start, out_refs, rows):
    tokens = from_ref.shape[0]
    tiles = out_refs[0].shape[1] // 128
    for tile in range(tiles):
        for fold in range(SUBLANES):
            at = start + (fold * tiles + tile) * 128
            rows[tile, pl.ds(fold, tokens, stride=SUBLANES), :] = from_ref[:, at : at + 128].astype(jnp.float32)
    for tile in range(tiles):
        block = rows[tile].astype(jnp.bfloat16)
        for out_ref in out_refs:
            out_ref[:, tile * 128 : (tile + 1) * 128] = block


def fold_kernel(waits, chunks, from_ref, *refs):
    outs, rows = refs[waits:-1], refs[-1]
    for chunk in range(chunks):
        width = outs[chunk].shape[1]
        also = [outs[chunks].at[chunk]] if chunks > 1 else []
        fold_one(from_ref, chunk * SUBLANES * width, [outs[chunk], *also], rows)


def folded(array, chunks, waits):
    shape = (array.shape[0] * SUBLANES, array.shape[1] // (chunks * SUBLANES))
    shapes = [shape] * chunks + ([(chunks, *shape)] if chunks > 1 else [])
    return pl.pallas_call(
        functools.partial(fold_kernel, len(waits), chunks),
        out_shape=[jax.ShapeDtypeStruct(shape, array.dtype) for shape in shapes],
        in_specs=[VMEM] + [ANY] * len(waits),
        out_specs=[VMEM] * len(shapes),
        scratch_shapes=[pltpu.VMEM((shape[1] // 128, shape[0], 128), jnp.float32)],
        compiler_params=pltpu.CompilerParams(vmem_limit_bytes=4 * 2**20),
        cost_estimate=pl.CostEstimate(flops=0, bytes_accessed=4 * array.size, transcendentals=0),
        name="fold",
    )(array, *waits)


def pile_kernel(blocks, *refs):
    for step in range(blocks):
        refs[-1][step] = refs[step][...]


def pile(blocks, waits):
    return pl.pallas_call(
        functools.partial(pile_kernel, len(blocks)),
        out_shape=jax.ShapeDtypeStruct((len(blocks), *blocks[0].shape), blocks[0].dtype),
        in_specs=[VMEM] * len(blocks) + [ANY] * len(waits),
        out_specs=VMEM,
        compiler_params=pltpu.CompilerParams(vmem_limit_bytes=room(3, len(blocks))),
        cost_estimate=pl.CostEstimate(flops=0, bytes_accessed=2 * len(blocks) * blocks[0].size, transcendentals=0),
        name="pile",
    )(*blocks, *waits)


def fetch_kernel(from_ref, *refs):
    to_ref, done = refs[-2:]
    copy = pltpu.make_async_copy(from_ref, to_ref, done)
    copy.start()
    copy.wait()


def fetch(array, waits):
    return pl.pallas_call(
        fetch_kernel,
        out_shape=jax.ShapeDtypeStruct(array.shape, array.dtype),
        in_specs=[ANY] * (1 + len(waits)),
        out_specs=VMEM,
        scratch_shapes=[pltpu.SemaphoreType.DMA],
        compiler_params=pltpu.CompilerParams(vmem_limit_bytes=16 * 2**20),
        cost_estimate=pl.CostEstimate(flops=0, bytes_accessed=2 * array.size, transcendentals=0),
        name="fetch",
    )(array, *waits)


def after(arrays, waits):
    return pl.pallas_call(
        lambda *refs: None,
        out_shape=[jax.ShapeDtypeStruct(array.shape, array.dtype) for array in arrays],
        in_specs=[ANY] * (len(arrays) + len(waits)),
        out_specs=[ANY] * len(arrays),
        input_output_aliases={i: i for i in range(len(arrays))},
        compiler_params=pltpu.CompilerParams(vmem_limit_bytes=2**20),
        cost_estimate=pl.CostEstimate(flops=0, bytes_accessed=0, transcendentals=0),
        name="after",
    )(*arrays, *waits)


def both_classes(own_ref, other_ref):
    own, other = own_ref[...].astype(jnp.float32), other_ref[...].astype(jnp.float32)
    first = lax.rem(lax.axis_index("wide"), CORES) == 0
    left = jnp.concatenate([jnp.where(first, own, other), jnp.where(first, other, own)], 1)
    return left.astype(jnp.bfloat16)


def eigenvalues(left, block):
    total = jnp.dot(left, block, preferred_element_type=jnp.float32)
    return (total / block.shape[0]).astype(jnp.bfloat16)


def combine_kernel(own_ref, other_ref, z_ref, y_ref, cz_ref, out_ref):
    steps, _, width = z_ref.shape
    devices = steps * CORES * PAIR
    me = lax.axis_index("wide")
    left = both_classes(own_ref, other_ref)
    for ref, chip_bit, core_bit in ((z_ref, 0, 0), (y_ref, 1, 0), (cz_ref, 0, 1)):

        def put(step, _, ref=ref, chip_bit=chip_bit, core_bit=core_bit):
            chip, core = origin(me, devices, step, chip_bit, core_bit)
            at = pl.multiple_of((chip * CORES + core) * width, 128)
            out_ref[:, pl.ds(at, width)] = eigenvalues(left, ref[step])

        repeat(steps, put)


def combine(own, other, z, y, cz):
    steps, total_tokens, width = z.shape
    features = steps * CORES * PAIR * width
    return pl.pallas_call(
        combine_kernel,
        out_shape=jax.ShapeDtypeStruct((own.shape[0], features), jnp.bfloat16),
        in_specs=[VMEM] * 5,
        out_specs=VMEM,
        compiler_params=pltpu.CompilerParams(vmem_limit_bytes=room(6, steps)),
        cost_estimate=pl.CostEstimate(
            flops=2 * own.shape[0] * total_tokens * features, bytes_accessed=4 * own.shape[0] * features, transcendentals=0
        ),
        name="combine",
    )(own, other, z, y, cz)


def finish_kernel(own_ref, other_ref, cy_ref, _, out_ref, blocks, done):
    steps, _, width = cy_ref.shape
    devices = steps * CORES * PAIR
    me = lax.axis_index("wide")
    left = both_classes(own_ref, other_ref)
    copies = []
    for step in range(steps):
        chip, core = origin(me, devices, step, 1, 1)
        at = pl.multiple_of((chip * CORES + core) * width, 128)
        blocks[step] = eigenvalues(left, cy_ref[step])
        copies.append(pltpu.make_async_copy(blocks.at[step], out_ref.at[:, pl.ds(at, width)], done.at[step]))
        copies[-1].start()
    for copy in copies:
        copy.wait()


def finish(own, other, cy, result):
    steps, total_tokens, width = cy.shape
    return pl.pallas_call(
        finish_kernel,
        out_shape=jax.ShapeDtypeStruct(result.shape, result.dtype),
        in_specs=[VMEM] * 3 + [ANY],
        out_specs=ANY,
        scratch_shapes=[
            pltpu.VMEM((steps, own.shape[0], width), result.dtype),
            pltpu.SemaphoreType.DMA((steps,)),
        ],
        input_output_aliases={3: 0},
        compiler_params=pltpu.CompilerParams(vmem_limit_bytes=room(4, steps)),
        cost_estimate=pl.CostEstimate(
            flops=2 * own.shape[0] * total_tokens * steps * width, bytes_accessed=4 * cy.size, transcendentals=0
        ),
        name="finish",
    )(own, other, cy, result)


def local(acts, grads, basis_in, basis_out):
    devices = lax.axis_size("wide")
    steps = devices // (CORES * PAIR)
    tokens = acts.shape[0]

    def along_all(block):
        return [send(block, along(devices, step)) for step in range(1, steps)]

    def others(z):
        y = send(z, across(devices))
        return z, y, send(z, swap(devices)), send(y, swap(devices))

    [block] = folded(grads, 1, [])
    *own, every = folded(acts, CHUNKS, [block])
    mine = basis_in.T
    theirs = send(mine, swap(devices))
    own_across = send(every, across(devices))
    grads_all = others(pile([block] + along_all(block), [theirs, every]))

    acts_z, acts_y = [], []

    def chunk_along(chunk, waits):
        acts_z.append(pile(along_all(own[chunk]), waits))
        acts_y.append(send(acts_z[-1], across(devices)))

    def part(chunk, before):
        return rotate_in(tokens, chunk, own[chunk], own_across, acts_z[chunk], acts_y[chunk], mine, theirs, before)

    fetched = fetch(basis_out, [grads_all[0]])
    chunk_along(0, [fetched])
    sq_out = rotate_out(tokens, *grads_all, fetched, [acts_z[0], own_across])
    came = along_all(sq_out)
    for chunk in range(1, CHUNKS):
        chunk_along(chunk, [sq_out])
    total = part(0, [])
    z = pile([sq_out] + came, [*total, acts_z[-1]])
    y = send(z, across(devices))
    for chunk in range(1, CHUNKS):
        total = part(chunk, total)
    sq_in, given = total
    other = send(given, swap(devices))
    [y] = after([y], [other])
    cz, cy = send(z, swap(devices)), send(y, swap(devices))
    return finish(sq_in, other, cy, combine(sq_in, other, z, y, cz))


def solution(mesh):
    return jax.shard_map(
        local,
        mesh=mesh,
        in_specs=(
            P(("groups", "wide"), None),
            P(("groups", "wide"), None),
            P("groups", "wide"),
            P("groups", "wide"),
        ),
        out_specs=P(("groups", "wide"), None),
        check_vma=False,
    )
```

```python
import functools

import jax
import jax.numpy as jnp
from jax import lax
from jax.experimental import pallas as pl
from jax.experimental.pallas import tpu as pltpu
from jax.sharding import PartitionSpec as P

CORES = 2
PAIR = 2
SUBLANES = 8
FOLDS = 2
CHUNKS = 2
VMEM = pl.BlockSpec(memory_space=pltpu.VMEM)
ANY = pl.BlockSpec(memory_space=pl.ANY)


def along(devices, by):
    each = CORES * PAIR
    return [(d, (d + by * each) % devices) for d in range(devices)]


def across(devices):
    return [(d, d ^ CORES) for d in range(devices)]


def swap(devices):
    return [(d, d ^ 1) for d in range(devices)]


def send(block, pairs):
    return lax.ppermute(block, "wide", pairs)


def origin(me, devices, step, other_chip, other_core):
    each = CORES * PAIR
    pair = lax.rem(me // each + devices // each - step, devices // each)
    chip = lax.rem(me // CORES, PAIR)
    core = lax.rem(me, CORES)
    if other_chip:
        chip = 1 - chip
    if other_core:
        core = 1 - core
    return pair * PAIR + chip, core


def room(mib, blocks):
    return mib * 2**20 if blocks <= SUBLANES else 24 * 2**20


def repeat(times, body, carry=None, loop=False):
    if loop or times > SUBLANES:
        return lax.fori_loop(0, times, body, carry)
    for step in range(times):
        carry = body(step, carry)
    return carry


def unfold_store(rows, slot, block):
    height = block.shape[0]
    at = pl.ds(pl.multiple_of(slot * height, SUBLANES), height)
    for tile in range(rows.shape[0]):
        rows[tile, at, :] = block[:, tile * 128 : (tile + 1) * 128].astype(jnp.float32)


def unfold_load(rows, fold, tokens):
    tiles = [rows[tile, pl.ds(fold, tokens, stride=SUBLANES), :] for tile in range(rows.shape[0])]
    return jnp.concatenate([tile.astype(jnp.bfloat16) for tile in tiles], 1)


def rotate_out_kernel(tokens, waits, z_ref, y_ref, cz_ref, cy_ref, basis_ref, *refs):
    sq_ref, rows, total = refs[waits:]
    steps, height, width = z_ref.shape
    devices = steps * CORES * PAIR
    me = lax.axis_index("wide")

    @pl.when(pl.program_id(0) == 0)
    def _():
        for ref, chip_bit, core_bit in ((z_ref, 0, 0), (y_ref, 1, 0), (cz_ref, 0, 1), (cy_ref, 1, 1)):

            def put(step, _, ref=ref, chip_bit=chip_bit, core_bit=core_bit):
                chip, core = origin(me, devices, step, chip_bit, core_bit)
                unfold_store(rows, core * (devices // CORES) + chip, ref[step])

            repeat(steps, put)
        total[...] = jnp.zeros_like(total)

    def add(fold, _):
        left = unfold_load(rows, pl.program_id(0) * FOLDS + fold, devices * tokens)
        right = basis_ref[pl.ds(pl.multiple_of(fold * width, 128), width), :]
        total[...] += jnp.dot(left, right, preferred_element_type=jnp.float32)

    repeat(FOLDS, add, None, steps > SUBLANES)

    @pl.when(pl.program_id(0) == pl.num_programs(0) - 1)
    def _():
        sq_ref[...] = (total[...] * total[...]).astype(sq_ref.dtype)


def rotate_out(tokens, z, y, cz, cy, basis, waits):
    steps, height, width = z.shape
    total = steps * CORES * PAIR * tokens
    columns = basis.shape[1]
    return pl.pallas_call(
        functools.partial(rotate_out_kernel, tokens, len(waits)),
        grid=(SUBLANES // FOLDS,),
        out_shape=jax.ShapeDtypeStruct((total, columns), jnp.bfloat16),
        in_specs=[VMEM] * 4 + [pl.BlockSpec((FOLDS * width, columns), lambda i: (i, 0))] + [ANY] * len(waits),
        out_specs=VMEM,
        scratch_shapes=[
            pltpu.VMEM((width // 128, total * SUBLANES, 128), jnp.float32),
            pltpu.VMEM((total, columns), jnp.float32),
        ],
        compiler_params=pltpu.CompilerParams(vmem_limit_bytes=room(10, steps)),
        cost_estimate=pl.CostEstimate(
            flops=2 * total * basis.shape[0] * columns, bytes_accessed=2 * basis.size, transcendentals=0
        ),
        name="rotate_out",
    )(z, y, cz, cy, basis, *waits)


def rotate_in_kernel(tokens, chunk, before, last, own_ref, across_ref, z_ref, y_ref, mine_ref, theirs_ref, *refs):
    outs, (total, rows) = refs[before:-2], refs[-2:]
    height, width = own_ref.shape
    steps = z_ref.shape[0] + 1
    devices = steps * CORES * PAIR
    chips = devices // CORES
    me = lax.axis_index("wide")

    def put(chip, block):
        unfold_store(rows, chip, block)

    @pl.when(pl.program_id(0) == 0)
    def _():
        put(origin(me, devices, 0, 0, 0)[0], own_ref[...])
        put(origin(me, devices, 0, 1, 0)[0], across_ref[chunk])
        for ref, chip_bit in ((z_ref, 0), (y_ref, 1)):

            def put_far(step, _, ref=ref, chip_bit=chip_bit):
                put(origin(me, devices, step + 1, chip_bit, 0)[0], ref[step])

            repeat(steps - 1, put_far)
        total[...] = refs[0][...] if before else jnp.zeros_like(total)

    def add(fold, _):
        at = pl.ds(pl.multiple_of(fold * width, 128), width)
        right = unfold_load(rows, pl.program_id(0) * FOLDS + fold, chips * tokens)
        left = jnp.concatenate([mine_ref[:, at], theirs_ref[:, at]])
        total[...] += lax.dot_general(left, right, (((1,), (1,)), ((), ())), preferred_element_type=jnp.float32)

    repeat(FOLDS, add, None, steps > SUBLANES)

    @pl.when(pl.program_id(0) == pl.num_programs(0) - 1)
    def _():
        if last:
            squares = (total[...] * total[...]).astype(jnp.bfloat16)
            outs[0][...] = squares[: outs[0].shape[0]]
            outs[1][...] = squares[outs[0].shape[0] :]
        else:
            outs[0][...] = total[...]


def rotate_in(tokens, chunk, own, across, z, y, mine, theirs, before):
    height, width = own.shape
    chips = (z.shape[0] + 1) * PAIR
    last = chunk == CHUNKS - 1
    basis = pl.BlockSpec((mine.shape[0], FOLDS * width), lambda i: (0, chunk * (SUBLANES // FOLDS) + i))
    whole = jax.ShapeDtypeStruct((2 * mine.shape[0], chips * tokens), jnp.float32)
    half = jax.ShapeDtypeStruct((mine.shape[0], chips * tokens), jnp.bfloat16)
    return pl.pallas_call(
        functools.partial(rotate_in_kernel, tokens, chunk, len(before), last),
        grid=(SUBLANES // FOLDS,),
        out_shape=(half, half) if last else (whole,),
        in_specs=[VMEM] * 4 + [basis] * 2 + [VMEM] * len(before),
        out_specs=(VMEM, VMEM) if last else (VMEM,),
        scratch_shapes=[
            pltpu.VMEM(whole.shape, jnp.float32),
            pltpu.VMEM((width // 128, chips * height, 128), jnp.float32),
        ],
        compiler_params=pltpu.CompilerParams(vmem_limit_bytes=room(9, chips)),
        cost_estimate=pl.CostEstimate(
            flops=4 * chips * tokens * mine.shape[0] * SUBLANES * width,
            bytes_accessed=4 * mine.shape[0] * SUBLANES * width,
            transcendentals=0,
        ),
        name="rotate_in",
    )(own, across, z, y, mine, theirs, *before)


def fold_one(from_ref, start, out_refs, rows):
    tokens = from_ref.shape[0]
    tiles = out_refs[0].shape[1] // 128
    for tile in range(tiles):
        for fold in range(SUBLANES):
            at = start + (fold * tiles + tile) * 128
            rows[tile, pl.ds(fold, tokens, stride=SUBLANES), :] = from_ref[:, at : at + 128].astype(jnp.float32)
    for tile in range(tiles):
        block = rows[tile, : tokens * SUBLANES, :].astype(jnp.bfloat16)
        for out_ref in out_refs:
            out_ref[:, tile * 128 : (tile + 1) * 128] = block


def fold_kernel(waits, chunks, from_ref, *refs):
    outs, rows = refs[waits:-1], refs[-1]
    for chunk in range(chunks):
        width = outs[chunk].shape[1]
        also = [outs[chunks].at[chunk]] if chunks > 1 else []
        fold_one(from_ref, chunk * SUBLANES * width, [outs[chunk], *also], rows)


def folded(array, chunks, waits):
    shape = (array.shape[0] * SUBLANES, array.shape[1] // (chunks * SUBLANES))
    shapes = [shape] * chunks + ([(chunks, *shape)] if chunks > 1 else [])
    return pl.pallas_call(
        functools.partial(fold_kernel, len(waits), chunks),
        out_shape=[jax.ShapeDtypeStruct(shape, array.dtype) for shape in shapes],
        in_specs=[VMEM] + [ANY] * len(waits),
        out_specs=[VMEM] * len(shapes),
        scratch_shapes=[pltpu.VMEM((shape[1] // 128, pl.cdiv(array.shape[0], SUBLANES) * SUBLANES**2, 128), jnp.float32)],
        compiler_params=pltpu.CompilerParams(vmem_limit_bytes=4 * 2**20),
        cost_estimate=pl.CostEstimate(flops=0, bytes_accessed=4 * array.size, transcendentals=0),
        name="fold",
    )(array, *waits)


def pile_kernel(blocks, *refs):
    for step in range(blocks):
        refs[-1][step] = refs[step][...]


def pile(blocks, waits):
    return pl.pallas_call(
        functools.partial(pile_kernel, len(blocks)),
        out_shape=jax.ShapeDtypeStruct((len(blocks), *blocks[0].shape), blocks[0].dtype),
        in_specs=[VMEM] * len(blocks) + [ANY] * len(waits),
        out_specs=VMEM,
        compiler_params=pltpu.CompilerParams(vmem_limit_bytes=room(3, len(blocks))),
        cost_estimate=pl.CostEstimate(flops=0, bytes_accessed=2 * len(blocks) * blocks[0].size, transcendentals=0),
        name="pile",
    )(*blocks, *waits)


def fetch_kernel(from_ref, *refs):
    to_ref, done = refs[-2:]
    copy = pltpu.make_async_copy(from_ref, to_ref, done)
    copy.start()
    copy.wait()


def fetch(array, waits):
    return pl.pallas_call(
        fetch_kernel,
        out_shape=jax.ShapeDtypeStruct(array.shape, array.dtype),
        in_specs=[ANY] * (1 + len(waits)),
        out_specs=VMEM,
        scratch_shapes=[pltpu.SemaphoreType.DMA],
        compiler_params=pltpu.CompilerParams(vmem_limit_bytes=16 * 2**20),
        cost_estimate=pl.CostEstimate(flops=0, bytes_accessed=2 * array.size, transcendentals=0),
        name="fetch",
    )(array, *waits)


def after(arrays, waits):
    return pl.pallas_call(
        lambda *refs: None,
        out_shape=[jax.ShapeDtypeStruct(array.shape, array.dtype) for array in arrays],
        in_specs=[ANY] * (len(arrays) + len(waits)),
        out_specs=[ANY] * len(arrays),
        input_output_aliases={i: i for i in range(len(arrays))},
        compiler_params=pltpu.CompilerParams(vmem_limit_bytes=2**20),
        cost_estimate=pl.CostEstimate(flops=0, bytes_accessed=0, transcendentals=0),
        name="after",
    )(*arrays, *waits)


def both_classes(own_ref, other_ref):
    own, other = own_ref[...].astype(jnp.float32), other_ref[...].astype(jnp.float32)
    first = lax.rem(lax.axis_index("wide"), CORES) == 0
    left = jnp.concatenate([jnp.where(first, own, other), jnp.where(first, other, own)], 1)
    return left.astype(jnp.bfloat16)


def eigenvalues(left, block):
    total = jnp.dot(left, block, preferred_element_type=jnp.float32)
    return (total / block.shape[0]).astype(jnp.bfloat16)


def combine_kernel(own_ref, other_ref, z_ref, y_ref, cz_ref, out_ref):
    steps, _, width = z_ref.shape
    devices = steps * CORES * PAIR
    me = lax.axis_index("wide")
    left = both_classes(own_ref, other_ref)
    for ref, chip_bit, core_bit in ((z_ref, 0, 0), (y_ref, 1, 0), (cz_ref, 0, 1)):

        def put(step, _, ref=ref, chip_bit=chip_bit, core_bit=core_bit):
            chip, core = origin(me, devices, step, chip_bit, core_bit)
            at = pl.multiple_of((chip * CORES + core) * width, 128)
            out_ref[:, pl.ds(at, width)] = eigenvalues(left, ref[step])

        repeat(steps, put)


def combine(own, other, z, y, cz):
    steps, total_tokens, width = z.shape
    features = steps * CORES * PAIR * width
    return pl.pallas_call(
        combine_kernel,
        out_shape=jax.ShapeDtypeStruct((own.shape[0], features), jnp.bfloat16),
        in_specs=[VMEM] * 5,
        out_specs=VMEM,
        compiler_params=pltpu.CompilerParams(vmem_limit_bytes=room(6, steps)),
        cost_estimate=pl.CostEstimate(
            flops=2 * own.shape[0] * total_tokens * features, bytes_accessed=4 * own.shape[0] * features, transcendentals=0
        ),
        name="combine",
    )(own, other, z, y, cz)


def finish_kernel(own_ref, other_ref, cy_ref, _, out_ref, blocks, done):
    steps, _, width = cy_ref.shape
    devices = steps * CORES * PAIR
    me = lax.axis_index("wide")
    left = both_classes(own_ref, other_ref)
    copies = []
    for step in range(steps):
        chip, core = origin(me, devices, step, 1, 1)
        at = pl.multiple_of((chip * CORES + core) * width, 128)
        blocks[step] = eigenvalues(left, cy_ref[step])
        copies.append(pltpu.make_async_copy(blocks.at[step], out_ref.at[:, pl.ds(at, width)], done.at[step]))
        copies[-1].start()
    for copy in copies:
        copy.wait()


def finish(own, other, cy, result):
    steps, total_tokens, width = cy.shape
    return pl.pallas_call(
        finish_kernel,
        out_shape=jax.ShapeDtypeStruct(result.shape, result.dtype),
        in_specs=[VMEM] * 3 + [ANY],
        out_specs=ANY,
        scratch_shapes=[
            pltpu.VMEM((steps, own.shape[0], width), result.dtype),
            pltpu.SemaphoreType.DMA((steps,)),
        ],
        input_output_aliases={3: 0},
        compiler_params=pltpu.CompilerParams(vmem_limit_bytes=room(4, steps)),
        cost_estimate=pl.CostEstimate(
            flops=2 * own.shape[0] * total_tokens * steps * width, bytes_accessed=4 * cy.size, transcendentals=0
        ),
        name="finish",
    )(own, other, cy, result)


def local(acts, grads, basis_in, basis_out):
    devices = lax.axis_size("wide")
    steps = devices // (CORES * PAIR)
    tokens = acts.shape[0]

    def along_all(block):
        return [send(block, along(devices, step)) for step in range(1, steps)]

    def others(z):
        y = send(z, across(devices))
        return z, y, send(z, swap(devices)), send(y, swap(devices))

    [block] = folded(grads, 1, [])
    *own, every = folded(acts, CHUNKS, [block])
    mine = basis_in.T
    theirs = send(mine, swap(devices))
    own_across = send(every, across(devices))
    grads_all = others(pile([block] + along_all(block), [theirs, every]))

    acts_z, acts_y = [], []

    def chunk_along(chunk, waits):
        acts_z.append(pile(along_all(own[chunk]), waits))
        acts_y.append(send(acts_z[-1], across(devices)))

    def part(chunk, before):
        return rotate_in(tokens, chunk, own[chunk], own_across, acts_z[chunk], acts_y[chunk], mine, theirs, before)

    fetched = fetch(basis_out, [grads_all[0]])
    chunk_along(0, [fetched])
    sq_out = rotate_out(tokens, *grads_all, fetched, [acts_z[0], own_across])
    came = along_all(sq_out)
    for chunk in range(1, CHUNKS):
        chunk_along(chunk, [sq_out])
    total = part(0, [])
    z = pile([sq_out] + came, [*total, acts_z[-1]])
    y = send(z, across(devices))
    for chunk in range(1, CHUNKS):
        total = part(chunk, total)
    sq_in, given = total
    other = send(given, swap(devices))
    [y] = after([y], [other])
    cz, cy = send(z, swap(devices)), send(y, swap(devices))
    return finish(sq_in, other, cy, combine(sq_in, other, z, y, cz))


def solution(mesh):
    return jax.shard_map(
        local,
        mesh=mesh,
        in_specs=(
            P(("groups", "wide"), None),
            P(("groups", "wide"), None),
            P("groups", "wide"),
            P("groups", "wide"),
        ),
        out_specs=P(("groups", "wide"), None),
        check_vma=False,
    )
```

```python
import functools

import jax
import jax.numpy as jnp
from jax import lax
from jax.experimental import pallas as pl
from jax.experimental.pallas import tpu as pltpu
from jax.sharding import PartitionSpec as P

CORES = 2
PAIR = 2
SUBLANES = 8
FOLDS = 4
CHUNKS = 2
VMEM = pl.BlockSpec(memory_space=pltpu.VMEM)
ANY = pl.BlockSpec(memory_space=pl.ANY)


def along(devices, by):
    each = CORES * PAIR
    return [(d, (d + by * each) % devices) for d in range(devices)]


def across(devices):
    return [(d, d ^ CORES) for d in range(devices)]


def swap(devices):
    return [(d, d ^ 1) for d in range(devices)]


def send(block, pairs):
    return lax.ppermute(block, "wide", pairs)


def origin(me, devices, step, other_chip, other_core):
    each = CORES * PAIR
    pair = lax.rem(me // each + devices // each - step, devices // each)
    chip = lax.rem(me // CORES, PAIR)
    core = lax.rem(me, CORES)
    if other_chip:
        chip = 1 - chip
    if other_core:
        core = 1 - core
    return pair * PAIR + chip, core


def room(mib, blocks):
    return mib * 2**20 if blocks <= SUBLANES else 24 * 2**20


def repeat(times, body, carry=None, loop=False):
    if loop or times > SUBLANES:
        return lax.fori_loop(0, times, body, carry)
    for step in range(times):
        carry = body(step, carry)
    return carry


def unfold_store(rows, slot, block):
    height = block.shape[0]
    at = pl.ds(pl.multiple_of(slot * height, SUBLANES), height)
    for tile in range(rows.shape[0]):
        rows[tile, at, :] = block[:, tile * 128 : (tile + 1) * 128].astype(jnp.float32)


def unfold_load(rows, fold, tokens):
    tiles = [rows[tile, pl.ds(fold, tokens, stride=SUBLANES), :] for tile in range(rows.shape[0])]
    return jnp.concatenate([tile.astype(jnp.bfloat16) for tile in tiles], 1)


def rotate_out_kernel(tokens, waits, z_ref, y_ref, cz_ref, cy_ref, basis_ref, *refs):
    sq_ref, rows, total = refs[waits:]
    steps, height, width = z_ref.shape
    devices = steps * CORES * PAIR
    me = lax.axis_index("wide")

    @pl.when(pl.program_id(0) == 0)
    def _():
        for ref, chip_bit, core_bit in ((z_ref, 0, 0), (y_ref, 1, 0), (cz_ref, 0, 1), (cy_ref, 1, 1)):

            def put(step, _, ref=ref, chip_bit=chip_bit, core_bit=core_bit):
                chip, core = origin(me, devices, step, chip_bit, core_bit)
                unfold_store(rows, core * (devices // CORES) + chip, ref[step])

            repeat(steps, put)
        total[...] = jnp.zeros_like(total)

    def add(fold, _):
        left = unfold_load(rows, pl.program_id(0) * FOLDS + fold, devices * tokens)
        right = basis_ref[pl.ds(pl.multiple_of(fold * width, 128), width), :]
        total[...] += jnp.dot(left, right, preferred_element_type=jnp.float32)

    repeat(FOLDS, add, None, steps > SUBLANES)

    @pl.when(pl.program_id(0) == pl.num_programs(0) - 1)
    def _():
        sq_ref[...] = (total[...] * total[...]).astype(sq_ref.dtype)


def rotate_out(tokens, z, y, cz, cy, basis, waits):
    steps, height, width = z.shape
    total = steps * CORES * PAIR * tokens
    columns = basis.shape[1]
    return pl.pallas_call(
        functools.partial(rotate_out_kernel, tokens, len(waits)),
        grid=(SUBLANES // FOLDS,),
        out_shape=jax.ShapeDtypeStruct((total, columns), jnp.bfloat16),
        in_specs=[VMEM] * 4 + [pl.BlockSpec((FOLDS * width, columns), lambda i: (i, 0))] + [ANY] * len(waits),
        out_specs=VMEM,
        scratch_shapes=[
            pltpu.VMEM((width // 128, total * SUBLANES, 128), jnp.float32),
            pltpu.VMEM((total, columns), jnp.float32),
        ],
        compiler_params=pltpu.CompilerParams(vmem_limit_bytes=room(14, steps)),
        cost_estimate=pl.CostEstimate(
            flops=2 * total * basis.shape[0] * columns, bytes_accessed=2 * basis.size, transcendentals=0
        ),
        name="rotate_out",
    )(z, y, cz, cy, basis, *waits)


def rotate_in_kernel(tokens, chunk, before, last, own_ref, across_ref, z_ref, y_ref, mine_ref, theirs_ref, *refs):
    outs, (total, rows) = refs[before:-2], refs[-2:]
    height, width = own_ref.shape
    steps = z_ref.shape[0] + 1
    devices = steps * CORES * PAIR
    chips = devices // CORES
    me = lax.axis_index("wide")

    def put(chip, block):
        unfold_store(rows, chip, block)

    @pl.when(pl.program_id(0) == 0)
    def _():
        put(origin(me, devices, 0, 0, 0)[0], own_ref[...])
        put(origin(me, devices, 0, 1, 0)[0], across_ref[chunk])
        for ref, chip_bit in ((z_ref, 0), (y_ref, 1)):

            def put_far(step, _, ref=ref, chip_bit=chip_bit):
                put(origin(me, devices, step + 1, chip_bit, 0)[0], ref[step])

            repeat(steps - 1, put_far)
        total[...] = refs[0][...] if before else jnp.zeros_like(total)

    def add(fold, _):
        at = pl.ds(pl.multiple_of(fold * width, 128), width)
        right = unfold_load(rows, pl.program_id(0) * FOLDS + fold, chips * tokens)
        left = jnp.concatenate([mine_ref[:, at], theirs_ref[:, at]])
        total[...] += lax.dot_general(left, right, (((1,), (1,)), ((), ())), preferred_element_type=jnp.float32)

    repeat(FOLDS, add, None, steps > SUBLANES)

    @pl.when(pl.program_id(0) == pl.num_programs(0) - 1)
    def _():
        if last:
            squares = (total[...] * total[...]).astype(jnp.bfloat16)
            outs[0][...] = squares[: outs[0].shape[0]]
            outs[1][...] = squares[outs[0].shape[0] :]
        else:
            outs[0][...] = total[...]


def rotate_in(tokens, chunk, own, across, z, y, mine, theirs, before):
    height, width = own.shape
    chips = (z.shape[0] + 1) * PAIR
    last = chunk == CHUNKS - 1
    basis = pl.BlockSpec((mine.shape[0], FOLDS * width), lambda i: (0, chunk * (SUBLANES // FOLDS) + i))
    whole = jax.ShapeDtypeStruct((2 * mine.shape[0], chips * tokens), jnp.float32)
    half = jax.ShapeDtypeStruct((mine.shape[0], chips * tokens), jnp.bfloat16)
    return pl.pallas_call(
        functools.partial(rotate_in_kernel, tokens, chunk, len(before), last),
        grid=(SUBLANES // FOLDS,),
        out_shape=(half, half) if last else (whole,),
        in_specs=[VMEM] * 4 + [basis] * 2 + [VMEM] * len(before),
        out_specs=(VMEM, VMEM) if last else (VMEM,),
        scratch_shapes=[
            pltpu.VMEM(whole.shape, jnp.float32),
            pltpu.VMEM((width // 128, chips * height, 128), jnp.float32),
        ],
        compiler_params=pltpu.CompilerParams(vmem_limit_bytes=room(14, chips)),
        cost_estimate=pl.CostEstimate(
            flops=4 * chips * tokens * mine.shape[0] * SUBLANES * width,
            bytes_accessed=4 * mine.shape[0] * SUBLANES * width,
            transcendentals=0,
        ),
        name="rotate_in",
    )(own, across, z, y, mine, theirs, *before)


def fold_one(from_ref, start, out_refs, rows):
    tokens = from_ref.shape[0]
    tiles = out_refs[0].shape[1] // 128
    for tile in range(tiles):
        for fold in range(SUBLANES):
            at = start + (fold * tiles + tile) * 128
            rows[tile, pl.ds(fold, tokens, stride=SUBLANES), :] = from_ref[:, at : at + 128].astype(jnp.float32)
    for tile in range(tiles):
        block = rows[tile, : tokens * SUBLANES, :].astype(jnp.bfloat16)
        for out_ref in out_refs:
            out_ref[:, tile * 128 : (tile + 1) * 128] = block


def fold_kernel(waits, chunks, from_ref, *refs):
    outs, rows = refs[waits:-1], refs[-1]
    for chunk in range(chunks):
        width = outs[chunk].shape[1]
        also = [outs[chunks].at[chunk]] if chunks > 1 else []
        fold_one(from_ref, chunk * SUBLANES * width, [outs[chunk], *also], rows)


def folded(array, chunks, waits):
    shape = (array.shape[0] * SUBLANES, array.shape[1] // (chunks * SUBLANES))
    shapes = [shape] * chunks + ([(chunks, *shape)] if chunks > 1 else [])
    return pl.pallas_call(
        functools.partial(fold_kernel, len(waits), chunks),
        out_shape=[jax.ShapeDtypeStruct(shape, array.dtype) for shape in shapes],
        in_specs=[VMEM] + [ANY] * len(waits),
        out_specs=[VMEM] * len(shapes),
        scratch_shapes=[pltpu.VMEM((shape[1] // 128, pl.cdiv(array.shape[0], SUBLANES) * SUBLANES**2, 128), jnp.float32)],
        compiler_params=pltpu.CompilerParams(vmem_limit_bytes=4 * 2**20),
        cost_estimate=pl.CostEstimate(flops=0, bytes_accessed=4 * array.size, transcendentals=0),
        name="fold",
    )(array, *waits)


def pile_kernel(blocks, *refs):
    for step in range(blocks):
        refs[-1][step] = refs[step][...]


def pile(blocks, waits):
    return pl.pallas_call(
        functools.partial(pile_kernel, len(blocks)),
        out_shape=jax.ShapeDtypeStruct((len(blocks), *blocks[0].shape), blocks[0].dtype),
        in_specs=[VMEM] * len(blocks) + [ANY] * len(waits),
        out_specs=VMEM,
        compiler_params=pltpu.CompilerParams(vmem_limit_bytes=room(3, len(blocks))),
        cost_estimate=pl.CostEstimate(flops=0, bytes_accessed=2 * len(blocks) * blocks[0].size, transcendentals=0),
        name="pile",
    )(*blocks, *waits)


def fetch_kernel(from_ref, *refs):
    to_ref, done = refs[-2:]
    copy = pltpu.make_async_copy(from_ref, to_ref, done)
    copy.start()
    copy.wait()


def fetch(array, waits):
    return pl.pallas_call(
        fetch_kernel,
        out_shape=jax.ShapeDtypeStruct(array.shape, array.dtype),
        in_specs=[ANY] * (1 + len(waits)),
        out_specs=VMEM,
        scratch_shapes=[pltpu.SemaphoreType.DMA],
        compiler_params=pltpu.CompilerParams(vmem_limit_bytes=16 * 2**20),
        cost_estimate=pl.CostEstimate(flops=0, bytes_accessed=2 * array.size, transcendentals=0),
        name="fetch",
    )(array, *waits)


def after(arrays, waits):
    return pl.pallas_call(
        lambda *refs: None,
        out_shape=[jax.ShapeDtypeStruct(array.shape, array.dtype) for array in arrays],
        in_specs=[ANY] * (len(arrays) + len(waits)),
        out_specs=[ANY] * len(arrays),
        input_output_aliases={i: i for i in range(len(arrays))},
        compiler_params=pltpu.CompilerParams(vmem_limit_bytes=2**20),
        cost_estimate=pl.CostEstimate(flops=0, bytes_accessed=0, transcendentals=0),
        name="after",
    )(*arrays, *waits)


def both_classes(own_ref, other_ref):
    own, other = own_ref[...].astype(jnp.float32), other_ref[...].astype(jnp.float32)
    first = lax.rem(lax.axis_index("wide"), CORES) == 0
    left = jnp.concatenate([jnp.where(first, own, other), jnp.where(first, other, own)], 1)
    return left.astype(jnp.bfloat16)


def eigenvalues(left, block):
    total = jnp.dot(left, block, preferred_element_type=jnp.float32)
    return (total / block.shape[0]).astype(jnp.bfloat16)


def combine_kernel(own_ref, other_ref, z_ref, y_ref, cz_ref, out_ref):
    steps, _, width = z_ref.shape
    devices = steps * CORES * PAIR
    me = lax.axis_index("wide")
    left = both_classes(own_ref, other_ref)
    for ref, chip_bit, core_bit in ((z_ref, 0, 0), (y_ref, 1, 0), (cz_ref, 0, 1)):

        def put(step, _, ref=ref, chip_bit=chip_bit, core_bit=core_bit):
            chip, core = origin(me, devices, step, chip_bit, core_bit)
            at = pl.multiple_of((chip * CORES + core) * width, 128)
            out_ref[:, pl.ds(at, width)] = eigenvalues(left, ref[step])

        repeat(steps, put)


def combine(own, other, z, y, cz):
    steps, total_tokens, width = z.shape
    features = steps * CORES * PAIR * width
    return pl.pallas_call(
        combine_kernel,
        out_shape=jax.ShapeDtypeStruct((own.shape[0], features), jnp.bfloat16),
        in_specs=[VMEM] * 5,
        out_specs=VMEM,
        compiler_params=pltpu.CompilerParams(vmem_limit_bytes=room(6, steps)),
        cost_estimate=pl.CostEstimate(
            flops=2 * own.shape[0] * total_tokens * features, bytes_accessed=4 * own.shape[0] * features, transcendentals=0
        ),
        name="combine",
    )(own, other, z, y, cz)


def finish_kernel(own_ref, other_ref, cy_ref, _, out_ref, blocks, done):
    steps, _, width = cy_ref.shape
    devices = steps * CORES * PAIR
    me = lax.axis_index("wide")
    left = both_classes(own_ref, other_ref)
    copies = []
    for step in range(steps):
        chip, core = origin(me, devices, step, 1, 1)
        at = pl.multiple_of((chip * CORES + core) * width, 128)
        blocks[step] = eigenvalues(left, cy_ref[step])
        copies.append(pltpu.make_async_copy(blocks.at[step], out_ref.at[:, pl.ds(at, width)], done.at[step]))
        copies[-1].start()
    for copy in copies:
        copy.wait()


def finish(own, other, cy, result):
    steps, total_tokens, width = cy.shape
    return pl.pallas_call(
        finish_kernel,
        out_shape=jax.ShapeDtypeStruct(result.shape, result.dtype),
        in_specs=[VMEM] * 3 + [ANY],
        out_specs=ANY,
        scratch_shapes=[
            pltpu.VMEM((steps, own.shape[0], width), result.dtype),
            pltpu.SemaphoreType.DMA((steps,)),
        ],
        input_output_aliases={3: 0},
        compiler_params=pltpu.CompilerParams(vmem_limit_bytes=room(4, steps)),
        cost_estimate=pl.CostEstimate(
            flops=2 * own.shape[0] * total_tokens * steps * width, bytes_accessed=4 * cy.size, transcendentals=0
        ),
        name="finish",
    )(own, other, cy, result)


def local(acts, grads, basis_in, basis_out):
    devices = lax.axis_size("wide")
    steps = devices // (CORES * PAIR)
    tokens = acts.shape[0]

    def along_all(block):
        return [send(block, along(devices, step)) for step in range(1, steps)]

    def others(z):
        y = send(z, across(devices))
        return z, y, send(z, swap(devices)), send(y, swap(devices))

    [block] = folded(grads, 1, [])
    *own, every = folded(acts, CHUNKS, [block])
    mine = basis_in.T
    theirs = send(mine, swap(devices))
    own_across = send(every, across(devices))
    grads_all = others(pile([block] + along_all(block), [theirs, every]))

    acts_z, acts_y = [], []

    def chunk_along(chunk, waits):
        acts_z.append(pile(along_all(own[chunk]), waits))
        acts_y.append(send(acts_z[-1], across(devices)))

    def part(chunk, before):
        return rotate_in(tokens, chunk, own[chunk], own_across, acts_z[chunk], acts_y[chunk], mine, theirs, before)

    fetched = fetch(basis_out, [grads_all[0]])
    chunk_along(0, [fetched])
    sq_out = rotate_out(tokens, *grads_all, fetched, [acts_z[0], own_across])
    came = along_all(sq_out)
    for chunk in range(1, CHUNKS):
        chunk_along(chunk, [sq_out])
    total = part(0, [])
    z = pile([sq_out] + came, [*total, acts_z[-1]])
    y = send(z, across(devices))
    for chunk in range(1, CHUNKS):
        total = part(chunk, total)
    sq_in, given = total
    other = send(given, swap(devices))
    [y] = after([y], [other])
    cz, cy = send(z, swap(devices)), send(y, swap(devices))
    return finish(sq_in, other, cy, combine(sq_in, other, z, y, cz))


def solution(mesh):
    return jax.shard_map(
        local,
        mesh=mesh,
        in_specs=(
            P(("groups", "wide"), None),
            P(("groups", "wide"), None),
            P("groups", "wide"),
            P("groups", "wide"),
        ),
        out_specs=P(("groups", "wide"), None),
        check_vma=False,
    )
```
